32 devices in a mesh: narrow: 2 (over core), wide: 16 (over z, y, x).
Axes of the slice: x: 2, y: 2, z: 4, core: 2. Of those that a mesh axis runs over, the one named last changes fastest.
Arguments:
- inputs: bfloat16 [2, 32, 256, 1536], P(None, ('narrow', 'wide')), may hold values from -6 to 6
- cotangent: bfloat16 [2, 32, 256, 1536], P(None, ('narrow', 'wide')), may hold values from -6 to 6
- lengths: int32 [2, 32], P(None, ('narrow', 'wide')), may hold values from 32 to 256, as said below
- gains: float32 [2, 1536], P(None, 'wide'), may hold values from 0.5 to 1.5
- gains_momentum: float32 [2, 1536], P(None, 'wide'), may hold values from -768 to 768
- gains_average: float32 [2, 1536], P(None, 'wide'), may hold values from 0.5 to 1.5
- qkv_weight: float32 [3, 1536, 1536], P(None, 'wide'), may hold values from -0.15625 to 0.15625
- qkv_momentum: float32 [3, 1536, 1536], P(None, 'wide'), may hold values from -384 to 384
- qkv_average: float32 [3, 1536, 1536], P(None, 'wide'), may hold values from -0.15625 to 0.15625
- out_weight: float32 [1536, 1536], P('wide'), may hold values from -0.625 to 0.625
- out_momentum: float32 [1536, 1536], P('wide'), may hold values from -160 to 160
- out_average: float32 [1536, 1536], P('wide'), may hold values from -0.625 to 0.625
- conv_taps: float32 [16, 6, 11], replicated, may hold values from -0.5 to 1.5
- taps_momentum: float32 [16, 6, 11], replicated, may hold values from -2560 to 2560
- taps_average: float32 [16, 6, 11], replicated, may hold values from -0.5 to 1.5
- head_mix: float32 [16, 2], replicated, may hold values from -0.5 to 1.3
- mix_momentum: float32 [16, 2], replicated, may hold values from -2560 to 2560
- mix_average: float32 [16, 2], replicated, may hold values from -0.5 to 1.3
- gateup_weight: float32 [1536, 2, 4096], P('wide'), may hold values from -0.15625 to 0.15625
- gateup_momentum: float32 [1536, 2, 4096], P('wide'), may hold values from -224 to 224
- gateup_average: float32 [1536, 2, 4096], P('wide'), may hold values from -0.15625 to 0.15625
- down_weight: float32 [4096, 1536], P('wide'), may hold values from -0.09375 to 0.09375
- down_momentum: float32 [4096, 1536], P('wide'), may hold values from -448 to 448
- down_average: float32 [4096, 1536], P('wide'), may hold values from -0.09375 to 0.09375
Outputs:
- output: bfloat16 [2, 32, 256, 1536], P(None, ('narrow', 'wide'))
- input_grad: bfloat16 [2, 32, 256, 1536], P(None, ('narrow', 'wide'))
- gains_momentum_new: float32 [2, 1536], P(None, 'wide')
- gains_new: float32 [2, 1536], P(None, 'wide')
- gains_average_new: float32 [2, 1536], P(None, 'wide')
- qkv_momentum_new: float32 [3, 1536, 1536], P(None, 'wide')
- qkv_new: float32 [3, 1536, 1536], P(None, 'wide')
- qkv_average_new: float32 [3, 1536, 1536], P(None, 'wide')
- out_momentum_new: float32 [1536, 1536], P('wide')
- out_new: float32 [1536, 1536], P('wide')
- out_average_new: float32 [1536, 1536], P('wide')
- taps_momentum_new: float32 [16, 6, 11], replicated
- taps_new: float32 [16, 6, 11], replicated
- taps_average_new: float32 [16, 6, 11], replicated
- mix_momentum_new: float32 [16, 2], replicated
- mix_new: float32 [16, 2], replicated
- mix_average_new: float32 [16, 2], replicated
- gateup_momentum_new: float32 [1536, 2, 4096], P('wide')
- gateup_new: float32 [1536, 2, 4096], P('wide')
- gateup_average_new: float32 [1536, 2, 4096], P('wide')
- down_momentum_new: float32 [4096, 1536], P('wide')
- down_new: float32 [4096, 1536], P('wide')
- down_average_new: float32 [4096, 1536], P('wide')
The draws below stay inside these ranges and needn't reach their ends.
Inputs may be any that keep to these rules, and one draw needn't show every extreme that they name: `lengths`: at least one sequence has all 256 tokens valid.
All inputs are finite; a program needn't handle non-finite values.
Results may differ from the reference program's by a relative error of at most 0.017.
The reference program's roundings to bfloat16 on the way count: a program that leaves them out, or rounds other values in their place, can miss the bound.
Values may be sent and summed in bfloat16 or wider, within the bound.
No kernel may reach another device: no remote copies, remote signals or barrier semaphores. Data moves between devices by JAX's collectives and lax.ppermute only.
A program may use at most 768 MiB of HBM per device.

```python
import math
import jax
import jax.numpy as jnp
from jax import lax

D = 1536
H = 16
E = 96
FF = 4096
CQ = 6
CK = 11
G = 2
MB = 2
LEN = 256
BATCH = 32
TOKENS = 16384


def draw_lengths(key, part):
    key = jax.random.fold_in(key, 11)
    key_values, key_spot = jax.random.split(key)
    drawn_lengths = jax.random.randint(key_values, (MB * BATCH,), LEN // 8, LEN + 1)
    full_spot = jax.random.randint(key_spot, (), 0, MB * BATCH)
    flat_lengths = jnp.where(jnp.arange(MB * BATCH) == full_spot, LEN, drawn_lengths)
    return flat_lengths.reshape(MB, BATCH).astype(jnp.int32)


def tap_field(key, spread):
    noise_part = jnp.clip(jax.random.normal(key, (H, CQ, CK), jnp.float32) * spread, -0.5, 0.5)
    lag_index = jnp.arange(CQ)[None, :, None]
    shift_index = jnp.arange(CK)[None, None, :]
    centre = jnp.where((lag_index == 0) & (shift_index == CK // 2), 1.0, 0.0).astype(jnp.float32)
    return centre + noise_part


def mix_field(key, reach_max):
    key_own, key_other = jax.random.split(key)
    own_part = jax.random.uniform(key_own, (H, G), jnp.float32, 0.7, 1.3)
    other_part = jax.random.uniform(key_other, (H, G), jnp.float32, -reach_max, reach_max)
    matching = jnp.arange(H)[:, None] % G == jnp.arange(G)[None, :]
    return jnp.where(matching, own_part, other_part)


def draw_conv_taps(key, part):
    key = jax.random.fold_in(key, 21)
    return tap_field(key, 0.12)


def draw_taps_average(key, part):
    key = jax.random.fold_in(key, 22)
    return tap_field(key, 0.12)


def draw_head_mix(key, part):
    key = jax.random.fold_in(key, 31)
    return mix_field(key, 0.5)


def draw_mix_average(key, part):
    key = jax.random.fold_in(key, 32)
    return mix_field(key, 0.5)


def steps_of(key, dims, cuts, low, top_value):
    factor_of, own = 1.0, jax.random.fold_in(key, 6)
    for dim, blocks in cuts:
        steps = jnp.exp(jax.random.uniform(jax.random.fold_in(own, dim), (blocks,), jnp.float32, low / len(cuts), top_value / len(cuts)))
        factor_of = factor_of * jnp.repeat(steps, dims[dim] // blocks).reshape([-1 if axis == dim else 1 for axis in range(len(dims))])
    return factor_of


def scatter_about(own_key, extent, width, reach, pieces=(), held_as=jnp.bfloat16):
    level = steps_of(own_key, extent, pieces, -0.22, 0.18) if pieces else 1.0
    values = jax.random.normal(own_key, extent, jnp.float32) * width * level
    return jnp.minimum(jnp.maximum(values, -reach), reach).astype(held_as)


def setup_inputs(seed: int = 0) -> dict:
    keys = jax.random.split(jax.random.key(seed), 25)
    inputs = scatter_about(keys[0], (MB, BATCH, LEN, D), 1.0, 6.0, ((1, 32),))
    cotangent = scatter_about(keys[1], (MB, BATCH, LEN, D), 1.0, 6.0, ((1, 32),))
    lengths = draw_lengths(jax.random.fold_in(keys[24], 71), 0)
    gains = jnp.clip(1.0 + 0.1 * jax.random.normal(keys[3], (2, D), jnp.float32), 0.5, 1.5)
    gains_momentum = scatter_about(keys[4], (2, D), (TOKENS ** 0.5), 768.0, ((1, 16),), jnp.float32)
    gains_average = jnp.clip(1.0 + 0.1 * jax.random.normal(keys[5], (2, D), jnp.float32), 0.5, 1.5)
    qkv_weight = scatter_about(keys[6], (3, D, D), D ** -0.5, 0.15625, ((1, 16),), jnp.float32)
    qkv_momentum = scatter_about(keys[7], (3, D, D), (0.5 * TOKENS ** 0.5), 384.0, ((1, 16),), jnp.float32)
    qkv_average = scatter_about(keys[8], (3, D, D), D ** -0.5, 0.15625, ((1, 16),), jnp.float32)
    out_weight = scatter_about(keys[9], (D, D), (D // 16) ** -0.5, 0.625, ((0, 16),), jnp.float32)
    out_momentum = scatter_about(keys[10], (D, D), (0.2 * TOKENS ** 0.5), 160.0, ((0, 16),), jnp.float32)
    out_average = scatter_about(keys[11], (D, D), (D // 16) ** -0.5, 0.625, ((0, 16),), jnp.float32)
    conv_taps = draw_conv_taps(jax.random.fold_in(keys[24], 71), 0)
    taps_momentum = scatter_about(keys[13], (H, CQ, CK), (0.2 * (TOKENS * LEN) ** 0.5), 2560.0, (), jnp.float32)
    taps_average = draw_taps_average(jax.random.fold_in(keys[24], 71), 0)
    head_mix = draw_head_mix(jax.random.fold_in(keys[24], 71), 0)
    mix_momentum = scatter_about(keys[16], (H, G), (0.2 * (TOKENS * LEN) ** 0.5), 2560.0, (), jnp.float32)
    mix_average = draw_mix_average(jax.random.fold_in(keys[24], 71), 0)
    gateup_weight = scatter_about(keys[18], (D, 2, FF), D ** -0.5, 0.15625, ((0, 16),), jnp.float32)
    gateup_momentum = scatter_about(keys[19], (D, 2, FF), (0.3 * TOKENS ** 0.5), 224.0, ((0, 16),), jnp.float32)
    gateup_average = scatter_about(keys[20], (D, 2, FF), D ** -0.5, 0.15625, ((0, 16),), jnp.float32)
    down_weight = scatter_about(keys[21], (FF, D), FF ** -0.5, 0.09375, ((0, 16),), jnp.float32)
    down_momentum = scatter_about(keys[22], (FF, D), (0.6 * TOKENS ** 0.5), 448.0, ((0, 16),), jnp.float32)
    down_average = scatter_about(keys[23], (FF, D), FF ** -0.5, 0.09375, ((0, 16),), jnp.float32)
    return {"inputs": inputs, "cotangent": cotangent, "lengths": lengths, "gains": gains, "gains_momentum": gains_momentum, "gains_average": gains_average, "qkv_weight": qkv_weight, "qkv_momentum": qkv_momentum, "qkv_average": qkv_average, "out_weight": out_weight, "out_momentum": out_momentum, "out_average": out_average, "conv_taps": conv_taps, "taps_momentum": taps_momentum, "taps_average": taps_average, "head_mix": head_mix, "mix_momentum": mix_momentum, "mix_average": mix_average, "gateup_weight": gateup_weight, "gateup_momentum": gateup_momentum, "gateup_average": gateup_average, "down_weight": down_weight, "down_momentum": down_momentum, "down_average": down_average}


@jax.custom_vjp
def low(v):
    return lax.optimization_barrier(v.astype(jnp.bfloat16)).astype(jnp.float32)

@jax.custom_vjp
def low_back(v):
    return v

def low_keep(v):
    return (low(v), None)

def low_pass(kept, grad):
    return (grad,)

def back_keep(v):
    return (v, None)

def back_low(kept, grad):
    return (low(grad),)
low.defvjp(low_keep, low_pass)
low_back.defvjp(back_keep, back_low)
EPSILON = 1e-05
MOMENTUM = 0.9
AVERAGE = 0.7
RATES = (0.1, 0.019, 0.19, 0.2, 0.5, 0.031, 0.0097)
PER_PAIR = (False, False, False, True, True, False, False)
HIGHEST = lax.Precision.HIGHEST

def rms_scale(values):
    return lax.rsqrt(lax.optimization_barrier(jnp.mean(values * values, axis=-1, keepdims=True)) + EPSILON)

def attention_core(raw_scores, conv_taps, head_mix, valid_len):
    seq_count = raw_scores.shape[0]
    head_count = raw_scores.shape[1]
    seq_len = raw_scores.shape[2]
    lag_count = conv_taps.shape[1]
    shift_count = conv_taps.shape[2]
    half_keys = shift_count // 2
    row_iota = lax.broadcasted_iota(jnp.int32, (seq_len, seq_len), 0)
    col_iota = lax.broadcasted_iota(jnp.int32, (seq_len, seq_len), 1)
    allowed = (col_iota <= row_iota)[None, None] & (col_iota[None, None] < valid_len[:, None, None, None])
    masked = jnp.where(allowed, raw_scores * (1.0 / math.sqrt(E)), 0.0)
    padded = jnp.pad(masked, ((0, 0), (0, 0), (lag_count - 1, 0), (half_keys, half_keys)))
    conv_total = jnp.zeros_like(masked)
    for lag_index in range(lag_count):
        for shift_index in range(shift_count):
            row_start = lag_count - 1 - lag_index
            col_start = 2 * half_keys - shift_index
            tap_slice = padded[:, :, row_start:row_start + seq_len, col_start:col_start + seq_len]
            conv_total = conv_total + conv_taps[:, lag_index, shift_index][None, :, None, None] * tap_slice
    logits = jnp.where(allowed, conv_total, -jnp.inf)
    row_top = lax.optimization_barrier(jnp.max(logits, axis=-1, keepdims=True))
    exp_terms = jnp.exp(logits - row_top)
    softmax_out = exp_terms / lax.optimization_barrier(jnp.sum(exp_terms, axis=-1, keepdims=True))
    grouped = softmax_out.reshape(seq_count, head_count // G, G, seq_len, seq_len)
    mixing = head_mix.reshape(head_count // G, G, G)
    blended = jnp.einsum('goi,sgikl->sgokl', mixing, grouped, precision=HIGHEST)
    return blended.reshape(seq_count, head_count, seq_len, seq_len)

def block_forward(sequences, valid_len, gains_low, qkv_low, out_low, conv_taps, head_mix, gateup_low, down_low):
    seq_count = sequences.shape[0]
    seq_len = sequences.shape[1]
    model_width = sequences.shape[2]
    states = sequences.reshape(seq_count * seq_len, model_width)
    normed = low(states * rms_scale(states) * gains_low[0])
    projected = jnp.einsum('rd,kde->kre', normed, qkv_low, precision=HIGHEST)
    projected = low_back(low(projected))
    head_split = projected.reshape(3, seq_count, seq_len, H, E)
    raw_scores = jnp.einsum('sqhe,skhe->shqk', head_split[0], head_split[1], precision=HIGHEST)
    raw_scores = low_back(raw_scores)
    mixed = low(attention_core(raw_scores, conv_taps, head_mix, valid_len))
    context = jnp.einsum('shqk,skhe->sqhe', mixed, head_split[2], precision=HIGHEST)
    context = low_back(low(context.reshape(seq_count * seq_len, model_width)))
    attended = low_back(jnp.dot(context, out_low, precision=HIGHEST))
    middle = states + attended
    second = low(middle * rms_scale(middle) * gains_low[1])
    gate_up = low_back(jnp.einsum('rd,dkf->rkf', second, gateup_low, precision=HIGHEST))
    hidden = low(jax.nn.silu(gate_up[:, 0]) * gate_up[:, 1])
    final = low_back(jnp.dot(hidden, down_low, precision=HIGHEST))
    return (middle + final).reshape(seq_count, seq_len, model_width)

def nesterov(master, moment, average, gradient, step_rate):
    new_moment = MOMENTUM * moment + gradient
    new_master = master - step_rate * (gradient + MOMENTUM * new_moment)
    return (new_moment, new_master, AVERAGE * average + (1.0 - AVERAGE) * new_master)

def reference(inputs, cotangent, lengths, gains, gains_momentum, gains_average, qkv_weight, qkv_momentum, qkv_average, out_weight, out_momentum, out_average, conv_taps, taps_momentum, taps_average, head_mix, mix_momentum, mix_average, gateup_weight, gateup_momentum, gateup_average, down_weight, down_momentum, down_average):
    packed = math.gcd(BATCH, max(1, 1024 // LEN))
    pack_shape = (MB * BATCH // packed, packed, LEN, D)
    states = inputs.astype(jnp.float32).reshape(pack_shape)
    valid_packs = lengths.reshape(MB * BATCH // packed, packed).astype(jnp.int32)
    params = (gains, qkv_weight, out_weight, conv_taps, head_mix, gateup_weight, down_weight)

    def whole(state_packs, weights):
        gains_low = low(weights[0])
        qkv_low = low(weights[1])
        out_low = low(weights[2])
        gateup_low = low(weights[5])
        down_low = low(weights[6])

        def one_pack(carry_in, pack_item):
            result = jax.checkpoint(block_forward)(pack_item[0], pack_item[1], gains_low, qkv_low, out_low, weights[3], weights[4], gateup_low, down_low)
            return (carry_in, result)
        unused, results = lax.scan(one_pack, jnp.zeros((), jnp.float32), (state_packs, valid_packs))
        return results
    results, pull_back = jax.vjp(whole, states, params)
    state_grad, grads = pull_back(cotangent.astype(jnp.float32).reshape(pack_shape))
    tokens_all = MB * BATCH * LEN

    def rate_for(position):
        return RATES[position] / math.sqrt(tokens_all * (LEN if PER_PAIR[position] else 1))
    gains_out = nesterov(gains, gains_momentum, gains_average, grads[0], rate_for(0))
    qkv_out = nesterov(qkv_weight, qkv_momentum, qkv_average, grads[1], rate_for(1))
    out_out = nesterov(out_weight, out_momentum, out_average, grads[2], rate_for(2))
    taps_out = nesterov(conv_taps, taps_momentum, taps_average, grads[3], rate_for(3))
    mix_out = nesterov(head_mix, mix_momentum, mix_average, grads[4], rate_for(4))
    gateup_out = nesterov(gateup_weight, gateup_momentum, gateup_average, grads[5], rate_for(5))
    down_out = nesterov(down_weight, down_momentum, down_average, grads[6], rate_for(6))
    full_shape = (MB, BATCH, LEN, D)
    return (results.reshape(full_shape).astype(jnp.bfloat16), state_grad.reshape(full_shape).astype(jnp.bfloat16), gains_out[0], gains_out[1], gains_out[2], qkv_out[0], qkv_out[1], qkv_out[2], out_out[0], out_out[1], out_out[2], taps_out[0], taps_out[1], taps_out[2], mix_out[0], mix_out[1], mix_out[2], gateup_out[0], gateup_out[1], gateup_out[2], down_out[0], down_out[1], down_out[2])
```

```python
import math

import jax
import jax.numpy as jnp
from jax import lax
from jax.experimental import pallas as pl
from jax.experimental.pallas import tpu as pltpu
from jax.sharding import PartitionSpec as P

H = 16
E = 96
G = 2


EPSILON = 1e-05
MOMENTUM = 0.9
AVERAGE = 0.7
RATES = (0.1, 0.019, 0.19, 0.2, 0.5, 0.031, 0.0097)
PER_PAIR = (False, False, False, True, True, False, False)
F32 = jnp.float32
BF16 = jnp.bfloat16
SCALE = 1.0 / math.sqrt(E)


def permute(values, pairs):
    return lax.ppermute(values, "wide", pairs)


def swap_cores(values):
    return lax.ppermute(values, "narrow", [(0, 1), (1, 0)])


BLOCK = 16


def z_pairs(moves):
    return [(a * 4 + q, b * 4 + q) for a, b in moves for q in range(4)]


Z_PAIR = z_pairs([(0, 1), (1, 0), (2, 3), (3, 2)])
Z_MID = z_pairs([(1, 2), (2, 1)])
Z_OUT = z_pairs([(1, 0), (2, 3)])
Z_IN = z_pairs([(0, 1), (3, 2)])
X_PAIR = [(i, i ^ 1) for i in range(BLOCK)]
Y_PAIR = [(i, i ^ 2) for i in range(BLOCK)]


def cut_columns(columns):
    tiles = columns // 128
    return (tiles - tiles // 5) * 128


def after(values, *needed):
    def nothing(*refs):
        del refs

    return pl.pallas_call(
        nothing,
        out_shape=jax.ShapeDtypeStruct(values.shape, values.dtype),
        in_specs=[pl.BlockSpec(memory_space=pl.ANY)] * (1 + len(needed)),
        out_specs=pl.BlockSpec(memory_space=pl.ANY),
        input_output_aliases={0: 0},
    )(values, *needed)


def line_gather(piece):
    z = lax.axis_index("wide") // 4
    odd = (z % 2) == 1
    other = permute(piece, Z_PAIR)
    near = jnp.stack([jnp.where(odd, other, piece), jnp.where(odd, piece, other)])
    crossed = permute(near, Z_MID)
    handed = permute(crossed, Z_OUT)
    far = jnp.where((z == 1) | (z == 2), crossed, handed)
    return near, far


def gather_begin(piece, *needed):
    if lax.axis_size("wide") != BLOCK:
        return (piece,)
    if needed:
        piece = after(piece, *needed)
    cut = cut_columns(piece.shape[1])
    lines = [line_gather(piece[:, :cut])]
    own = piece[:, cut:]
    by_x = permute(own, X_PAIR)
    by_y = permute(own, Y_PAIR)
    plane = jnp.stack([own, by_x, by_y, permute(by_x, Y_PAIR)])
    lines.append(line_gather(plane))
    return lines


def gather_end(lines, *needed):
    count = lax.axis_size("wide")
    if count != BLOCK:
        return lax.all_gather(lines[0], "wide", axis=0, tiled=True)
    (near, far), rest = lines
    rows, cut = near.shape[1:]
    columns = cut + rest[0].shape[-1]
    if needed:
        near, far = after(near, *needed), after(far, *needed)
    me = lax.axis_index("wide")
    index = jnp.stack([me // 4, me % 4]).astype(jnp.int32)
    arrays = []
    places = []

    def place(array, pick, half, lane, low, high):
        position = [n for n, known in enumerate(arrays) if known is array]
        if not position:
            arrays.append(array)
            position = [len(arrays) - 1]
        places.append((position[0], pick, half, lane, low, high))

    for half, block in enumerate((near, far)):
        by_x = permute(block, X_PAIR)
        by_y = permute(block, Y_PAIR)
        both = permute(by_y, X_PAIR) if half == 0 else permute(by_x, Y_PAIR)
        for lane, array in enumerate((block, by_x, by_y, both)):
            place(array, None, half, lane, 0, cut)
    for half, block in enumerate(rest):
        for lane in range(4):
            place(block, lane, half, lane, cut, columns)

    def assemble(index_ref, *refs):
        out_ref, sems = refs[len(arrays)], refs[len(arrays) + 1]
        pair, lane_me = index_ref[0] // 2, index_ref[1]
        copies = []
        for n, (position, pick, half, lane, low, high) in enumerate(places):
            source = refs[position] if pick is None else refs[position].at[:, pick]
            target = out_ref.at[
                pl.ds(2 * (pair ^ half), 2), lane_me ^ lane, :, pl.ds(low, high - low)
            ]
            copies.append(pltpu.make_async_copy(source, target, sems.at[n]))
        for copy in copies:
            copy.start()
        for copy in copies:
            copy.wait()

    full = pl.pallas_call(
        assemble,
        out_shape=jax.ShapeDtypeStruct((4, 4, rows, columns), near.dtype),
        in_specs=[pl.BlockSpec(memory_space=pltpu.SMEM)]
        + [pl.BlockSpec(memory_space=pl.ANY)] * len(arrays),
        out_specs=pl.BlockSpec(memory_space=pltpu.VMEM),
        scratch_shapes=[pltpu.SemaphoreType.DMA((len(places),))],
        compiler_params=pltpu.CompilerParams(vmem_limit_bytes=48 << 20),
    )(index, *arrays)
    return full.reshape(count * rows, columns)


def fold(*terms):
    return sum(term.astype(F32) for term in terms).astype(BF16)


def trade(values, bit, pairs):
    keep = lax.dynamic_index_in_dim(values, bit, 0, keepdims=False)
    give = lax.dynamic_index_in_dim(values, 1 - bit, 0, keepdims=False)
    return fold(keep, permute(give, pairs))


def line_sum(near, far, odd):
    far = fold(far, permute(far, Z_IN))
    near = fold(near, permute(far, Z_MID))
    return trade(near, odd, Z_PAIR)


def scatter_sum(partial):
    count = lax.axis_size("wide")
    if count != BLOCK:
        return lax.psum_scatter(partial, "wide", scatter_dimension=0, tiled=True)
    me = lax.axis_index("wide")
    pair, odd, y, x = me // 8, (me // 4) % 2, (me // 2) % 2, me % 2
    columns = partial.shape[1]
    rows = partial.shape[0] // count
    cut = cut_columns(columns)
    blocks = partial.reshape(2, 2, 2, 2, rows, columns)

    def block(half, y_at, x_at):
        found = lax.dynamic_slice(
            blocks, (half, 0, y_at, x_at, 0, 0), (1, 2, 1, 1, rows, cut)
        )
        return found.reshape(2, rows, cut)

    far = fold(block(1 - pair, y, 1 - x), permute(block(1 - pair, 1 - y, 1 - x), Y_PAIR))
    far = fold(
        block(1 - pair, y, x),
        permute(block(1 - pair, 1 - y, x), Y_PAIR),
        permute(far, X_PAIR),
    )
    near = fold(block(pair, 1 - y, x), permute(block(pair, 1 - y, 1 - x), X_PAIR))
    near = fold(
        block(pair, y, x),
        permute(block(pair, y, 1 - x), X_PAIR),
        permute(near, Y_PAIR),
    )
    done = line_sum(near, far, odd)
    if columns > cut:
        rest = blocks[..., cut:]
        near = lax.dynamic_index_in_dim(rest, pair, 0, keepdims=False)
        far = lax.dynamic_index_in_dim(rest, 1 - pair, 0, keepdims=False)
        last = trade(trade(line_sum(near, far, odd), y, Y_PAIR), x, X_PAIR)
        done = jnp.concatenate([done, last], axis=1)
    return done


def gather_small(values):
    if lax.axis_size("wide") != BLOCK:
        return lax.all_gather(values, "wide")
    me = lax.axis_index("wide")
    pair, y, x = me // 8, (me // 2) % 2, me % 2

    def both(mine, other, bit):
        return jnp.where(bit == 0, jnp.stack([mine, other]), jnp.stack([other, mine]))

    row = both(values, permute(values, X_PAIR), x)
    plane = both(row, permute(row, Y_PAIR), y)
    near, far = line_gather(plane)
    return both(near, far, pair).reshape((BLOCK,) + values.shape)


def sum_small(values):
    values = values + swap_cores(values)
    if lax.axis_size("wide") != BLOCK:
        return lax.psum(values, "wide")
    z = lax.axis_index("wide") // 4
    for pairs in (X_PAIR, Y_PAIR, Z_PAIR):
        values = values + permute(values, pairs)
    total = values + permute(values, Z_MID)
    return jnp.where((z == 1) | (z == 2), total, permute(total, Z_OUT))


def allowed_mask(length, size):
    rows = lax.broadcasted_iota(jnp.int32, (size, size), 0)
    cols = lax.broadcasted_iota(jnp.int32, (size, size), 1)
    return (cols <= rows) & (cols < length)


def near_diagonal(size, reach):
    rows = lax.broadcasted_iota(jnp.int32, (size, size), 0)
    cols = lax.broadcasted_iota(jnp.int32, (size, size), 1)
    return jnp.abs(rows - cols) <= reach


def dot_nn(a, b):
    return lax.dot_general(a, b, (((1,), (0,)), ((), ())), preferred_element_type=F32)


def dot_nt(a, b):
    return lax.dot_general(a, b, (((1,), (1,)), ((), ())), preferred_element_type=F32)


def dot_tn(a, b):
    return lax.dot_general(a, b, (((0,), (0,)), ((), ())), preferred_element_type=F32)


def split_low(values):
    top = values.astype(BF16)
    return top, (values - top.astype(F32)).astype(BF16)


def attention_forward(projected, base_rows, head_mix, seq_lengths, lags, reach):
    heads = head_mix.shape[0]
    groups = heads // G
    seqs = seq_lengths.shape[0]
    size = projected.shape[0] // seqs

    def kernel(
        len_ref, mix_ref, base_ref, proj_ref, ctx_ref, p_ref,
        top_taps, low_taps, pad_top, pad_low, left_top, left_low, split, joined,
    ):
        seq = pl.program_id(0)

        @pl.when(seq == 0)
        def _():
            band = near_diagonal(size, reach)

            def build(h, carry):
                for a in range(lags):
                    row = jnp.broadcast_to(base_ref[h, a : a + 1, :], (size, size))
                    rolled = pltpu.roll(row, 0, 1, stride=1, stride_axis=0)
                    top, low = split_low(jnp.where(band, rolled, 0.0))
                    top_taps[h, a * size : (a + 1) * size, :] = top
                    low_taps[h, a * size : (a + 1) * size, :] = low
                return carry

            lax.fori_loop(0, heads, build, 0)
            pad_top[0:8, :] = jnp.zeros((8, size), F32)
            pad_low[0:8, :] = jnp.zeros((8, size), F32)

        for n in range(3 * heads):
            split[n] = proj_ref[:, n * E : (n + 1) * E]
        allowed = allowed_mask(len_ref[seq], size)

        def group_step(group, carry):
            probs = []
            for c in range(G):
                h = G * group + c
                raw = dot_nt(split[h], split[heads + h])
                masked = jnp.where(allowed, raw * SCALE, 0.0)
                top = masked.astype(BF16).astype(F32)
                pad_top[8 : 8 + size, :] = top
                pad_low[8 : 8 + size, :] = masked - top
                for a in range(lags):
                    cols = slice(a * size, (a + 1) * size)
                    left_top[:, cols] = pad_top[8 - a : 8 - a + size, :].astype(BF16)
                    left_low[:, cols] = pad_low[8 - a : 8 - a + size, :].astype(BF16)
                logits = (
                    dot_nn(left_top[...], top_taps[h])
                    + dot_nn(left_low[...], top_taps[h])
                    + dot_nn(left_top[...], low_taps[h])
                )
                logits = jnp.where(allowed, logits, -jnp.inf)
                terms = jnp.exp(logits - jnp.max(logits, axis=-1, keepdims=True))
                prob = terms * (1.0 / jnp.sum(terms, axis=-1, keepdims=True))
                p_ref[h, 0] = prob
                probs.append(prob)
            for c in range(G):
                h = G * group + c
                mixed = sum(mix_ref[h, i] * probs[i] for i in range(G))
                joined[h] = dot_nn(mixed.astype(BF16), split[2 * heads + h]).astype(BF16)
            return carry

        lax.fori_loop(0, groups, group_step, 0)
        for h in range(heads):
            ctx_ref[:, h * E : (h + 1) * E] = joined[h]

    flops = 2 * heads * seqs * size * size * (3 * lags * size + 2 * E)
    return pl.pallas_call(
        kernel,
        grid=(seqs,),
        out_shape=(
            jax.ShapeDtypeStruct((seqs * size, heads * E), BF16),
            jax.ShapeDtypeStruct((heads, seqs, size, size), F32),
        ),
        in_specs=[
            pl.BlockSpec(memory_space=pltpu.SMEM),
            pl.BlockSpec(memory_space=pltpu.SMEM),
            pl.BlockSpec((heads, 8, size), lambda s: (0, 0, 0)),
            pl.BlockSpec((size, 3 * heads * E), lambda s: (s, 0)),
        ],
        out_specs=(
            pl.BlockSpec((size, heads * E), lambda s: (s, 0)),
            pl.BlockSpec((heads, 1, size, size), lambda s: (0, s, 0, 0)),
        ),
        scratch_shapes=[
            pltpu.VMEM((heads, lags * size, size), BF16),
            pltpu.VMEM((heads, lags * size, size), BF16),
            pltpu.VMEM((size + 8, size), F32),
            pltpu.VMEM((size + 8, size), F32),
            pltpu.VMEM((size, lags * size), BF16),
            pltpu.VMEM((size, lags * size), BF16),
            pltpu.VMEM((3 * heads, size, E), BF16),
            pltpu.VMEM((heads, size, E), BF16),
        ],
        compiler_params=pltpu.CompilerParams(vmem_limit_bytes=48 << 20),
        cost_estimate=pl.CostEstimate(
            flops=flops, bytes_accessed=20 << 20, transcendentals=heads * seqs * size * size
        ),
    )(seq_lengths, head_mix, base_rows, projected)


def attention_backward(projected, probs, d_context, base_rows, head_mix, seq_lengths, lags, reach):
    heads = head_mix.shape[0]
    groups = heads // G
    seqs = seq_lengths.shape[0]
    size = projected.shape[0] // seqs

    def kernel(
        len_ref, mix_ref, base_ref, proj_ref, p_ref, dc_ref, dproj_ref, tap_ref, dmix_ref,
        back_taps, pad, left, products, split, split_dc, joined,
    ):
        seq = pl.program_id(0)
        rows = lax.broadcasted_iota(jnp.int32, (size, size), 0)
        cols = lax.broadcasted_iota(jnp.int32, (size, size), 1)

        @pl.when(seq == 0)
        def _():
            band = near_diagonal(size, reach)

            def build(h, carry):
                for a in range(lags):
                    row = jnp.broadcast_to(base_ref[h, a : a + 1, :], (size, size))
                    rolled = pltpu.roll(row, 0, 1, stride=1, stride_axis=0)
                    back_taps[h, a * size : (a + 1) * size, :] = jnp.where(
                        band, rolled, 0.0
                    ).astype(BF16)
                products[h] = jnp.zeros((size, lags * size), F32)
                return carry

            lax.fori_loop(0, heads, build, 0)
            pad[size : size + 8, :] = jnp.zeros((8, size), F32)
            dmix_ref[...] = jnp.zeros_like(dmix_ref)

        for n in range(3 * heads):
            split[n] = proj_ref[:, n * E : (n + 1) * E]
        for h in range(heads):
            split_dc[h] = dc_ref[:, h * E : (h + 1) * E]
        allowed = allowed_mask(len_ref[seq], size)
        reverse = (rows + cols == size - 1).astype(F32).astype(BF16)

        def group_step(group, carry):
            d_probs = [None] * G
            sums = []
            for c in range(G):
                h = G * group + c
                d_mixed = dot_nt(split_dc[h], split[2 * heads + h])
                mixed = sum(mix_ref[h, i] * p_ref[G * group + i, 0] for i in range(G))
                joined[2 * heads + h] = dot_tn(mixed.astype(BF16), split_dc[h]).astype(BF16)
                for i in range(G):
                    prob = p_ref[G * group + i, 0]
                    sums.append(jnp.sum(d_mixed * prob, axis=0, keepdims=True))
                    term = mix_ref[h, i] * d_mixed
                    d_probs[i] = term if d_probs[i] is None else d_probs[i] + term
            sums.append(jnp.zeros((8 - G * G, size), F32))
            dmix_ref[group] += jnp.concatenate(sums, axis=0)
            for c in range(G):
                h = G * group + c
                prob = p_ref[h, 0]
                weighted = prob * d_probs[c]
                pad[0:size, :] = weighted - prob * jnp.sum(weighted, axis=-1, keepdims=True)
                for a in range(lags):
                    left[:, a * size : (a + 1) * size] = pad[a : a + size, :].astype(BF16)
                d_masked = dot_nn(left[...], back_taps[h])
                raw = dot_nt(split[h], split[heads + h])
                masked = jnp.where(allowed, raw * SCALE, 0.0).astype(BF16)
                turned = dot_nn(masked, reverse).astype(BF16)
                products[h] += dot_tn(turned, left[...])
                d_raw = jnp.where(allowed, d_masked * SCALE, 0.0).astype(BF16)
                joined[h] = dot_nn(d_raw, split[heads + h]).astype(BF16)
                joined[heads + h] = dot_tn(d_raw, split[h]).astype(BF16)
            return carry

        lax.fori_loop(0, groups, group_step, 0)
        for n in range(3 * heads):
            dproj_ref[:, n * E : (n + 1) * E] = joined[n]

        @pl.when(seq == seqs - 1)
        def _():
            band = jnp.abs(size - 1 - rows - cols) <= reach

            def collect(h, carry):
                for a in range(lags):
                    kept = jnp.where(band, products[h, :, a * size : (a + 1) * size], 0.0)
                    rolled = pltpu.roll(kept, 0, 1, stride=1, stride_axis=0)
                    tap_ref[h, a : a + 1, :] = jnp.sum(rolled, axis=0, keepdims=True)
                tap_ref[h, lags:8, :] = jnp.zeros((8 - lags, size), F32)
                return carry

            lax.fori_loop(0, heads, collect, 0)

    flops = 2 * heads * seqs * size * size * ((2 * lags + 1) * size + 5 * E)
    d_projected, taps_rows, mix_rows = pl.pallas_call(
        kernel,
        grid=(seqs,),
        out_shape=(
            jax.ShapeDtypeStruct(projected.shape, BF16),
            jax.ShapeDtypeStruct((heads, 8, size), F32),
            jax.ShapeDtypeStruct((groups, 8, size), F32),
        ),
        in_specs=[
            pl.BlockSpec(memory_space=pltpu.SMEM),
            pl.BlockSpec(memory_space=pltpu.SMEM),
            pl.BlockSpec((heads, 8, size), lambda s: (0, 0, 0)),
            pl.BlockSpec((size, 3 * heads * E), lambda s: (s, 0)),
            pl.BlockSpec((heads, 1, size, size), lambda s: (0, s, 0, 0)),
            pl.BlockSpec((size, heads * E), lambda s: (s, 0)),
        ],
        out_specs=(
            pl.BlockSpec((size, 3 * heads * E), lambda s: (s, 0)),
            pl.BlockSpec((heads, 8, size), lambda s: (0, 0, 0)),
            pl.BlockSpec((groups, 8, size), lambda s: (0, 0, 0)),
        ),
        scratch_shapes=[
            pltpu.VMEM((heads, lags * size, size), BF16),
            pltpu.VMEM((size + 8, size), F32),
            pltpu.VMEM((size, lags * size), BF16),
            pltpu.VMEM((heads, size, lags * size), F32),
            pltpu.VMEM((3 * heads, size, E), BF16),
            pltpu.VMEM((heads, size, E), BF16),
            pltpu.VMEM((3 * heads, size, E), BF16),
        ],
        compiler_params=pltpu.CompilerParams(vmem_limit_bytes=52 << 20),
        cost_estimate=pl.CostEstimate(
            flops=flops, bytes_accessed=20 << 20, transcendentals=0
        ),
    )(seq_lengths, head_mix, base_rows, projected, probs, d_context)
    shifts = 2 * reach + 1
    at = [(size - 1 - reach + b) % size for b in range(shifts)]
    taps_grad = jnp.stack([taps_rows[:, :lags, i] for i in at], axis=-1)
    mix_grad = jnp.sum(mix_rows[:, : G * G], axis=-1).reshape(heads, G)
    return d_projected, taps_grad, mix_grad


def base_rows_of(taps, size, turned):
    heads, lags, shifts = taps.shape
    reach = shifts // 2
    rows = taps[:, :, ::-1] if turned else taps
    rows = jnp.concatenate(
        [rows[:, :, reach:], jnp.zeros((heads, lags, size - shifts), F32), rows[:, :, :reach]],
        axis=-1,
    )
    return jnp.pad(rows, ((0, 0), (0, 8 - lags), (0, 0)))


HIDDEN_BLOCK = 256


def feed_forward(second, second_turned, d_final, gateup, down):
    tokens, width = second.shape
    hidden_count = down.shape[0]
    block = HIDDEN_BLOCK
    part = tokens // 2

    def kernel(x_ref, xt_ref, d_ref, gu_ref, down_ref, hidden_ref, dgu_ref, grad_ref):
        for m in range(0, tokens, part):
            rows = slice(m, m + part)
            gate_up = dot_nn(x_ref[rows, :], gu_ref[...])
            gate, up = gate_up[:, :block], gate_up[:, block:]
            sig = jax.nn.sigmoid(gate)
            silu = gate * sig
            hidden_ref[rows, :] = (silu * up).astype(BF16)
            d_hidden = dot_nt(d_ref[rows, :], down_ref[...])
            d_gate = d_hidden * up * sig * (1.0 + gate * (1.0 - sig))
            dgu_ref[rows, :block] = d_gate.astype(BF16)
            dgu_ref[rows, block:] = (d_hidden * silu).astype(BF16)
        grad_ref[...] = dot_nn(xt_ref[...], dgu_ref[...]).astype(BF16)

    def whole(shape):
        return pl.BlockSpec(shape, lambda j: (0, 0), pipeline_mode=pl.Buffered(1))

    return pl.pallas_call(
        kernel,
        grid=(hidden_count // block,),
        out_shape=(
            jax.ShapeDtypeStruct((tokens, hidden_count), BF16),
            jax.ShapeDtypeStruct((tokens, 2 * hidden_count), BF16),
            jax.ShapeDtypeStruct((width, 2 * hidden_count), BF16),
        ),
        in_specs=[
            whole((tokens, width)),
            whole((width, tokens)),
            whole((tokens, width)),
            pl.BlockSpec((width, 2 * block), lambda j: (0, j)),
            pl.BlockSpec((block, width), lambda j: (j, 0)),
        ],
        out_specs=(
            pl.BlockSpec((tokens, block), lambda j: (0, j)),
            pl.BlockSpec((tokens, 2 * block), lambda j: (0, j)),
            pl.BlockSpec((width, 2 * block), lambda j: (0, j)),
        ),
        compiler_params=pltpu.CompilerParams(vmem_limit_bytes=52 << 20),
        cost_estimate=pl.CostEstimate(
            flops=10 * tokens * width * hidden_count,
            bytes_accessed=48 << 20,
            transcendentals=tokens * hidden_count,
        ),
    )(second, second_turned, d_final, gateup, down)


def rms_scale(values):
    return lax.rsqrt(jnp.mean(values * values, axis=-1, keepdims=True) + EPSILON)


def norm_back(values, scale_rows, gain_row, upstream):
    normal_rows = values * scale_rows
    gain_grad = jnp.sum(upstream * normal_rows, axis=0)
    weighted = upstream * gain_row
    values_grad = scale_rows * (
        weighted - normal_rows * jnp.mean(weighted * normal_rows, axis=-1, keepdims=True)
    )
    return (gain_grad, values_grad)


def matmul(a, b, dims, out=F32):
    return lax.dot_general(a, b, (dims, ((), ())), preferred_element_type=F32).astype(out)


def nesterov(master, moment, average, gradient, step_rate):
    new_moment = MOMENTUM * moment + gradient
    new_master = master - step_rate * (gradient + MOMENTUM * new_moment)
    return (new_moment, new_master, AVERAGE * average + (1.0 - AVERAGE) * new_master)


def on_device(
    inputs,
    cotangent,
    lengths,
    gains,
    gains_momentum,
    gains_average,
    qkv_weight,
    qkv_momentum,
    qkv_average,
    out_weight,
    out_momentum,
    out_average,
    conv_taps,
    taps_momentum,
    taps_average,
    head_mix,
    mix_momentum,
    mix_average,
    gateup_weight,
    gateup_momentum,
    gateup_average,
    down_weight,
    down_momentum,
    down_average,
):
    micro_count, seq_count, seq_len, width = inputs.shape
    lags, shifts = conv_taps.shape[1:]
    reach = shifts // 2
    core = lax.axis_index("narrow")
    me = lax.axis_index("wide")
    wide = lax.axis_size("wide")
    cores = lax.axis_size("narrow")
    rows = width // wide
    own_heads = H // cores
    own_cols = own_heads * E
    hidden_all = gateup_weight.shape[2]
    own_hidden = hidden_all // cores
    units = hidden_all // (wide * cores)
    tokens = micro_count * seq_count * seq_len

    def by_core(mine, other, axis):
        return jnp.where(
            core == 0,
            jnp.concatenate([mine, other], axis=axis),
            jnp.concatenate([other, mine], axis=axis),
        )

    def core_part(values, axis):
        return lax.dynamic_index_in_dim(values, core, axis, keepdims=False)

    def other_part(values, axis):
        return lax.dynamic_index_in_dim(values, 1 - core, axis, keepdims=False)

    def rows_of_core(values, axis):
        shape = values.shape
        split = values.reshape(
            shape[:axis] + (cores, shape[axis] // cores) + shape[axis + 1 :]
        )
        return core_part(split, axis), other_part(split, axis)

    gains_full = gather_small(gains.astype(BF16)).transpose(1, 0, 2)
    gains_full = gains_full.reshape(2, width).astype(F32)
    qkv_piece = rows_of_core(qkv_weight.astype(BF16).transpose(1, 0, 2), 2)[0]
    qkv_piece = qkv_piece.reshape(rows, 3 * own_cols)
    out_piece = rows_of_core(out_weight.astype(BF16), 0)[0]
    group = HIDDEN_BLOCK // units
    gateup_split = gateup_weight.astype(BF16).reshape(rows, 2, wide // group, group, cores, units)
    gateup_piece = core_part(gateup_split, 4).transpose(0, 2, 1, 3, 4)
    gateup_piece = gateup_piece.reshape(rows, 2 * own_hidden)
    down_piece = rows_of_core(down_weight.astype(BF16), 0)[0]

    half = rows // cores
    qkv_lines = gather_begin(qkv_piece)
    rows_lines = gather_begin(jnp.concatenate([out_piece, down_piece]), qkv_lines[0][0])
    gateup_lines = gather_begin(gateup_piece, rows_lines[0][0])
    qkv_full = gather_end(qkv_lines)
    rows_full = gather_end(rows_lines, qkv_full)
    rows_full = rows_full.reshape(wide, half + units, width)
    out_half = rows_full[:, :half]
    out_full = by_core(out_half[:, None], swap_cores(out_half)[:, None], 1)
    out_full = out_full.reshape(width, width)
    down_full = rows_full[:, half:].reshape(own_hidden, width)

    states = inputs.reshape(tokens, width).astype(F32)
    first_scale = rms_scale(states)
    normed_own = (states * first_scale * gains_full[0]).astype(BF16)
    normed = jnp.concatenate([normed_own, swap_cores(normed_own)])
    d_final_own = cotangent.reshape(tokens, width)
    d_final = jnp.concatenate([d_final_own, swap_cores(d_final_own)])
    lengths_own = lengths.reshape(-1)
    seq_lengths = jnp.concatenate([lengths_own, swap_cores(lengths_own)])
    all_tokens = cores * tokens

    taps_own = rows_of_core(conv_taps, 0)[0]
    mix_own = rows_of_core(head_mix, 0)[0]

    projected = matmul(normed, qkv_full, ((1,), (0,)), BF16)
    context_own, probs = attention_forward(
        projected, base_rows_of(taps_own, seq_len, False), mix_own, seq_lengths, lags, reach
    )
    gateup_full = gather_end(gateup_lines, context_own)
    context = by_core(context_own[:tokens], swap_cores(context_own[tokens:]), 1)
    middle = states + matmul(context, out_full, ((1,), (0,)))
    second_scale = rms_scale(middle)
    second_own = (middle * second_scale * gains_full[1]).astype(BF16)
    second = jnp.concatenate([second_own, swap_cores(second_own)])

    hidden, d_gate_up, gateup_grad = feed_forward(
        second, second.T, d_final, gateup_full, down_full
    )
    gateup_share = lax.psum_scatter(gateup_grad, "wide", scatter_dimension=0, tiled=True)
    down_grad = matmul(hidden, d_final, ((0,), (0,)), BF16)
    d_second_parts = matmul(d_gate_up, gateup_full, ((1,), (1,)))
    d_second = d_second_parts[:tokens] + swap_cores(d_second_parts[tokens:])
    result_parts = matmul(hidden, down_full, ((1,), (0,)))
    output = middle + (result_parts[:tokens] + swap_cores(result_parts[tokens:]))
    output = output.astype(BF16).reshape(inputs.shape)

    d_output = d_final_own.astype(F32)
    second_gain, d_norm_two = norm_back(middle, second_scale, gains_full[1], d_second)
    d_middle = d_output + d_norm_two
    d_attended = d_middle.astype(BF16)
    d_context = matmul(d_attended, out_full, ((1,), (1,)), BF16)
    mine, theirs = rows_of_core(d_context, 1)
    d_context_all = jnp.concatenate([mine, swap_cores(theirs)])
    out_grad = matmul(context, d_attended, ((0,), (0,)), BF16).reshape(wide, rows, width)
    out_mine, out_theirs = rows_of_core(out_grad, 1)
    out_grad = fold(out_mine, swap_cores(out_theirs))
    rows_grad = jnp.concatenate([out_grad, down_grad.reshape(wide, units, width)], axis=1)
    rows_share = scatter_sum(rows_grad.reshape(-1, width))
    out_share, down_share = rows_share[:half], rows_share[half:]

    d_projected, taps_grad, mix_grad = attention_backward(
        projected,
        probs,
        d_context_all,
        base_rows_of(taps_own, seq_len, True),
        mix_own,
        seq_lengths,
        lags,
        reach,
    )
    qkv_grad = matmul(normed, d_projected, ((0,), (0,)), BF16)
    qkv_share = scatter_sum(qkv_grad)
    d_normed_parts = matmul(d_projected, qkv_full, ((1,), (1,)))
    d_normed = d_normed_parts[:tokens] + swap_cores(d_normed_parts[tokens:])
    first_gain, d_norm_one = norm_back(states, first_scale, gains_full[0], d_normed)
    input_grad = (d_middle + d_norm_one).astype(BF16).reshape(inputs.shape)

    def spread(values):
        held = jnp.zeros((cores,) + values.shape, F32)
        return lax.dynamic_update_index_in_dim(held, values, core, 0).reshape(-1)

    packed = jnp.concatenate([first_gain, second_gain, spread(taps_grad), spread(mix_grad)])
    packed = sum_small(packed)
    gains_grad = lax.dynamic_slice_in_dim(
        packed[: 2 * width].reshape(2, width), me * rows, rows, axis=1
    )
    taps_total = packed[2 * width : 2 * width + conv_taps.size].reshape(conv_taps.shape)
    mix_total = packed[2 * width + conv_taps.size :].reshape(head_mix.shape)

    qkv_other = swap_cores(qkv_share)
    qkv_total = by_core(
        qkv_share.reshape(rows, 3, own_cols), qkv_other.reshape(rows, 3, own_cols), 2
    ).transpose(1, 0, 2)
    rows_other = swap_cores(rows_share)
    out_total = by_core(out_share, rows_other[:half], 0)
    gateup_other = swap_cores(gateup_share)
    split_shape = (rows, wide // group, 2, group, 1, units)
    gateup_total = by_core(
        gateup_share.reshape(split_shape), gateup_other.reshape(split_shape), 4
    ).transpose(0, 2, 1, 3, 4, 5).reshape(gateup_weight.shape)
    down_total = by_core(down_share, rows_other[half:], 0)

    tokens_all = tokens * cores * wide

    def rate_for(position):
        return RATES[position] / math.sqrt(tokens_all * (seq_len if PER_PAIR[position] else 1))

    def step(master, moment, average, gradient, position):
        return nesterov(master, moment, average, gradient.astype(F32), rate_for(position))

    return (
        output,
        input_grad,
        *step(gains, gains_momentum, gains_average, gains_grad, 0),
        *step(qkv_weight, qkv_momentum, qkv_average, qkv_total, 1),
        *step(out_weight, out_momentum, out_average, out_total, 2),
        *step(conv_taps, taps_momentum, taps_average, taps_total, 3),
        *step(head_mix, mix_momentum, mix_average, mix_total, 4),
        *step(gateup_weight, gateup_momentum, gateup_average, gateup_total, 5),
        *step(down_weight, down_momentum, down_average, down_total, 6),
    )


def solution(mesh):
    batch = P(None, ("narrow", "wide"), None, None)
    gain = P(None, "wide")
    qkv = P(None, "wide", None)
    row = P("wide", None)
    row3 = P("wide", None, None)
    params = (gain,) * 3 + (qkv,) * 3 + (row,) * 3 + (P(),) * 6 + (row3,) * 3 + (row,) * 3
    return jax.shard_map(
        on_device,
        mesh=mesh,
        in_specs=(batch, batch, P(None, ("narrow", "wide"))) + params,
        out_specs=(batch, batch) + params,
        check_vma=False,
    )
```

```python
import math

import jax
import jax.numpy as jnp
from jax import lax
from jax.experimental import pallas as pl
from jax.experimental.pallas import tpu as pltpu
from jax.sharding import PartitionSpec as P

H = 16
E = 96
G = 2


EPSILON = 1e-05
MOMENTUM = 0.9
AVERAGE = 0.7
RATES = (0.1, 0.019, 0.19, 0.2, 0.5, 0.031, 0.0097)
PER_PAIR = (False, False, False, True, True, False, False)
F32 = jnp.float32
BF16 = jnp.bfloat16
SCALE = 1.0 / math.sqrt(E)


def permute(values, pairs):
    return lax.ppermute(values, "wide", pairs)


def swap_cores(values):
    return lax.ppermute(values, "narrow", [(0, 1), (1, 0)])


BLOCK = 16


def z_pairs(moves):
    return [(a * 4 + q, b * 4 + q) for a, b in moves for q in range(4)]


Z_PAIR = z_pairs([(0, 1), (1, 0), (2, 3), (3, 2)])
Z_MID = z_pairs([(1, 2), (2, 1)])
Z_OUT = z_pairs([(1, 0), (2, 3)])
Z_IN = z_pairs([(0, 1), (3, 2)])
X_PAIR = [(i, i ^ 1) for i in range(BLOCK)]
Y_PAIR = [(i, i ^ 2) for i in range(BLOCK)]


def after(values, *needed):
    def nothing(*refs):
        del refs

    return pl.pallas_call(
        nothing,
        out_shape=jax.ShapeDtypeStruct(values.shape, values.dtype),
        in_specs=[pl.BlockSpec(memory_space=pl.ANY)] * (1 + len(needed)),
        out_specs=pl.BlockSpec(memory_space=pl.ANY),
        input_output_aliases={0: 0},
    )(values, *needed)


def line_gather(piece):
    z = lax.axis_index("wide") // 4
    odd = (z % 2) == 1
    up = [permute(piece, z_pairs([(0, 1), (1, 2), (2, 3)]))]
    down = [permute(piece, z_pairs([(1, 0), (2, 1), (3, 2)]))]
    up.append(permute(up[0], z_pairs([(1, 2), (2, 3)])))
    down.append(permute(down[0], z_pairs([(1, 0), (2, 1)])))
    up.append(permute(up[1], z_pairs([(2, 3)])))
    down.append(permute(down[1], z_pairs([(1, 0)])))
    near = jnp.stack([jnp.where(odd, up[0], piece), jnp.where(odd, piece, down[0])])

    def by_place(*choices):
        return jnp.where(
            z < 2,
            jnp.where(z == 0, choices[0], choices[1]),
            jnp.where(z == 2, choices[2], choices[3]),
        )

    def far(*needed):
        up_last, down_last = after(up[2], *needed), after(down[2], *needed)
        return jnp.stack(
            [
                by_place(down[1], down[0], up[1], up_last),
                by_place(down_last, down[1], up[0], up[1]),
            ]
        )

    return near, far, up[1], down[1]


def line_and_plane(piece):
    z = lax.axis_index("wide") // 4
    odd = (z % 2) == 1

    def across(values, x_first):
        return (values, permute(values, X_PAIR), permute(values, Y_PAIR), x_first)

    own = across(piece, False)
    up = permute(piece, z_pairs([(0, 1), (1, 2), (2, 3)]))
    down = permute(piece, z_pairs([(1, 0), (2, 1), (3, 2)]))
    beside = across(jnp.where(odd, up, down), True)
    up_two = permute(after(up, *own[1:3]), z_pairs([(1, 2), (2, 3)]))
    down_two = permute(after(down, *own[1:3]), z_pairs([(1, 0), (2, 1)]))
    up_three = permute(after(up_two, *beside[1:3]), z_pairs([(2, 3)]))
    down_three = permute(after(down_two, *beside[1:3]), z_pairs([(1, 0)]))

    def by_place(*choices):
        return jnp.where(
            z < 2,
            jnp.where(z == 0, choices[0], choices[1]),
            jnp.where(z == 2, choices[2], choices[3]),
        )

    far0 = across(by_place(down_two, down, up_two, up_three), False)
    far1 = across(by_place(down_three, down_two, up, up_two), True)
    return [("own", own), ("beside", beside), ("far0", far0), ("far1", far1)]


def gather(piece, lines, widths, needed=()):
    count = lax.axis_size("wide")
    rows = piece.shape[0]
    starts = [sum(widths[:i]) for i in range(len(widths))]
    if count != BLOCK:
        full = lax.all_gather(piece, "wide", axis=0, tiled=True)
        return [full[:, low : low + width] for low, width in zip(starts, widths)]
    me = lax.axis_index("wide")
    index = jnp.stack([me // 4, me % 4]).astype(jnp.int32)
    arrays = []
    places = []
    for place, across in lines:
        kept, by_x, by_y, x_first = across
        both = permute(by_x, Y_PAIR) if x_first else permute(by_y, X_PAIR)
        for lane, array in enumerate((kept, by_x, by_y, both)):
            arrays.append(array)
            places.append((place, lane))

    def assemble(index_ref, *refs):
        out_refs, sems = refs[-1 - len(widths) : -1], refs[-1]
        z = index_ref[0]
        z_places = {"own": z, "beside": z ^ 1, "far0": 2 - (z // 2) * 2, "far1": 3 - (z // 2) * 2}
        copies = []
        for n, (place, lane) in enumerate(places):
            for out_ref, low, width in zip(out_refs, starts, widths):
                copies.append(
                    pltpu.make_async_copy(
                        refs[n].at[:, pl.ds(low, width)],
                        out_ref.at[z_places[place], index_ref[1] ^ lane],
                        sems.at[len(copies)],
                    )
                )
        for copy in copies:
            copy.start()
        for copy in copies:
            copy.wait()

    full = pl.pallas_call(
        assemble,
        out_shape=[jax.ShapeDtypeStruct((4, 4, rows, width), piece.dtype) for width in widths],
        in_specs=[pl.BlockSpec(memory_space=pltpu.SMEM)]
        + [pl.BlockSpec(memory_space=pl.ANY)] * (len(arrays) + len(needed)),
        out_specs=[pl.BlockSpec(memory_space=pltpu.VMEM)] * len(widths),
        scratch_shapes=[pltpu.SemaphoreType.DMA((len(arrays) * len(widths),))],
        compiler_params=pltpu.CompilerParams(vmem_limit_bytes=48 << 20),
    )(index, *arrays, *needed)
    return [part.reshape(count * rows, -1) for part in full]


def fold(*terms):
    return sum(term.astype(F32) for term in terms).astype(BF16)


def trade(values, bit, pairs):
    keep = lax.dynamic_index_in_dim(values, bit, 0, keepdims=False)
    give = lax.dynamic_index_in_dim(values, 1 - bit, 0, keepdims=False)
    return fold(keep, permute(give, pairs))


def line_begin(far):
    z = lax.axis_index("wide") // 4
    farthest = jnp.where(z < 2, far[1], far[0])
    up = permute(farthest, z_pairs([(0, 1)]))
    down = permute(farthest, z_pairs([(3, 2)]))
    return up, down


def line_middle(far, up, down):
    z = lax.axis_index("wide") // 4
    up = permute(fold(jnp.where(z == 0, far[0], far[1]), up), z_pairs([(0, 1), (1, 2)]))
    down = permute(fold(jnp.where(z == 3, far[1], far[0]), down), z_pairs([(3, 2), (2, 1)]))
    return up, down


def line_end(near, far, up, down):
    z = lax.axis_index("wide") // 4
    up = permute(
        fold(jnp.where(z == 1, far[0], near[1]), up), z_pairs([(0, 1), (1, 2), (2, 3)])
    )
    down = permute(
        fold(jnp.where(z == 2, far[1], near[0]), down), z_pairs([(3, 2), (2, 1), (1, 0)])
    )
    return fold(jnp.where(z % 2 == 1, near[1], near[0]), up, down)


def scatter_begin(*partials):
    count = lax.axis_size("wide")
    if count != BLOCK:
        return (jnp.concatenate(partials, axis=1),), None
    me = lax.axis_index("wide")
    pair, y, x = me // 8, (me // 2) % 2, me % 2

    def block(half, y_at, x_at):
        found = []
        for partial in partials:
            rows, columns = partial.shape[0] // count, partial.shape[1]
            part = lax.dynamic_slice(
                partial.reshape(2, 2, 2, 2, rows, columns),
                (half, 0, y_at, x_at, 0, 0),
                (1, 2, 1, 1, rows, columns),
            )
            found.append(part.reshape(2, rows, columns))
        return jnp.concatenate(found, axis=2)

    out = (
        block(1 - pair, 1 - y, 1 - x),
        block(pair, 1 - y, 1 - x),
        block(1 - pair, 1 - y, x),
        block(pair, y, 1 - x),
    )
    return out, block


def scatter_first(out, block):
    if block is None:
        return ()
    return permute(out[0], Y_PAIR), permute(out[1], X_PAIR)


def scatter_plane(out, block, arrivals, needed):
    if block is None:
        return out
    me = lax.axis_index("wide")
    pair, y, x = me // 8, (me // 2) % 2, me % 2
    by_y, by_x = permute(out[2], Y_PAIR), after(permute(out[3], X_PAIR), *needed)
    far = fold(block(1 - pair, y, 1 - x), arrivals[0])
    near = fold(block(pair, 1 - y, x), arrivals[1])
    far = fold(block(1 - pair, y, x), by_y, permute(far, X_PAIR))
    near = fold(block(pair, y, x), by_x, permute(near, Y_PAIR))
    return near, far


def scatter_line(sums, *needed):
    if lax.axis_size("wide") != BLOCK:
        return lax.psum_scatter(sums[0], "wide", scatter_dimension=0, tiled=True)
    near, far = sums
    steps = line_middle(far, *line_begin(far))
    return line_end(after(near, *needed), far, *steps)


def pair_groups():
    count = lax.axis_size("wide")
    return [[i for i in range(count) if i % 2 == x] for x in range(2)]


def x_pairs():
    return [(i, i ^ 1) for i in range(lax.axis_size("wide"))]


def both_by(bit, mine, other):
    return jnp.where(bit == 0, jnp.stack([mine, other]), jnp.stack([other, mine]))


def ff_pair(mine, theirs):
    return both_by(lax.axis_index("wide") % 2, mine, permute(theirs, x_pairs()))


def ff_cross(lines):
    return permute(lines, Y_PAIR)


def ff_end(arrays, rows, units):
    count = lax.axis_size("wide")
    tall, columns = arrays[0].shape[-2:]
    cols = (rows * count) // columns
    blocks = (tall - cols * units) // rows
    gateup_shape = (blocks, count * rows, columns)
    down_shape = (count * units, cols * columns)
    if count != BLOCK:
        full = lax.all_gather(arrays[0], "wide", axis_index_groups=pair_groups())
        full = full.reshape(count, tall, columns)
        gateup = full[:, : blocks * rows].reshape(count, blocks, rows, columns)
        down = full[:, blocks * rows :].reshape(count, cols, units, columns)
        return (
            gateup.transpose(1, 0, 2, 3).reshape(gateup_shape),
            down.transpose(0, 2, 1, 3).reshape(down_shape),
        )
    me = lax.axis_index("wide")
    index = jnp.stack([me // 8, (me // 2) % 2]).astype(jnp.int32)

    def assemble(index_ref, *refs):
        gateup_ref, down_ref, sems = refs[len(arrays) :]
        copies = []

        def copy(source, target):
            copies.append(pltpu.make_async_copy(source, target, sems.at[len(copies)]))

        for n in range(len(arrays)):
            half, lane = n // 2, n % 2
            for z in range(2):
                for x in range(2):
                    z_at = 2 * (index_ref[0] ^ half) + z
                    at = z_at * 4 + (index_ref[1] ^ lane) * 2 + x
                    source = refs[n].at[z, x]
                    for j in range(blocks):
                        target = gateup_ref.at[j, pl.ds(pl.multiple_of(at * rows, 16), rows)]
                        copy(source.at[pl.ds(j * rows, rows)], target)
                    for i in range(cols):
                        target = down_ref.at[
                            pl.ds(pl.multiple_of(at * units, 16), units),
                            pl.ds(i * columns, columns),
                        ]
                        copy(source.at[pl.ds(blocks * rows + i * units, units)], target)
        for started in copies:
            started.start()
        for started in copies:
            started.wait()

    return pl.pallas_call(
        assemble,
        out_shape=(
            jax.ShapeDtypeStruct(gateup_shape, BF16),
            jax.ShapeDtypeStruct(down_shape, BF16),
        ),
        in_specs=[pl.BlockSpec(memory_space=pltpu.SMEM)]
        + [pl.BlockSpec(memory_space=pl.ANY)] * len(arrays),
        out_specs=(pl.BlockSpec(memory_space=pltpu.VMEM),) * 2,
        scratch_shapes=[pltpu.SemaphoreType.DMA((len(arrays) * 4 * (blocks + cols),))],
        compiler_params=pltpu.CompilerParams(vmem_limit_bytes=48 << 20),
    )(index, *arrays)


def ff_part(gateup_grad, down_grad, half, y):
    parts = []
    for grad in (gateup_grad, down_grad):
        blocks = grad.reshape((2, 2, 2, 2) + grad.shape[1:])
        found = lax.dynamic_slice(
            blocks, (half, 0, y, 0, 0, 0), (1, 2, 1, 2) + grad.shape[1:]
        )
        parts.append(found.reshape((2, 2) + grad.shape[1:]))
    return jnp.concatenate(parts, axis=2)


def ff_scatter_whole(gateup_grad, down_grad):
    packed = jnp.concatenate([gateup_grad, down_grad], axis=1)
    return lax.psum_scatter(
        packed.reshape((packed.shape[0] // 2, 2) + packed.shape[1:]),
        "wide",
        scatter_dimension=0,
        axis_index_groups=pair_groups(),
    )


def ff_last(total):
    x = lax.axis_index("wide") % 2
    keep = lax.dynamic_index_in_dim(total, x, 0, keepdims=False)
    give = lax.dynamic_index_in_dim(total, 1 - x, 0, keepdims=False)
    return keep, permute(give, x_pairs())


def gather_small(values):
    if lax.axis_size("wide") != BLOCK:
        return lax.all_gather(values, "wide")
    me = lax.axis_index("wide")
    pair, y, x = me // 8, (me // 2) % 2, me % 2

    def both(mine, other, bit):
        return jnp.where(bit == 0, jnp.stack([mine, other]), jnp.stack([other, mine]))

    row = both(values, permute(values, X_PAIR), x)
    plane = both(row, permute(row, Y_PAIR), y)
    near, far = line_gather(plane)[:2]
    return both(near, far(), pair).reshape((BLOCK,) + values.shape)


def sum_small(values):
    values = values + swap_cores(values)
    if lax.axis_size("wide") != BLOCK:
        return lax.psum(values, "wide")
    corner = [(i, i ^ 3) for i in range(BLOCK)]
    values = (values + permute(values, X_PAIR)) + (
        permute(values, Y_PAIR) + permute(values, corner)
    )
    one, two, three = (
        permute(values, z_pairs([(z, (z + hop) % 4) for z in range(4)])) for hop in (1, 2, 3)
    )
    return (values + two) + (one + three)


def allowed_mask(length, size):
    rows = lax.broadcasted_iota(jnp.int32, (size, size), 0)
    cols = lax.broadcasted_iota(jnp.int32, (size, size), 1)
    return (cols <= rows) & (cols < length)


def near_diagonal(size, reach):
    rows = lax.broadcasted_iota(jnp.int32, (size, size), 0)
    cols = lax.broadcasted_iota(jnp.int32, (size, size), 1)
    return jnp.abs(rows - cols) <= reach


def dot_nn(a, b):
    return lax.dot_general(a, b, (((1,), (0,)), ((), ())), preferred_element_type=F32)


def dot_nt(a, b):
    return lax.dot_general(a, b, (((1,), (1,)), ((), ())), preferred_element_type=F32)


def dot_tn(a, b):
    return lax.dot_general(a, b, (((0,), (0,)), ((), ())), preferred_element_type=F32)


def split_low(values):
    top = values.astype(BF16)
    return top, (values - top.astype(F32)).astype(BF16)


def attention_forward(projected, base_rows, head_mix, seq_lengths, lags, reach):
    heads = head_mix.shape[0]
    groups = heads // G
    seqs = seq_lengths.shape[0]
    size = projected.shape[0] // seqs

    def kernel(
        len_ref, mix_ref, base_ref, proj_ref, ctx_ref, p_ref,
        top_taps, low_taps, pad_top, pad_low, left_top, left_low, split, joined,
    ):
        seq = pl.program_id(0)

        @pl.when(seq == 0)
        def _():
            band = near_diagonal(size, reach)

            def build(h, carry):
                for a in range(lags):
                    row = jnp.broadcast_to(base_ref[h, a : a + 1, :], (size, size))
                    rolled = pltpu.roll(row, 0, 1, stride=1, stride_axis=0)
                    top, low = split_low(jnp.where(band, rolled, 0.0))
                    top_taps[h, a * size : (a + 1) * size, :] = top
                    low_taps[h, a * size : (a + 1) * size, :] = low
                return carry

            lax.fori_loop(0, heads, build, 0)
            pad_top[0:8, :] = jnp.zeros((8, size), F32)
            pad_low[0:8, :] = jnp.zeros((8, size), F32)

        for n in range(3 * heads):
            split[n] = proj_ref[:, n * E : (n + 1) * E]
        allowed = allowed_mask(len_ref[seq], size)

        def group_step(group, carry):
            probs = []
            for c in range(G):
                h = G * group + c
                raw = dot_nt(split[h], split[heads + h])
                masked = jnp.where(allowed, raw * SCALE, 0.0)
                top = masked.astype(BF16).astype(F32)
                pad_top[8 : 8 + size, :] = top
                pad_low[8 : 8 + size, :] = masked - top
                for a in range(lags):
                    cols = slice(a * size, (a + 1) * size)
                    left_top[:, cols] = pad_top[8 - a : 8 - a + size, :].astype(BF16)
                    left_low[:, cols] = pad_low[8 - a : 8 - a + size, :].astype(BF16)
                logits = (
                    dot_nn(left_top[...], top_taps[h])
                    + dot_nn(left_low[...], top_taps[h])
                    + dot_nn(left_top[...], low_taps[h])
                )
                logits = jnp.where(allowed, logits, -jnp.inf)
                terms = jnp.exp(logits - jnp.max(logits, axis=-1, keepdims=True))
                prob = terms * (1.0 / jnp.sum(terms, axis=-1, keepdims=True))
                p_ref[h, 0] = prob
                probs.append(prob)
            for c in range(G):
                h = G * group + c
                mixed = sum(mix_ref[h, i] * probs[i] for i in range(G))
                joined[h] = dot_nn(mixed.astype(BF16), split[2 * heads + h]).astype(BF16)
            return carry

        lax.fori_loop(0, groups, group_step, 0)
        for h in range(heads):
            ctx_ref[:, h * E : (h + 1) * E] = joined[h]

    flops = 2 * heads * seqs * size * size * (3 * lags * size + 2 * E)
    return pl.pallas_call(
        kernel,
        grid=(seqs,),
        out_shape=(
            jax.ShapeDtypeStruct((seqs * size, heads * E), BF16),
            jax.ShapeDtypeStruct((heads, seqs, size, size), F32),
        ),
        in_specs=[
            pl.BlockSpec(memory_space=pltpu.SMEM),
            pl.BlockSpec(memory_space=pltpu.SMEM),
            pl.BlockSpec((heads, 8, size), lambda s: (0, 0, 0)),
            pl.BlockSpec((size, 3 * heads * E), lambda s: (s, 0)),
        ],
        out_specs=(
            pl.BlockSpec((size, heads * E), lambda s: (s, 0)),
            pl.BlockSpec((heads, 1, size, size), lambda s: (0, s, 0, 0)),
        ),
        scratch_shapes=[
            pltpu.VMEM((heads, lags * size, size), BF16),
            pltpu.VMEM((heads, lags * size, size), BF16),
            pltpu.VMEM((size + 8, size), F32),
            pltpu.VMEM((size + 8, size), F32),
            pltpu.VMEM((size, lags * size), BF16),
            pltpu.VMEM((size, lags * size), BF16),
            pltpu.VMEM((3 * heads, size, E), BF16),
            pltpu.VMEM((heads, size, E), BF16),
        ],
        compiler_params=pltpu.CompilerParams(vmem_limit_bytes=48 << 20),
        cost_estimate=pl.CostEstimate(
            flops=flops, bytes_accessed=20 << 20, transcendentals=heads * seqs * size * size
        ),
    )(seq_lengths, head_mix, base_rows, projected)


def attention_backward(projected, probs, d_context, base_rows, head_mix, seq_lengths, lags, reach):
    heads = head_mix.shape[0]
    groups = heads // G
    seqs = seq_lengths.shape[0]
    size = projected.shape[0] // seqs

    def kernel(
        len_ref, mix_ref, base_ref, proj_ref, p_ref, dc_ref, dproj_ref, tap_ref, dmix_ref,
        back_taps, pad, left, products, split, split_dc, joined,
    ):
        seq = pl.program_id(0)
        rows = lax.broadcasted_iota(jnp.int32, (size, size), 0)
        cols = lax.broadcasted_iota(jnp.int32, (size, size), 1)

        @pl.when(seq == 0)
        def _():
            band = near_diagonal(size, reach)

            def build(h, carry):
                for a in range(lags):
                    row = jnp.broadcast_to(base_ref[h, a : a + 1, :], (size, size))
                    rolled = pltpu.roll(row, 0, 1, stride=1, stride_axis=0)
                    back_taps[h, a * size : (a + 1) * size, :] = jnp.where(
                        band, rolled, 0.0
                    ).astype(BF16)
                products[h] = jnp.zeros((size, lags * size), F32)
                return carry

            lax.fori_loop(0, heads, build, 0)
            pad[size : size + 8, :] = jnp.zeros((8, size), F32)
            dmix_ref[...] = jnp.zeros_like(dmix_ref)

        for n in range(3 * heads):
            split[n] = proj_ref[:, n * E : (n + 1) * E]
        for h in range(heads):
            split_dc[h] = dc_ref[:, h * E : (h + 1) * E]
        allowed = allowed_mask(len_ref[seq], size)
        reverse = (rows + cols == size - 1).astype(F32).astype(BF16)

        def group_step(group, carry):
            d_probs = [None] * G
            sums = []
            for c in range(G):
                h = G * group + c
                d_mixed = dot_nt(split_dc[h], split[2 * heads + h])
                mixed = sum(mix_ref[h, i] * p_ref[G * group + i, 0] for i in range(G))
                joined[2 * heads + h] = dot_tn(mixed.astype(BF16), split_dc[h]).astype(BF16)
                for i in range(G):
                    prob = p_ref[G * group + i, 0]
                    sums.append(jnp.sum(d_mixed * prob, axis=0, keepdims=True))
                    term = mix_ref[h, i] * d_mixed
                    d_probs[i] = term if d_probs[i] is None else d_probs[i] + term
            sums.append(jnp.zeros((8 - G * G, size), F32))
            dmix_ref[group] += jnp.concatenate(sums, axis=0)
            for c in range(G):
                h = G * group + c
                prob = p_ref[h, 0]
                weighted = prob * d_probs[c]
                pad[0:size, :] = weighted - prob * jnp.sum(weighted, axis=-1, keepdims=True)
                for a in range(lags):
                    left[:, a * size : (a + 1) * size] = pad[a : a + size, :].astype(BF16)
                d_masked = dot_nn(left[...], back_taps[h])
                raw = dot_nt(split[h], split[heads + h])
                masked = jnp.where(allowed, raw * SCALE, 0.0).astype(BF16)
                turned = dot_nn(masked, reverse).astype(BF16)
                products[h] += dot_tn(turned, left[...])
                d_raw = jnp.where(allowed, d_masked * SCALE, 0.0).astype(BF16)
                joined[h] = dot_nn(d_raw, split[heads + h]).astype(BF16)
                joined[heads + h] = dot_tn(d_raw, split[h]).astype(BF16)
            return carry

        lax.fori_loop(0, groups, group_step, 0)
        for n in range(3 * heads):
            dproj_ref[:, n * E : (n + 1) * E] = joined[n]

        @pl.when(seq == seqs - 1)
        def _():
            band = jnp.abs(size - 1 - rows - cols) <= reach

            def collect(h, carry):
                for a in range(lags):
                    kept = jnp.where(band, products[h, :, a * size : (a + 1) * size], 0.0)
                    rolled = pltpu.roll(kept, 0, 1, stride=1, stride_axis=0)
                    tap_ref[h, a : a + 1, :] = jnp.sum(rolled, axis=0, keepdims=True)
                tap_ref[h, lags:8, :] = jnp.zeros((8 - lags, size), F32)
                return carry

            lax.fori_loop(0, heads, collect, 0)

    flops = 2 * heads * seqs * size * size * ((2 * lags + 1) * size + 5 * E)
    d_projected, taps_rows, mix_rows = pl.pallas_call(
        kernel,
        grid=(seqs,),
        out_shape=(
            jax.ShapeDtypeStruct(projected.shape, BF16),
            jax.ShapeDtypeStruct((heads, 8, size), F32),
            jax.ShapeDtypeStruct((groups, 8, size), F32),
        ),
        in_specs=[
            pl.BlockSpec(memory_space=pltpu.SMEM),
            pl.BlockSpec(memory_space=pltpu.SMEM),
            pl.BlockSpec((heads, 8, size), lambda s: (0, 0, 0)),
            pl.BlockSpec((size, 3 * heads * E), lambda s: (s, 0)),
            pl.BlockSpec((heads, 1, size, size), lambda s: (0, s, 0, 0)),
            pl.BlockSpec((size, heads * E), lambda s: (s, 0)),
        ],
        out_specs=(
            pl.BlockSpec((size, 3 * heads * E), lambda s: (s, 0)),
            pl.BlockSpec((heads, 8, size), lambda s: (0, 0, 0)),
            pl.BlockSpec((groups, 8, size), lambda s: (0, 0, 0)),
        ),
        scratch_shapes=[
            pltpu.VMEM((heads, lags * size, size), BF16),
            pltpu.VMEM((size + 8, size), F32),
            pltpu.VMEM((size, lags * size), BF16),
            pltpu.VMEM((heads, size, lags * size), F32),
            pltpu.VMEM((3 * heads, size, E), BF16),
            pltpu.VMEM((heads, size, E), BF16),
            pltpu.VMEM((3 * heads, size, E), BF16),
        ],
        compiler_params=pltpu.CompilerParams(vmem_limit_bytes=52 << 20),
        cost_estimate=pl.CostEstimate(
            flops=flops, bytes_accessed=20 << 20, transcendentals=0
        ),
    )(seq_lengths, head_mix, base_rows, projected, probs, d_context)
    shifts = 2 * reach + 1
    at = [(size - 1 - reach + b) % size for b in range(shifts)]
    taps_grad = jnp.stack([taps_rows[:, :lags, i] for i in at], axis=-1)
    mix_grad = jnp.sum(mix_rows[:, : G * G], axis=-1).reshape(heads, G)
    return d_projected, taps_grad, mix_grad


def base_rows_of(taps, size, turned):
    heads, lags, shifts = taps.shape
    reach = shifts // 2
    rows = taps[:, :, ::-1] if turned else taps
    rows = jnp.concatenate(
        [rows[:, :, reach:], jnp.zeros((heads, lags, size - shifts), F32), rows[:, :, :reach]],
        axis=-1,
    )
    return jnp.pad(rows, ((0, 0), (0, 8 - lags), (0, 0)))


HIDDEN_BLOCK = 256


def feed_forward(seconds, d_finals, gateup, down, count):
    part, width = seconds[0].shape
    tokens = 4 * part
    blocks = gateup.shape[0]
    block = HIDDEN_BLOCK
    rows, units = width // count, down.shape[0] // count
    cols = width // (2 * block)
    packed = count == BLOCK

    def kernel(*refs):
        x_refs, d_refs, (gu_ref, down_ref) = refs[:4], refs[4:8], refs[8:10]
        hidden_ref, dgu_ref, grad_ref, down_grad_ref, turned = refs[10:]

        @pl.when(pl.program_id(0) == 0)
        def _():
            for m in range(0, tokens, 256):
                source = x_refs[m // part][m % part : m % part + 256, :]
                turned[:, m : m + 256] = source.T

        down_grad = None
        for n in range(4):
            at = slice(n * part, (n + 1) * part)
            gate_up = dot_nn(x_refs[n][...], gu_ref[0])
            gate, up = gate_up[:, :block], gate_up[:, block:]
            sig = jax.nn.sigmoid(gate)
            silu = gate * sig
            hidden = (silu * up).astype(BF16)
            hidden_ref[at, :] = hidden
            d_hidden = dot_nt(d_refs[n][...], down_ref[...])
            d_gate = d_hidden * up * sig * (1.0 + gate * (1.0 - sig))
            dgu_ref[at, :block] = d_gate.astype(BF16)
            dgu_ref[at, block:] = (d_hidden * silu).astype(BF16)
            term = dot_tn(hidden, d_refs[n][...])
            down_grad = term if down_grad is None else down_grad + term
        grad = dot_nn(turned[...], dgu_ref[...]).astype(BF16)
        down_grad = down_grad.astype(BF16)
        if packed:
            grad_ref[...] = grad.reshape(count, rows, 2 * block)
            for i in range(cols):
                columns = down_grad[:, i * 2 * block : (i + 1) * 2 * block]
                down_grad_ref[:, i * units : (i + 1) * units, :] = columns.reshape(
                    block // units, units, 2 * block
                )
        else:
            grad_ref[0] = grad
            down_grad_ref[...] = down_grad

    def whole(shape):
        return pl.BlockSpec(shape, lambda j: (0, 0), pipeline_mode=pl.Buffered(1))

    gateup_part = pl.BlockSpec((1, width, 2 * block), lambda j: (j, 0, 0))
    down_part = pl.BlockSpec((block, width), lambda j: (j, 0))
    if packed:
        grad_shapes = ((count, blocks * rows, 2 * block), (count, cols * units, 2 * block))
        grad_specs = (
            pl.BlockSpec((count, rows, 2 * block), lambda j: (0, j, 0)),
            pl.BlockSpec((block // units, cols * units, 2 * block), lambda j: (j, 0, 0)),
        )
    else:
        grad_shapes = (gateup.shape, down.shape)
        grad_specs = (gateup_part, down_part)
    hidden, d_gate_up, gateup_grad, down_grad = pl.pallas_call(
        kernel,
        grid=(blocks,),
        out_shape=(
            jax.ShapeDtypeStruct((tokens, blocks * block), BF16),
            jax.ShapeDtypeStruct((tokens, 2 * blocks * block), BF16),
        )
        + tuple(jax.ShapeDtypeStruct(shape, BF16) for shape in grad_shapes),
        in_specs=[whole((part, width))] * 8 + [gateup_part, down_part],
        out_specs=(
            pl.BlockSpec((tokens, block), lambda j: (0, j)),
            pl.BlockSpec((tokens, 2 * block), lambda j: (0, j)),
        )
        + grad_specs,
        scratch_shapes=[pltpu.VMEM((width, tokens), BF16)],
        compiler_params=pltpu.CompilerParams(vmem_limit_bytes=56 << 20),
        cost_estimate=pl.CostEstimate(
            flops=12 * tokens * width * blocks * block,
            bytes_accessed=48 << 20,
            transcendentals=tokens * blocks * block,
        ),
    )(*seconds, *d_finals, gateup, down)
    if not packed:
        gateup_grad = gateup_grad.reshape(blocks, count, rows, 2 * block)
        gateup_grad = gateup_grad.transpose(1, 0, 2, 3).reshape(count, -1, 2 * block)
        down_grad = down_grad.reshape(count, units, cols, 2 * block)
        down_grad = down_grad.transpose(0, 2, 1, 3).reshape(count, -1, 2 * block)
    return hidden, d_gate_up, gateup_grad, down_grad


def back_through_gateup(d_gate_up, gateup, first, count, kind, needed=()):
    blocks, width, columns = gateup.shape
    part = 256

    def kernel(d_ref, gu_ref, *refs):
        total = dot_nt(d_ref[:, :columns], gu_ref[0])
        for j in range(1, blocks):
            total = total + dot_nt(d_ref[:, j * columns : (j + 1) * columns], gu_ref[j])
        refs[-1][...] = total.astype(kind)

    return pl.pallas_call(
        kernel,
        grid=(count // part,),
        out_shape=jax.ShapeDtypeStruct((count, width), kind),
        in_specs=[
            pl.BlockSpec((part, blocks * columns), lambda m: (first // part + m, 0)),
            pl.BlockSpec(gateup.shape, lambda m: (0, 0, 0), pipeline_mode=pl.Buffered(1)),
        ]
        + [pl.BlockSpec(memory_space=pl.ANY)] * len(needed),
        out_specs=pl.BlockSpec((part, width), lambda m: (m, 0)),
        compiler_params=pltpu.CompilerParams(vmem_limit_bytes=48 << 20),
        cost_estimate=pl.CostEstimate(
            flops=2 * count * width * blocks * columns,
            bytes_accessed=16 << 20,
            transcendentals=0,
        ),
    )(d_gate_up, gateup, *needed)


def quarter_columns(wide, hidden_all):
    units = hidden_all // (4 * wide)
    return units, HIDDEN_BLOCK // units


def gateup_cast(weight, quarter):
    rows, _, hidden_all = weight.shape
    wide = lax.axis_size("wide")
    units, each = quarter_columns(wide, hidden_all)
    block = HIDDEN_BLOCK
    blocks = hidden_all // (4 * block)
    if wide != BLOCK:
        split = weight.astype(BF16).reshape(rows, 2, blocks, each, 4, units)
        split = split.transpose(4, 2, 0, 1, 3, 5).reshape(4, blocks * rows, 2 * block)
        return split[quarter], split[quarter ^ 2]

    def kernel(quarter_ref, in_ref, mine_ref, theirs_ref):
        found = []
        for t in range(4):
            parts = []
            for k in range(2):
                for w in range(each):
                    low = (4 * w + t) * units
                    parts.append(in_ref[:, k, low : low + units])
            found.append(jnp.concatenate(parts, axis=1).astype(BF16).astype(F32))
        for ref, flip in ((mine_ref, 0), (theirs_ref, 2)):
            at = quarter_ref[0] ^ flip
            chosen = found[0]
            for t in range(1, 4):
                chosen = jnp.where(at == t, found[t], chosen)
            ref[...] = chosen.astype(BF16)

    part = pl.BlockSpec((rows, 2 * block), lambda j: (j, 0))
    return pl.pallas_call(
        kernel,
        grid=(blocks,),
        out_shape=(jax.ShapeDtypeStruct((blocks * rows, 2 * block), BF16),) * 2,
        in_specs=[
            pl.BlockSpec(memory_space=pltpu.SMEM),
            pl.BlockSpec((rows, 2, 4 * block), lambda j: (0, 0, j)),
        ],
        out_specs=(part, part),
        compiler_params=pltpu.CompilerParams(vmem_limit_bytes=32 << 20),
    )(quarter.reshape(1).astype(jnp.int32), weight)


def gateup_step(master, moment, average, shares, quarter, rate):
    rows, _, hidden_all = master.shape
    wide = lax.axis_size("wide")
    units, each = quarter_columns(wide, hidden_all)
    block = HIDDEN_BLOCK
    blocks = hidden_all // (4 * block)
    if wide != BLOCK:
        split = jnp.stack(shares)[jnp.arange(4) ^ quarter]
        split = split.reshape(4, blocks, rows, 2, each, units).transpose(2, 3, 1, 4, 0, 5)
        return nesterov(
            master, moment, average, split.reshape(master.shape).astype(F32), rate
        )

    def kernel(quarter_ref, p_ref, m_ref, a_ref, *refs):
        ins, outs = refs[:4], refs[4:]
        given = [ref[...].astype(F32) for ref in ins]
        found = []
        for t in range(4):
            at = quarter_ref[0] ^ t
            chosen = given[0]
            for n in range(1, 4):
                chosen = jnp.where(at == n, given[n], chosen)
            found.append(chosen)
        for k in range(2):
            parts = []
            for w in range(each):
                low = k * block + w * units
                parts += [found[t][:, low : low + units] for t in range(4)]
            done = nesterov(
                p_ref[:, k, :], m_ref[:, k, :], a_ref[:, k, :], jnp.concatenate(parts, 1), rate
            )
            for ref, value in zip(outs, done):
                ref[:, k, :] = value

    whole = pl.BlockSpec((rows, 2, 4 * block), lambda j: (0, 0, j))
    part = pl.BlockSpec((rows, 2 * block), lambda j: (j, 0))
    return pl.pallas_call(
        kernel,
        grid=(blocks,),
        out_shape=(jax.ShapeDtypeStruct(master.shape, F32),) * 3,
        in_specs=[pl.BlockSpec(memory_space=pltpu.SMEM)] + [whole] * 3 + [part] * 4,
        out_specs=(whole,) * 3,
        compiler_params=pltpu.CompilerParams(vmem_limit_bytes=32 << 20),
    )(quarter.reshape(1).astype(jnp.int32), master, moment, average, *shares)


def rms_scale(values):
    return lax.rsqrt(jnp.mean(values * values, axis=-1, keepdims=True) + EPSILON)


def norm_back(values, scale_rows, gain_row, upstream):
    normal_rows = values * scale_rows
    gain_grad = jnp.sum(upstream * normal_rows, axis=0)
    weighted = upstream * gain_row
    values_grad = scale_rows * (
        weighted - normal_rows * jnp.mean(weighted * normal_rows, axis=-1, keepdims=True)
    )
    return (gain_grad, values_grad)


def matmul(a, b, dims, out=F32):
    return lax.dot_general(a, b, (dims, ((), ())), preferred_element_type=F32).astype(out)


def nesterov(master, moment, average, gradient, step_rate):
    new_moment = MOMENTUM * moment + gradient
    new_master = master - step_rate * (gradient + MOMENTUM * new_moment)
    return (new_moment, new_master, AVERAGE * average + (1.0 - AVERAGE) * new_master)


def on_device(
    inputs,
    cotangent,
    lengths,
    gains,
    gains_momentum,
    gains_average,
    qkv_weight,
    qkv_momentum,
    qkv_average,
    out_weight,
    out_momentum,
    out_average,
    conv_taps,
    taps_momentum,
    taps_average,
    head_mix,
    mix_momentum,
    mix_average,
    gateup_weight,
    gateup_momentum,
    gateup_average,
    down_weight,
    down_momentum,
    down_average,
):
    micro_count, seq_count, seq_len, width = inputs.shape
    lags, shifts = conv_taps.shape[1:]
    reach = shifts // 2
    core = lax.axis_index("narrow")
    me = lax.axis_index("wide")
    wide = lax.axis_size("wide")
    cores = lax.axis_size("narrow")
    rows = width // wide
    own_heads = H // cores
    own_cols = own_heads * E
    hidden_all = gateup_weight.shape[2]
    units = hidden_all // (wide * 2 * cores)
    quarter = (me % 2) * cores + core
    tokens = micro_count * seq_count * seq_len

    def by_core(mine, other, axis):
        return jnp.where(
            core == 0,
            jnp.concatenate([mine, other], axis=axis),
            jnp.concatenate([other, mine], axis=axis),
        )

    def core_part(values, axis):
        return lax.dynamic_index_in_dim(values, core, axis, keepdims=False)

    def other_part(values, axis):
        return lax.dynamic_index_in_dim(values, 1 - core, axis, keepdims=False)

    def rows_of_core(values, axis):
        shape = values.shape
        split = values.reshape(
            shape[:axis] + (cores, shape[axis] // cores) + shape[axis + 1 :]
        )
        return core_part(split, axis), other_part(split, axis)

    def to_beside(partial):
        other = swap_cores(partial[tokens:].astype(BF16))
        return fold(partial[:tokens], other)

    def on_chip(partial):
        other = swap_cores(partial[tokens:].astype(BF16))
        return partial[:tokens].astype(F32) + other.astype(F32)

    def when(values, *needed):
        return after(values, *needed) if wide == BLOCK else values

    qkv_piece = rows_of_core(qkv_weight.astype(BF16).transpose(1, 0, 2), 2)[0]
    qkv_piece = qkv_piece.reshape(rows, 3 * own_cols)
    gains_piece = jnp.pad(gains.T.astype(BF16), ((0, 0), (0, 126)))
    out_piece = rows_of_core(out_weight.astype(BF16), 1)[0]
    first_piece = jnp.concatenate([qkv_piece, out_piece, gains_piece], axis=1)
    widths = (3 * own_cols, width // cores, 128)
    wide_block = 2 * HIDDEN_BLOCK
    gateup_mine, gateup_theirs = gateup_cast(gateup_weight, quarter)
    down_split = down_weight.astype(BF16).reshape(4, units, width // wide_block, wide_block)
    down_split = down_split.transpose(0, 2, 1, 3).reshape(4, -1, wide_block)

    def ff_piece(gateup_part, at):
        down_part = lax.dynamic_index_in_dim(down_split, at, 0, keepdims=False)
        return jnp.concatenate([gateup_part, down_part])

    inputs_own = inputs.reshape(tokens, width)
    inputs_other = swap_cores(inputs_own)
    lengths_own = lengths.reshape(-1)
    seq_lengths = jnp.concatenate([lengths_own, swap_cores(lengths_own)])
    pair = ff_pair(ff_piece(gateup_mine, quarter), ff_piece(gateup_theirs, quarter ^ 2))
    if wide == BLOCK:
        first_lines = line_and_plane(first_piece)
        ff_lines = line_gather(after(pair, first_lines[2][1][0], first_lines[3][1][0]))
        first_full = gather(first_piece, first_lines, widths, ff_lines[2:])
    else:
        first_full = gather(first_piece, None, widths)
    qkv_full, out_half, gains_full = first_full
    gains_full = gains_full[:, :2].T.astype(F32)
    out_full = by_core(out_half, swap_cores(out_half), 1)
    out_mine, out_theirs = rows_of_core(out_full, 0)

    states = inputs_own.astype(F32)
    first_scale = rms_scale(states)

    def first_norm(values):
        values = values.astype(F32)
        return (values * rms_scale(values) * gains_full[0]).astype(BF16)

    normed = jnp.concatenate([first_norm(inputs_own), first_norm(inputs_other)])
    d_final_own = cotangent.reshape(tokens, width)
    d_final_beside = permute(when(d_final_own, qkv_full), x_pairs())
    d_finals = [d_final_own, swap_cores(d_final_own), d_final_beside, swap_cores(d_final_beside)]
    all_tokens = cores * tokens

    taps_own = rows_of_core(conv_taps, 0)[0]
    mix_own = rows_of_core(head_mix, 0)[0]

    projected = matmul(normed, qkv_full, ((1,), (0,)), BF16)
    if wide == BLOCK:
        ff_near = after(ff_lines[0], qkv_full)
        ff_near_across = ff_cross(ff_near)
        ff_far = ff_lines[1](projected)
        ff_far_across = ff_cross(ff_far)
    context_own, probs = attention_forward(
        projected, base_rows_of(taps_own, seq_len, False), mix_own, seq_lengths, lags, reach
    )
    if wide == BLOCK:
        context_own = after(context_own, ff_near_across, d_final_beside)
        ff_arrays = (ff_near, ff_near_across, ff_far, ff_far_across)
    else:
        ff_arrays = (pair,)
    gateup_full, down_full = ff_end(ff_arrays, rows, units)
    context_mine = context_own[:tokens]
    context_theirs = swap_cores(context_own[tokens:])
    context = by_core(context_mine, context_theirs, 1)
    middle = states + (
        matmul(context_mine, out_mine, ((1,), (0,)))
        + matmul(context_theirs, out_theirs, ((1,), (0,)))
    )
    second_scale = rms_scale(middle)
    second_own = (middle * second_scale * gains_full[1]).astype(BF16)
    second_beside = permute(second_own, x_pairs())
    seconds = [second_own, swap_cores(second_own), second_beside, swap_cores(second_beside)]

    hidden, d_gate_up, gateup_grad, down_grad = feed_forward(
        seconds, d_finals, gateup_full, down_full, wide
    )
    beside = to_beside(
        back_through_gateup(d_gate_up, gateup_full, 2 * tokens, 2 * tokens, BF16)
    )
    gateup_grad, down_grad = when(gateup_grad, beside), when(down_grad, beside)
    ff_sends = ()
    if wide == BLOCK:
        pair_at, y = me // 8, (me // 2) % 2
        ff_sends = [
            ff_part(gateup_grad, down_grad, at, 1 - y) for at in (1 - pair_at, pair_at)
        ]
        arrived_far, arrived_near = (permute(send, Y_PAIR) for send in ff_sends)
    hidden = when(hidden, *ff_sends)
    result_parts = matmul(hidden, down_full, ((1,), (0,)))
    d_second_here = on_chip(
        back_through_gateup(d_gate_up, gateup_full, 0, 2 * tokens, F32, ff_sends)
    )
    d_second_here = when(d_second_here, result_parts)
    d_second = d_second_here + permute(beside, x_pairs()).astype(F32)
    result_beside = when(to_beside(result_parts[2 * tokens :]), d_second)
    result_arrived = permute(result_beside, x_pairs())
    output = middle + (on_chip(result_parts[: 2 * tokens]) + result_arrived.astype(F32))
    output = output.astype(BF16).reshape(inputs.shape)

    d_output = d_final_own.astype(F32)
    second_gain, d_norm_two = norm_back(middle, second_scale, gains_full[1], d_second)
    d_middle = d_output + d_norm_two
    d_attended = d_middle.astype(BF16)
    theirs = matmul(d_attended, out_theirs, ((1,), (1,)), BF16)
    mine = matmul(d_attended, out_mine, ((1,), (1,)), BF16)
    d_context_all = jnp.concatenate([mine, swap_cores(theirs)])
    out_part = lax.dynamic_slice_in_dim(d_attended, (1 - core) * own_cols, own_cols, axis=1)
    out_sent = matmul(context, out_part, ((0,), (0,)), BF16)
    out_part = lax.dynamic_slice_in_dim(d_attended, core * own_cols, own_cols, axis=1)
    out_kept = matmul(context, out_part, ((0,), (0,)), BF16)
    d_context_all = when(d_context_all, out_sent, out_kept)
    if wide == BLOCK:
        far = fold(ff_part(gateup_grad, down_grad, 1 - pair_at, y), arrived_far)
        d_context_all = after(d_context_all, far)
        ff_steps = line_begin(far)
    d_projected, taps_grad, mix_grad = attention_backward(
        projected,
        probs,
        d_context_all,
        base_rows_of(taps_own, seq_len, True),
        mix_own,
        seq_lengths,
        lags,
        reach,
    )
    if wide == BLOCK:
        d_projected = after(d_projected, result_arrived, *ff_steps)
    qkv_grad = matmul(normed, d_projected, ((0,), (0,)), BF16)
    out_grad = fold(out_kept, swap_cores(out_sent))
    sends, kept = scatter_begin(qkv_grad, out_grad)
    arrivals = scatter_first(sends, kept)
    d_normed_parts = matmul(when(d_projected, *sends), qkv_full, ((1,), (1,)))
    ff_steps_done = ()
    if wide == BLOCK:
        ff_steps = line_middle(far, *(after(step, *sends) for step in ff_steps))
        d_normed_parts = after(d_normed_parts, *ff_steps)
        near = fold(
            ff_part(gateup_grad, down_grad, pair_at, y), after(arrived_near, *sends)
        )
        ff_total = line_end(near, far, *ff_steps)
        ff_steps_done = (ff_total,)
    else:
        ff_total = ff_scatter_whole(gateup_grad, down_grad)
    ff_mine, ff_theirs = ff_last(ff_total)
    first_sums = scatter_plane(sends, kept, arrivals, ff_steps_done)
    d_normed = d_normed_parts[:tokens] + swap_cores(d_normed_parts[tokens:])
    first_gain, d_norm_one = norm_back(states, first_scale, gains_full[0], d_normed)
    input_grad = (d_middle + d_norm_one).astype(BF16).reshape(inputs.shape)

    def spread(values):
        held = jnp.zeros((cores,) + values.shape, F32)
        return lax.dynamic_update_index_in_dim(held, values, core, 0).reshape(-1)

    packed = jnp.concatenate([first_gain, second_gain, spread(taps_grad), spread(mix_grad)])
    packed = sum_small(packed)
    gains_grad = lax.dynamic_slice_in_dim(
        packed[: 2 * width].reshape(2, width), me * rows, rows, axis=1
    )
    taps_total = packed[2 * width : 2 * width + conv_taps.size].reshape(conv_taps.shape)
    mix_total = packed[2 * width + conv_taps.size :].reshape(head_mix.shape)

    tokens_all = tokens * cores * wide

    def rate_for(position):
        return RATES[position] / math.sqrt(tokens_all * (seq_len if PER_PAIR[position] else 1))

    def step(master, moment, average, gradient, position):
        return nesterov(master, moment, average, gradient.astype(F32), rate_for(position))

    ff_shares = [ff_mine, swap_cores(ff_mine), ff_theirs, swap_cores(ff_theirs)]
    gateup_tall = ff_mine.shape[0] - width // wide_block * units
    down_shares = jnp.stack([share[gateup_tall:] for share in ff_shares])
    down_total = down_shares[jnp.arange(4) ^ quarter].reshape(4, -1, units, wide_block)
    down_total = down_total.transpose(0, 2, 1, 3).reshape(down_weight.shape)
    gateup_done = gateup_step(
        gateup_weight,
        gateup_momentum,
        gateup_average,
        [share[:gateup_tall] for share in ff_shares],
        quarter,
        rate_for(5),
    )
    down_done = step(down_weight, down_momentum, down_average, down_total, 6)

    first_share = scatter_line(first_sums, gateup_done[0], down_done[0], packed)
    first_other = swap_cores(first_share)
    qkv_total = by_core(
        first_share[:, : 3 * own_cols].reshape(rows, 3, own_cols),
        first_other[:, : 3 * own_cols].reshape(rows, 3, own_cols),
        2,
    ).transpose(1, 0, 2)
    out_total = by_core(first_share[:, 3 * own_cols :], first_other[:, 3 * own_cols :], 1)
    return (
        output,
        input_grad,
        *step(gains, gains_momentum, gains_average, gains_grad, 0),
        *step(qkv_weight, qkv_momentum, qkv_average, qkv_total, 1),
        *step(out_weight, out_momentum, out_average, out_total, 2),
        *step(conv_taps, taps_momentum, taps_average, taps_total, 3),
        *step(head_mix, mix_momentum, mix_average, mix_total, 4),
        *gateup_done,
        *down_done,
    )


def solution(mesh):
    batch = P(None, ("narrow", "wide"), None, None)
    gain = P(None, "wide")
    qkv = P(None, "wide", None)
    row = P("wide", None)
    row3 = P("wide", None, None)
    params = (gain,) * 3 + (qkv,) * 3 + (row,) * 3 + (P(),) * 6 + (row3,) * 3 + (row,) * 3
    return jax.shard_map(
        on_device,
        mesh=mesh,
        in_specs=(batch, batch, P(None, ("narrow", "wide"))) + params,
        out_specs=(batch, batch) + params,
        check_vma=False,
    )
```

```python
import math

import jax
import jax.numpy as jnp
from jax import lax
from jax.experimental import pallas as pl
from jax.experimental.pallas import tpu as pltpu
from jax.sharding import PartitionSpec as P

H = 16
E = 96
G = 2


EPSILON = 1e-05
MOMENTUM = 0.9
AVERAGE = 0.7
RATES = (0.1, 0.019, 0.19, 0.2, 0.5, 0.031, 0.0097)
PER_PAIR = (False, False, False, True, True, False, False)
F32 = jnp.float32
BF16 = jnp.bfloat16
SCALE = 1.0 / math.sqrt(E)
FREE = pl.CostEstimate(flops=1, bytes_accessed=1, transcendentals=0)


def permute(values, pairs):
    return lax.ppermute(values, "wide", pairs)


def swap_cores(values):
    return lax.ppermute(values, "narrow", [(0, 1), (1, 0)])


BLOCK = 16


def z_pairs(moves):
    return [(a * 4 + q, b * 4 + q) for a, b in moves for q in range(4)]


Z_PAIR = z_pairs([(0, 1), (1, 0), (2, 3), (3, 2)])
Z_MID = z_pairs([(1, 2), (2, 1)])
Z_OUT = z_pairs([(1, 0), (2, 3)])
Z_IN = z_pairs([(0, 1), (3, 2)])
X_PAIR = [(i, i ^ 1) for i in range(BLOCK)]
Y_PAIR = [(i, i ^ 2) for i in range(BLOCK)]


def after(values, *needed):
    def nothing(*refs):
        del refs

    return pl.pallas_call(
        nothing,
        cost_estimate=FREE,
        out_shape=jax.ShapeDtypeStruct(values.shape, values.dtype),
        in_specs=[pl.BlockSpec(memory_space=pl.ANY)] * (1 + len(needed)),
        out_specs=pl.BlockSpec(memory_space=pl.ANY),
        input_output_aliases={0: 0},
    )(values, *needed)


def line_gather(piece):
    z = lax.axis_index("wide") // 4
    odd = (z % 2) == 1
    up = [permute(piece, z_pairs([(0, 1), (1, 2), (2, 3)]))]
    down = [permute(piece, z_pairs([(1, 0), (2, 1), (3, 2)]))]
    up.append(permute(up[0], z_pairs([(1, 2), (2, 3)])))
    down.append(permute(down[0], z_pairs([(1, 0), (2, 1)])))
    up.append(permute(up[1], z_pairs([(2, 3)])))
    down.append(permute(down[1], z_pairs([(1, 0)])))
    near = jnp.stack([jnp.where(odd, up[0], piece), jnp.where(odd, piece, down[0])])

    def by_place(*choices):
        return jnp.where(
            z < 2,
            jnp.where(z == 0, choices[0], choices[1]),
            jnp.where(z == 2, choices[2], choices[3]),
        )

    def far(*needed):
        up_last, down_last = after(up[2], *needed), after(down[2], *needed)
        return jnp.stack(
            [
                by_place(down[1], down[0], up[1], up_last),
                by_place(down_last, down[1], up[0], up[1]),
            ]
        )

    return near, far, up[1], down[1]


def line_and_plane(piece):
    z = lax.axis_index("wide") // 4
    odd = (z % 2) == 1

    def across(values, x_first):
        return (values, permute(values, X_PAIR), permute(values, Y_PAIR), x_first)

    own = across(piece, False)
    up = permute(piece, z_pairs([(0, 1), (1, 2), (2, 3)]))
    down = permute(piece, z_pairs([(1, 0), (2, 1), (3, 2)]))
    beside = across(jnp.where(odd, up, down), True)
    up_two = permute(after(up, *own[1:3]), z_pairs([(1, 2), (2, 3)]))
    down_two = permute(after(down, *own[1:3]), z_pairs([(1, 0), (2, 1)]))
    up_three = permute(after(up_two, *beside[1:3]), z_pairs([(2, 3)]))
    down_three = permute(after(down_two, *beside[1:3]), z_pairs([(1, 0)]))

    def by_place(*choices):
        return jnp.where(
            z < 2,
            jnp.where(z == 0, choices[0], choices[1]),
            jnp.where(z == 2, choices[2], choices[3]),
        )

    far0 = across(by_place(down_two, down, up_two, up_three), False)
    far1 = across(by_place(down_three, down_two, up, up_two), True)
    return [("own", own), ("beside", beside), ("far0", far0), ("far1", far1)]


def gather(piece, lines, widths, needed=()):
    count = lax.axis_size("wide")
    rows = piece.shape[0]
    starts = [sum(widths[:i]) for i in range(len(widths))]
    if count != BLOCK:
        full = lax.all_gather(piece, "wide", axis=0, tiled=True)
        return [full[:, low : low + width] for low, width in zip(starts, widths)]
    me = lax.axis_index("wide")
    index = jnp.stack([me // 4, me % 4]).astype(jnp.int32)
    arrays = []
    places = []
    for place, across in lines:
        kept, by_x, by_y, x_first = across
        both = permute(by_x, Y_PAIR) if x_first else permute(by_y, X_PAIR)
        for lane, array in enumerate((kept, by_x, by_y, both)):
            arrays.append(array)
            places.append((place, lane))

    def assemble(index_ref, *refs):
        out_refs, sems = refs[-1 - len(widths) : -1], refs[-1]
        z = index_ref[0]
        z_places = {"own": z, "beside": z ^ 1, "far0": 2 - (z // 2) * 2, "far1": 3 - (z // 2) * 2}
        copies = []
        for n, (place, lane) in enumerate(places):
            for out_ref, low, width in zip(out_refs, starts, widths):
                copies.append(
                    pltpu.make_async_copy(
                        refs[n].at[:, pl.ds(low, width)],
                        out_ref.at[z_places[place], index_ref[1] ^ lane],
                        sems.at[len(copies)],
                    )
                )
        for copy in copies:
            copy.start()
        for copy in copies:
            copy.wait()

    full = pl.pallas_call(
        assemble,
        cost_estimate=FREE,
        out_shape=[jax.ShapeDtypeStruct((4, 4, rows, width), piece.dtype) for width in widths],
        in_specs=[pl.BlockSpec(memory_space=pltpu.SMEM)]
        + [pl.BlockSpec(memory_space=pl.ANY)] * (len(arrays) + len(needed)),
        out_specs=[pl.BlockSpec(memory_space=pltpu.VMEM)] * len(widths),
        scratch_shapes=[pltpu.SemaphoreType.DMA((len(arrays) * len(widths),))],
        compiler_params=pltpu.CompilerParams(vmem_limit_bytes=48 << 20),
    )(index, *arrays, *needed)
    return [part.reshape(count * rows, -1) for part in full]


def fold(*terms):
    return sum(term.astype(F32) for term in terms).astype(BF16)


def trade(values, bit, pairs):
    keep = lax.dynamic_index_in_dim(values, bit, 0, keepdims=False)
    give = lax.dynamic_index_in_dim(values, 1 - bit, 0, keepdims=False)
    return fold(keep, permute(give, pairs))


def line_begin(far):
    z = lax.axis_index("wide") // 4
    farthest = jnp.where(z < 2, far[1], far[0])
    up = permute(farthest, z_pairs([(0, 1)]))
    down = permute(farthest, z_pairs([(3, 2)]))
    return up, down


def line_middle(far, up, down):
    z = lax.axis_index("wide") // 4
    up = permute(fold(jnp.where(z == 0, far[0], far[1]), up), z_pairs([(0, 1), (1, 2)]))
    down = permute(fold(jnp.where(z == 3, far[1], far[0]), down), z_pairs([(3, 2), (2, 1)]))
    return up, down


def line_end(near, far, up, down):
    z = lax.axis_index("wide") // 4
    up = permute(
        fold(jnp.where(z == 1, far[0], near[1]), up), z_pairs([(0, 1), (1, 2), (2, 3)])
    )
    down = permute(
        fold(jnp.where(z == 2, far[1], near[0]), down), z_pairs([(3, 2), (2, 1), (1, 0)])
    )
    return fold(jnp.where(z % 2 == 1, near[1], near[0]), up, down)


def scatter_begin(*partials):
    count = lax.axis_size("wide")
    if count != BLOCK:
        return (jnp.concatenate(partials, axis=1),), None
    me = lax.axis_index("wide")
    pair, y, x = me // 8, (me // 2) % 2, me % 2

    def block(half, y_at, x_at):
        found = []
        for partial in partials:
            rows, columns = partial.shape[0] // count, partial.shape[1]
            part = lax.dynamic_slice(
                partial.reshape(2, 2, 2, 2, rows, columns),
                (half, 0, y_at, x_at, 0, 0),
                (1, 2, 1, 1, rows, columns),
            )
            found.append(part.reshape(2, rows, columns))
        return jnp.concatenate(found, axis=2)

    out = (
        block(1 - pair, 1 - y, 1 - x),
        block(pair, 1 - y, 1 - x),
        block(1 - pair, 1 - y, x),
        block(pair, y, 1 - x),
    )
    return out, block


def scatter_first(out, block):
    if block is None:
        return ()
    return permute(out[0], Y_PAIR), permute(out[1], X_PAIR)


def scatter_plane(out, block, arrivals, needed):
    if block is None:
        return out
    me = lax.axis_index("wide")
    pair, y, x = me // 8, (me // 2) % 2, me % 2
    by_y, by_x = permute(out[2], Y_PAIR), after(permute(out[3], X_PAIR), *needed)
    far = fold(block(1 - pair, y, 1 - x), arrivals[0])
    near = fold(block(pair, 1 - y, x), arrivals[1])
    far = fold(block(1 - pair, y, x), by_y, permute(far, X_PAIR))
    near = fold(block(pair, y, x), by_x, permute(near, Y_PAIR))
    return near, far


def scatter_line(sums, *needed):
    if lax.axis_size("wide") != BLOCK:
        return lax.psum_scatter(sums[0], "wide", scatter_dimension=0, tiled=True)
    near, far = sums
    steps = line_middle(far, *line_begin(far))
    return line_end(after(near, *needed), far, *steps)


def pair_groups():
    count = lax.axis_size("wide")
    return [[i for i in range(count) if i % 2 == x] for x in range(2)]


def x_pairs():
    return [(i, i ^ 1) for i in range(lax.axis_size("wide"))]


def both_by(bit, mine, other):
    return jnp.where(bit == 0, jnp.stack([mine, other]), jnp.stack([other, mine]))


def ff_pair(mine, theirs):
    return both_by(lax.axis_index("wide") % 2, mine, permute(theirs, x_pairs()))


def ff_cross(lines):
    return permute(lines, Y_PAIR)


def ff_end(arrays, rows, units):
    count = lax.axis_size("wide")
    tall, columns = arrays[0].shape[-2:]
    cols = (rows * count) // columns
    blocks = (tall - cols * units) // rows
    gateup_shape = (blocks, count * rows, columns)
    down_shape = (count * units, cols * columns)
    if count != BLOCK:
        full = lax.all_gather(arrays[0], "wide", axis_index_groups=pair_groups())
        full = full.reshape(count, tall, columns)
        gateup = full[:, : blocks * rows].reshape(count, blocks, rows, columns)
        down = full[:, blocks * rows :].reshape(count, cols, units, columns)
        return (
            gateup.transpose(1, 0, 2, 3).reshape(gateup_shape),
            down.transpose(0, 2, 1, 3).reshape(down_shape),
        )
    me = lax.axis_index("wide")
    index = jnp.stack([me // 8, (me // 2) % 2]).astype(jnp.int32)

    def assemble(index_ref, *refs):
        gateup_ref, down_ref, sems = refs[len(arrays) :]
        copies = []

        def copy(source, target):
            copies.append(pltpu.make_async_copy(source, target, sems.at[len(copies)]))

        for n in range(len(arrays)):
            half, lane = n // 2, n % 2
            for z in range(2):
                for x in range(2):
                    z_at = 2 * (index_ref[0] ^ half) + z
                    at = z_at * 4 + (index_ref[1] ^ lane) * 2 + x
                    source = refs[n].at[z, x]
                    for j in range(blocks):
                        target = gateup_ref.at[j, pl.ds(pl.multiple_of(at * rows, 16), rows)]
                        copy(source.at[pl.ds(j * rows, rows)], target)
                    for i in range(cols):
                        target = down_ref.at[
                            pl.ds(pl.multiple_of(at * units, 16), units),
                            pl.ds(i * columns, columns),
                        ]
                        copy(source.at[pl.ds(blocks * rows + i * units, units)], target)
        for started in copies:
            started.start()
        for started in copies:
            started.wait()

    return pl.pallas_call(
        assemble,
        cost_estimate=FREE,
        out_shape=(
            jax.ShapeDtypeStruct(gateup_shape, BF16),
            jax.ShapeDtypeStruct(down_shape, BF16),
        ),
        in_specs=[pl.BlockSpec(memory_space=pltpu.SMEM)]
        + [pl.BlockSpec(memory_space=pl.ANY)] * len(arrays),
        out_specs=(pl.BlockSpec(memory_space=pltpu.VMEM),) * 2,
        scratch_shapes=[pltpu.SemaphoreType.DMA((len(arrays) * 4 * (blocks + cols),))],
        compiler_params=pltpu.CompilerParams(vmem_limit_bytes=48 << 20),
    )(index, *arrays)


def ff_part(gateup_grad, down_grad, half, y):
    parts = []
    for grad in (gateup_grad, down_grad):
        blocks = grad.reshape((2, 2, 2, 2) + grad.shape[1:])
        found = lax.dynamic_slice(
            blocks, (half, 0, y, 0, 0, 0), (1, 2, 1, 2) + grad.shape[1:]
        )
        parts.append(found.reshape((2, 2) + grad.shape[1:]))
    return jnp.concatenate(parts, axis=2)


def ff_scatter_whole(gateup_grad, down_grad):
    packed = jnp.concatenate([gateup_grad, down_grad], axis=1)
    return lax.psum_scatter(
        packed.reshape((packed.shape[0] // 2, 2) + packed.shape[1:]),
        "wide",
        scatter_dimension=0,
        axis_index_groups=pair_groups(),
    )


def ff_last(total):
    x = lax.axis_index("wide") % 2
    keep = lax.dynamic_index_in_dim(total, x, 0, keepdims=False)
    give = lax.dynamic_index_in_dim(total, 1 - x, 0, keepdims=False)
    return keep, permute(give, x_pairs())


def gather_small(values):
    if lax.axis_size("wide") != BLOCK:
        return lax.all_gather(values, "wide")
    me = lax.axis_index("wide")
    pair, y, x = me // 8, (me // 2) % 2, me % 2

    def both(mine, other, bit):
        return jnp.where(bit == 0, jnp.stack([mine, other]), jnp.stack([other, mine]))

    row = both(values, permute(values, X_PAIR), x)
    plane = both(row, permute(row, Y_PAIR), y)
    near, far = line_gather(plane)[:2]
    return both(near, far(), pair).reshape((BLOCK,) + values.shape)


def sum_small(values):
    values = values + swap_cores(values)
    if lax.axis_size("wide") != BLOCK:
        return lax.psum(values, "wide")
    corner = [(i, i ^ 3) for i in range(BLOCK)]
    values = (values + permute(values, X_PAIR)) + (
        permute(values, Y_PAIR) + permute(values, corner)
    )
    one, two, three = (
        permute(values, z_pairs([(z, (z + hop) % 4) for z in range(4)])) for hop in (1, 2, 3)
    )
    return (values + two) + (one + three)


def allowed_mask(length, size):
    rows = lax.broadcasted_iota(jnp.int32, (size, size), 0)
    cols = lax.broadcasted_iota(jnp.int32, (size, size), 1)
    return (cols <= rows) & (cols < length)


def near_diagonal(size, reach):
    rows = lax.broadcasted_iota(jnp.int32, (size, size), 0)
    cols = lax.broadcasted_iota(jnp.int32, (size, size), 1)
    return jnp.abs(rows - cols) <= reach


def dot_nn(a, b):
    return lax.dot_general(a, b, (((1,), (0,)), ((), ())), preferred_element_type=F32)


def dot_nt(a, b):
    return lax.dot_general(a, b, (((1,), (1,)), ((), ())), preferred_element_type=F32)


def dot_tn(a, b):
    return lax.dot_general(a, b, (((0,), (0,)), ((), ())), preferred_element_type=F32)


def split_low(values):
    top = values.astype(BF16)
    return top, (values - top.astype(F32)).astype(BF16)


def attention_forward(projected, base_rows, head_mix, seq_lengths, lags, reach):
    heads = head_mix.shape[0]
    groups = heads // G
    seqs = seq_lengths.shape[0]
    size = projected.shape[0] // seqs

    def kernel(
        len_ref, mix_ref, base_ref, proj_ref, ctx_ref, p_ref,
        top_taps, low_taps, pad_top, pad_low, left_top, left_low, split, joined,
    ):
        seq = pl.program_id(0)

        @pl.when(seq == 0)
        def _():
            band = near_diagonal(size, reach)

            def build(h, carry):
                for a in range(lags):
                    row = jnp.broadcast_to(base_ref[h, a : a + 1, :], (size, size))
                    rolled = pltpu.roll(row, 0, 1, stride=1, stride_axis=0)
                    top, low = split_low(jnp.where(band, rolled, 0.0))
                    top_taps[h, a * size : (a + 1) * size, :] = top
                    low_taps[h, a * size : (a + 1) * size, :] = low
                return carry

            lax.fori_loop(0, heads, build, 0)
            pad_top[:, 0:8, :] = jnp.zeros((G, 8, size), F32)
            pad_low[:, 0:8, :] = jnp.zeros((G, 8, size), F32)

        for n in range(3 * heads):
            split[n] = proj_ref[:, n * E : (n + 1) * E]
        allowed = allowed_mask(len_ref[seq], size)

        def group_step(group, carry):
            probs = []
            for c in range(G):
                h = G * group + c
                raw = dot_nt(split[h], split[heads + h])
                masked = jnp.where(allowed, raw * SCALE, 0.0)
                top = masked.astype(BF16).astype(F32)
                pad_top[c, 8 : 8 + size, :] = top
                pad_low[c, 8 : 8 + size, :] = masked - top
                for a in range(lags):
                    cols = slice(a * size, (a + 1) * size)
                    left_top[c, :, cols] = pad_top[c, 8 - a : 8 - a + size, :].astype(BF16)
                    left_low[c, :, cols] = pad_low[c, 8 - a : 8 - a + size, :].astype(BF16)
                logits = (
                    dot_nn(left_top[c], top_taps[h])
                    + dot_nn(left_low[c], top_taps[h])
                    + dot_nn(left_top[c], low_taps[h])
                )
                logits = jnp.where(allowed, logits, -jnp.inf)
                terms = jnp.exp(logits - jnp.max(logits, axis=-1, keepdims=True))
                prob = terms * (1.0 / jnp.sum(terms, axis=-1, keepdims=True))
                p_ref[h, 0] = prob
                probs.append(prob)
            for c in range(G):
                h = G * group + c
                mixed = sum(mix_ref[h, i] * probs[i] for i in range(G))
                joined[h] = dot_nn(mixed.astype(BF16), split[2 * heads + h]).astype(BF16)
            return carry

        lax.fori_loop(0, groups, group_step, 0, unroll=4)
        for h in range(heads):
            ctx_ref[:, h * E : (h + 1) * E] = joined[h]

    flops = 2 * heads * seqs * size * size * (3 * lags * size + 2 * E)
    return pl.pallas_call(
        kernel,
        cost_estimate=FREE,
        grid=(seqs,),
        out_shape=(
            jax.ShapeDtypeStruct((seqs * size, heads * E), BF16),
            jax.ShapeDtypeStruct((heads, seqs, size, size), F32),
        ),
        in_specs=[
            pl.BlockSpec(memory_space=pltpu.SMEM),
            pl.BlockSpec(memory_space=pltpu.SMEM),
            pl.BlockSpec((heads, 8, size), lambda s: (0, 0, 0)),
            pl.BlockSpec((size, 3 * heads * E), lambda s: (s, 0)),
        ],
        out_specs=(
            pl.BlockSpec((size, heads * E), lambda s: (s, 0)),
            pl.BlockSpec((heads, 1, size, size), lambda s: (0, s, 0, 0)),
        ),
        scratch_shapes=[
            pltpu.VMEM((heads, lags * size, size), BF16),
            pltpu.VMEM((heads, lags * size, size), BF16),
            pltpu.VMEM((G, size + 8, size), F32),
            pltpu.VMEM((G, size + 8, size), F32),
            pltpu.VMEM((G, size, lags * size), BF16),
            pltpu.VMEM((G, size, lags * size), BF16),
            pltpu.VMEM((3 * heads, size, E), BF16),
            pltpu.VMEM((heads, size, E), BF16),
        ],
        compiler_params=pltpu.CompilerParams(vmem_limit_bytes=48 << 20),
    )(seq_lengths, head_mix, base_rows, projected)


def attention_backward(projected, probs, d_context, base_rows, head_mix, seq_lengths, lags, reach):
    heads = head_mix.shape[0]
    groups = heads // G
    seqs = seq_lengths.shape[0]
    size = projected.shape[0] // seqs

    def kernel(
        len_ref, mix_ref, base_ref, proj_ref, p_ref, dc_ref, dproj_ref, tap_ref, dmix_ref,
        back_taps, pad, left, products, split, split_dc, joined,
    ):
        seq = pl.program_id(0)
        rows = lax.broadcasted_iota(jnp.int32, (size, size), 0)
        cols = lax.broadcasted_iota(jnp.int32, (size, size), 1)

        @pl.when(seq == 0)
        def _():
            band = near_diagonal(size, reach)

            def build(h, carry):
                for a in range(lags):
                    row = jnp.broadcast_to(base_ref[h, a : a + 1, :], (size, size))
                    rolled = pltpu.roll(row, 0, 1, stride=1, stride_axis=0)
                    back_taps[h, a * size : (a + 1) * size, :] = jnp.where(
                        band, rolled, 0.0
                    ).astype(BF16)
                products[h] = jnp.zeros((size, lags * size), F32)
                return carry

            lax.fori_loop(0, heads, build, 0)
            pad[:, size : size + 8, :] = jnp.zeros((G, 8, size), F32)
            dmix_ref[...] = jnp.zeros_like(dmix_ref)

        for n in range(3 * heads):
            split[n] = proj_ref[:, n * E : (n + 1) * E]
        for h in range(heads):
            split_dc[h] = dc_ref[:, h * E : (h + 1) * E]
        allowed = allowed_mask(len_ref[seq], size)
        reverse = (rows + cols == size - 1).astype(F32).astype(BF16)

        def group_step(group, carry):
            d_probs = [None] * G
            sums = []
            for c in range(G):
                h = G * group + c
                d_mixed = dot_nt(split_dc[h], split[2 * heads + h])
                mixed = sum(mix_ref[h, i] * p_ref[G * group + i, 0] for i in range(G))
                joined[2 * heads + h] = dot_tn(mixed.astype(BF16), split_dc[h]).astype(BF16)
                for i in range(G):
                    prob = p_ref[G * group + i, 0]
                    sums.append(jnp.sum(d_mixed * prob, axis=0, keepdims=True))
                    term = mix_ref[h, i] * d_mixed
                    d_probs[i] = term if d_probs[i] is None else d_probs[i] + term
            sums.append(jnp.zeros((8 - G * G, size), F32))
            dmix_ref[group] += jnp.concatenate(sums, axis=0)
            for c in range(G):
                h = G * group + c
                prob = p_ref[h, 0]
                weighted = prob * d_probs[c]
                pad[c, 0:size, :] = weighted - prob * jnp.sum(weighted, axis=-1, keepdims=True)
                for a in range(lags):
                    left[c, :, a * size : (a + 1) * size] = pad[c, a : a + size, :].astype(BF16)
                d_masked = dot_nn(left[c], back_taps[h])
                raw = dot_nt(split[h], split[heads + h])
                masked = jnp.where(allowed, raw * SCALE, 0.0).astype(BF16)
                turned = dot_nn(masked, reverse).astype(BF16)
                products[h] += dot_tn(turned, left[c])
                d_raw = jnp.where(allowed, d_masked * SCALE, 0.0).astype(BF16)
                joined[h] = dot_nn(d_raw, split[heads + h]).astype(BF16)
                joined[heads + h] = dot_tn(d_raw, split[h]).astype(BF16)
            return carry

        lax.fori_loop(0, groups, group_step, 0, unroll=4)
        for n in range(3 * heads):
            dproj_ref[:, n * E : (n + 1) * E] = joined[n]

        @pl.when(seq == seqs - 1)
        def _():
            band = jnp.abs(size - 1 - rows - cols) <= reach

            def collect(h, carry):
                for a in range(lags):
                    kept = jnp.where(band, products[h, :, a * size : (a + 1) * size], 0.0)
                    rolled = pltpu.roll(kept, 0, 1, stride=1, stride_axis=0)
                    tap_ref[h, a : a + 1, :] = jnp.sum(rolled, axis=0, keepdims=True)
                tap_ref[h, lags:8, :] = jnp.zeros((8 - lags, size), F32)
                return carry

            lax.fori_loop(0, heads, collect, 0)

    flops = 2 * heads * seqs * size * size * ((2 * lags + 1) * size + 5 * E)
    d_projected, taps_rows, mix_rows = pl.pallas_call(
        kernel,
        cost_estimate=FREE,
        grid=(seqs,),
        out_shape=(
            jax.ShapeDtypeStruct(projected.shape, BF16),
            jax.ShapeDtypeStruct((heads, 8, size), F32),
            jax.ShapeDtypeStruct((groups, 8, size), F32),
        ),
        in_specs=[
            pl.BlockSpec(memory_space=pltpu.SMEM),
            pl.BlockSpec(memory_space=pltpu.SMEM),
            pl.BlockSpec((heads, 8, size), lambda s: (0, 0, 0)),
            pl.BlockSpec((size, 3 * heads * E), lambda s: (s, 0)),
            pl.BlockSpec((heads, 1, size, size), lambda s: (0, s, 0, 0)),
            pl.BlockSpec((size, heads * E), lambda s: (s, 0)),
        ],
        out_specs=(
            pl.BlockSpec((size, 3 * heads * E), lambda s: (s, 0)),
            pl.BlockSpec((heads, 8, size), lambda s: (0, 0, 0)),
            pl.BlockSpec((groups, 8, size), lambda s: (0, 0, 0)),
        ),
        scratch_shapes=[
            pltpu.VMEM((heads, lags * size, size), BF16),
            pltpu.VMEM((G, size + 8, size), F32),
            pltpu.VMEM((G, size, lags * size), BF16),
            pltpu.VMEM((heads, size, lags * size), F32),
            pltpu.VMEM((3 * heads, size, E), BF16),
            pltpu.VMEM((heads, size, E), BF16),
            pltpu.VMEM((3 * heads, size, E), BF16),
        ],
        compiler_params=pltpu.CompilerParams(vmem_limit_bytes=52 << 20),
    )(seq_lengths, head_mix, base_rows, projected, probs, d_context)
    shifts = 2 * reach + 1
    at = [(size - 1 - reach + b) % size for b in range(shifts)]
    taps_grad = jnp.stack([taps_rows[:, :lags, i] for i in at], axis=-1)
    mix_grad = jnp.sum(mix_rows[:, : G * G], axis=-1).reshape(heads, G)
    return d_projected, taps_grad, mix_grad


def base_rows_of(taps, size, turned):
    heads, lags, shifts = taps.shape
    reach = shifts // 2
    rows = taps[:, :, ::-1] if turned else taps
    rows = jnp.concatenate(
        [rows[:, :, reach:], jnp.zeros((heads, lags, size - shifts), F32), rows[:, :, :reach]],
        axis=-1,
    )
    return jnp.pad(rows, ((0, 0), (0, 8 - lags), (0, 0)))


HIDDEN_BLOCK = 256


def feed_forward(seconds, d_finals, gateup, down, count):
    part, width = seconds[0].shape
    tokens = 4 * part
    blocks = gateup.shape[0]
    block = HIDDEN_BLOCK
    rows, units = width // count, down.shape[0] // count
    cols = width // (2 * block)
    packed = count == BLOCK

    def kernel(*refs):
        x_refs, d_refs, (gu_ref, down_ref) = refs[:4], refs[4:8], refs[8:10]
        hidden_ref, dgu_ref, grad_ref, down_grad_ref, turned = refs[10:]

        @pl.when(pl.program_id(0) == 0)
        def _():
            for m in range(0, tokens, 256):
                source = x_refs[m // part][m % part : m % part + 256, :]
                turned[:, m : m + 256] = source.T

        down_grad = None
        for n in range(4):
            at = slice(n * part, (n + 1) * part)
            gate_up = dot_nn(x_refs[n][...], gu_ref[0])
            gate, up = gate_up[:, :block], gate_up[:, block:]
            sig = jax.nn.sigmoid(gate)
            silu = gate * sig
            hidden = (silu * up).astype(BF16)
            hidden_ref[at, :] = hidden
            d_hidden = dot_nt(d_refs[n][...], down_ref[...])
            d_gate = d_hidden * up * sig * (1.0 + gate * (1.0 - sig))
            dgu_ref[at, :block] = d_gate.astype(BF16)
            dgu_ref[at, block:] = (d_hidden * silu).astype(BF16)
            term = dot_tn(hidden, d_refs[n][...])
            down_grad = term if down_grad is None else down_grad + term
        grad = dot_nn(turned[...], dgu_ref[...]).astype(BF16)
        down_grad = down_grad.astype(BF16)
        if packed:
            grad_ref[...] = grad.reshape(count, rows, 2 * block)
            for i in range(cols):
                columns = down_grad[:, i * 2 * block : (i + 1) * 2 * block]
                down_grad_ref[:, i * units : (i + 1) * units, :] = columns.reshape(
                    block // units, units, 2 * block
                )
        else:
            grad_ref[0] = grad
            down_grad_ref[...] = down_grad

    def whole(shape):
        return pl.BlockSpec(shape, lambda j: (0, 0), pipeline_mode=pl.Buffered(1))

    gateup_part = pl.BlockSpec((1, width, 2 * block), lambda j: (j, 0, 0))
    down_part = pl.BlockSpec((block, width), lambda j: (j, 0))
    if packed:
        grad_shapes = ((count, blocks * rows, 2 * block), (count, cols * units, 2 * block))
        grad_specs = (
            pl.BlockSpec((count, rows, 2 * block), lambda j: (0, j, 0)),
            pl.BlockSpec((block // units, cols * units, 2 * block), lambda j: (j, 0, 0)),
        )
    else:
        grad_shapes = (gateup.shape, down.shape)
        grad_specs = (gateup_part, down_part)
    hidden, d_gate_up, gateup_grad, down_grad = pl.pallas_call(
        kernel,
        cost_estimate=FREE,
        grid=(blocks,),
        out_shape=(
            jax.ShapeDtypeStruct((tokens, blocks * block), BF16),
            jax.ShapeDtypeStruct((tokens, 2 * blocks * block), BF16),
        )
        + tuple(jax.ShapeDtypeStruct(shape, BF16) for shape in grad_shapes),
        in_specs=[whole((part, width))] * 8 + [gateup_part, down_part],
        out_specs=(
            pl.BlockSpec((tokens, block), lambda j: (0, j)),
            pl.BlockSpec((tokens, 2 * block), lambda j: (0, j)),
        )
        + grad_specs,
        scratch_shapes=[pltpu.VMEM((width, tokens), BF16)],
        compiler_params=pltpu.CompilerParams(vmem_limit_bytes=56 << 20),
    )(*seconds, *d_finals, gateup, down)
    if not packed:
        gateup_grad = gateup_grad.reshape(blocks, count, rows, 2 * block)
        gateup_grad = gateup_grad.transpose(1, 0, 2, 3).reshape(count, -1, 2 * block)
        down_grad = down_grad.reshape(count, units, cols, 2 * block)
        down_grad = down_grad.transpose(0, 2, 1, 3).reshape(count, -1, 2 * block)
    return hidden, d_gate_up, gateup_grad, down_grad


def back_through_gateup(d_gate_up, gateup, first, count, kind, needed=()):
    blocks, width, columns = gateup.shape
    part = 256

    def kernel(d_ref, gu_ref, *refs):
        total = dot_nt(d_ref[:, :columns], gu_ref[0])
        for j in range(1, blocks):
            total = total + dot_nt(d_ref[:, j * columns : (j + 1) * columns], gu_ref[j])
        refs[-1][...] = total.astype(kind)

    return pl.pallas_call(
        kernel,
        cost_estimate=FREE,
        grid=(count // part,),
        out_shape=jax.ShapeDtypeStruct((count, width), kind),
        in_specs=[
            pl.BlockSpec((part, blocks * columns), lambda m: (first // part + m, 0)),
            pl.BlockSpec(gateup.shape, lambda m: (0, 0, 0), pipeline_mode=pl.Buffered(1)),
        ]
        + [pl.BlockSpec(memory_space=pl.ANY)] * len(needed),
        out_specs=pl.BlockSpec((part, width), lambda m: (m, 0)),
        compiler_params=pltpu.CompilerParams(vmem_limit_bytes=48 << 20),
    )(d_gate_up, gateup, *needed)


def quarter_columns(wide, hidden_all):
    units = hidden_all // (4 * wide)
    return units, HIDDEN_BLOCK // units


def gateup_cast(weight, quarter):
    rows, _, hidden_all = weight.shape
    wide = lax.axis_size("wide")
    units, each = quarter_columns(wide, hidden_all)
    block = HIDDEN_BLOCK
    blocks = hidden_all // (4 * block)
    if wide != BLOCK:
        split = weight.astype(BF16).reshape(rows, 2, blocks, each, 4, units)
        split = split.transpose(4, 2, 0, 1, 3, 5).reshape(4, blocks * rows, 2 * block)
        return split[quarter], split[quarter ^ 2]

    def kernel(quarter_ref, in_ref, mine_ref, theirs_ref):
        found = []
        for t in range(4):
            parts = []
            for k in range(2):
                for w in range(each):
                    low = (4 * w + t) * units
                    parts.append(in_ref[:, k, low : low + units])
            found.append(jnp.concatenate(parts, axis=1).astype(BF16).astype(F32))
        for ref, flip in ((mine_ref, 0), (theirs_ref, 2)):
            at = quarter_ref[0] ^ flip
            chosen = found[0]
            for t in range(1, 4):
                chosen = jnp.where(at == t, found[t], chosen)
            ref[...] = chosen.astype(BF16)

    part = pl.BlockSpec((rows, 2 * block), lambda j: (j, 0))
    return pl.pallas_call(
        kernel,
        cost_estimate=FREE,
        grid=(blocks,),
        out_shape=(jax.ShapeDtypeStruct((blocks * rows, 2 * block), BF16),) * 2,
        in_specs=[
            pl.BlockSpec(memory_space=pltpu.SMEM),
            pl.BlockSpec((rows, 2, 4 * block), lambda j: (0, 0, j)),
        ],
        out_specs=(part, part),
        compiler_params=pltpu.CompilerParams(vmem_limit_bytes=32 << 20),
    )(quarter.reshape(1).astype(jnp.int32), weight)


def gateup_step(master, moment, average, shares, quarter, rate):
    rows, _, hidden_all = master.shape
    wide = lax.axis_size("wide")
    units, each = quarter_columns(wide, hidden_all)
    block = HIDDEN_BLOCK
    blocks = hidden_all // (4 * block)
    if wide != BLOCK:
        split = jnp.stack(shares)[jnp.arange(4) ^ quarter]
        split = split.reshape(4, blocks, rows, 2, each, units).transpose(2, 3, 1, 4, 0, 5)
        return nesterov(
            master, moment, average, split.reshape(master.shape).astype(F32), rate
        )

    def kernel(quarter_ref, p_ref, m_ref, a_ref, *refs):
        ins, outs = refs[:4], refs[4:]
        given = [ref[...].astype(F32) for ref in ins]
        found = []
        for t in range(4):
            at = quarter_ref[0] ^ t
            chosen = given[0]
            for n in range(1, 4):
                chosen = jnp.where(at == n, given[n], chosen)
            found.append(chosen)
        for k in range(2):
            parts = []
            for w in range(each):
                low = k * block + w * units
                parts += [found[t][:, low : low + units] for t in range(4)]
            done = nesterov(
                p_ref[:, k, :], m_ref[:, k, :], a_ref[:, k, :], jnp.concatenate(parts, 1), rate
            )
            for ref, value in zip(outs, done):
                ref[:, k, :] = value

    whole = pl.BlockSpec((rows, 2, 4 * block), lambda j: (0, 0, j))
    part = pl.BlockSpec((rows, 2 * block), lambda j: (j, 0))
    return pl.pallas_call(
        kernel,
        cost_estimate=FREE,
        grid=(blocks,),
        out_shape=(jax.ShapeDtypeStruct(master.shape, F32),) * 3,
        in_specs=[pl.BlockSpec(memory_space=pltpu.SMEM)] + [whole] * 3 + [part] * 4,
        out_specs=(whole,) * 3,
        compiler_params=pltpu.CompilerParams(vmem_limit_bytes=32 << 20),
    )(quarter.reshape(1).astype(jnp.int32), master, moment, average, *shares)


def rms_scale(values):
    return lax.rsqrt(jnp.mean(values * values, axis=-1, keepdims=True) + EPSILON)


def norm_back(values, scale_rows, gain_row, upstream):
    normal_rows = values * scale_rows
    gain_grad = jnp.sum(upstream * normal_rows, axis=0)
    weighted = upstream * gain_row
    values_grad = scale_rows * (
        weighted - normal_rows * jnp.mean(weighted * normal_rows, axis=-1, keepdims=True)
    )
    return (gain_grad, values_grad)


def matmul(a, b, dims, out=F32):
    return lax.dot_general(a, b, (dims, ((), ())), preferred_element_type=F32).astype(out)


def nesterov(master, moment, average, gradient, step_rate):
    new_moment = MOMENTUM * moment + gradient
    new_master = master - step_rate * (gradient + MOMENTUM * new_moment)
    return (new_moment, new_master, AVERAGE * average + (1.0 - AVERAGE) * new_master)


def on_device(
    inputs,
    cotangent,
    lengths,
    gains,
    gains_momentum,
    gains_average,
    qkv_weight,
    qkv_momentum,
    qkv_average,
    out_weight,
    out_momentum,
    out_average,
    conv_taps,
    taps_momentum,
    taps_average,
    head_mix,
    mix_momentum,
    mix_average,
    gateup_weight,
    gateup_momentum,
    gateup_average,
    down_weight,
    down_momentum,
    down_average,
):
    micro_count, seq_count, seq_len, width = inputs.shape
    lags, shifts = conv_taps.shape[1:]
    reach = shifts // 2
    core = lax.axis_index("narrow")
    me = lax.axis_index("wide")
    wide = lax.axis_size("wide")
    cores = lax.axis_size("narrow")
    rows = width // wide
    own_heads = H // cores
    own_cols = own_heads * E
    hidden_all = gateup_weight.shape[2]
    units = hidden_all // (wide * 2 * cores)
    quarter = (me % 2) * cores + core
    tokens = micro_count * seq_count * seq_len

    def by_core(mine, other, axis):
        return jnp.where(
            core == 0,
            jnp.concatenate([mine, other], axis=axis),
            jnp.concatenate([other, mine], axis=axis),
        )

    def core_part(values, axis):
        return lax.dynamic_index_in_dim(values, core, axis, keepdims=False)

    def other_part(values, axis):
        return lax.dynamic_index_in_dim(values, 1 - core, axis, keepdims=False)

    def rows_of_core(values, axis):
        shape = values.shape
        split = values.reshape(
            shape[:axis] + (cores, shape[axis] // cores) + shape[axis + 1 :]
        )
        return core_part(split, axis), other_part(split, axis)

    def to_beside(partial):
        other = swap_cores(partial[tokens:].astype(BF16))
        return fold(partial[:tokens], other)

    def on_chip(partial):
        other = swap_cores(partial[tokens:].astype(BF16))
        return partial[:tokens].astype(F32) + other.astype(F32)

    def when(values, *needed):
        return after(values, *needed) if wide == BLOCK else values

    qkv_piece = rows_of_core(qkv_weight.astype(BF16).transpose(1, 0, 2), 2)[0]
    qkv_piece = qkv_piece.reshape(rows, 3 * own_cols)
    gains_piece = jnp.pad(gains.T.astype(BF16), ((0, 0), (0, 126)))
    out_piece = rows_of_core(out_weight.astype(BF16), 1)[0]
    first_piece = jnp.concatenate([qkv_piece, out_piece, gains_piece], axis=1)
    widths = (3 * own_cols, width // cores, 128)
    wide_block = 2 * HIDDEN_BLOCK
    gateup_mine, gateup_theirs = gateup_cast(gateup_weight, quarter)
    down_split = down_weight.astype(BF16).reshape(4, units, width // wide_block, wide_block)
    down_split = down_split.transpose(0, 2, 1, 3).reshape(4, -1, wide_block)

    def ff_piece(gateup_part, at):
        down_part = lax.dynamic_index_in_dim(down_split, at, 0, keepdims=False)
        return jnp.concatenate([gateup_part, down_part])

    inputs_own = inputs.reshape(tokens, width)
    inputs_other = swap_cores(inputs_own)
    lengths_own = lengths.reshape(-1)
    seq_lengths = jnp.concatenate([lengths_own, swap_cores(lengths_own)])
    pair = ff_pair(ff_piece(gateup_mine, quarter), ff_piece(gateup_theirs, quarter ^ 2))
    if wide == BLOCK:
        first_lines = line_and_plane(first_piece)
        ff_lines = line_gather(after(pair, first_lines[2][1][0], first_lines[3][1][0]))
        first_full = gather(first_piece, first_lines, widths, ff_lines[2:])
    else:
        first_full = gather(first_piece, None, widths)
    qkv_full, out_half, gains_full = first_full
    gains_full = gains_full[:, :2].T.astype(F32)
    out_full = by_core(out_half, swap_cores(out_half), 1)
    out_mine, out_theirs = rows_of_core(out_full, 0)

    states = inputs_own.astype(F32)
    first_scale = rms_scale(states)

    def first_norm(values):
        values = values.astype(F32)
        return (values * rms_scale(values) * gains_full[0]).astype(BF16)

    normed = jnp.concatenate([first_norm(inputs_own), first_norm(inputs_other)])
    d_final_own = cotangent.reshape(tokens, width)
    d_final_beside = permute(d_final_own, x_pairs())
    d_finals = [d_final_own, swap_cores(d_final_own), d_final_beside, swap_cores(d_final_beside)]
    all_tokens = cores * tokens

    taps_own = rows_of_core(conv_taps, 0)[0]
    mix_own = rows_of_core(head_mix, 0)[0]

    projected = matmul(normed, qkv_full, ((1,), (0,)), BF16)
    if wide == BLOCK:
        ff_near = after(ff_lines[0], qkv_full)
        ff_near_across = ff_cross(ff_near)
    context_own, probs = attention_forward(
        projected, base_rows_of(taps_own, seq_len, False), mix_own, seq_lengths, lags, reach
    )
    if wide == BLOCK:
        context_own = after(context_own, ff_near_across, d_final_beside)
        ff_far = ff_lines[1](context_own)
        ff_far_across = ff_cross(ff_far)
        ff_arrays = (ff_near, ff_near_across, ff_far, ff_far_across)
    else:
        ff_arrays = (pair,)
    gateup_full, down_full = ff_end(ff_arrays, rows, units)
    context_mine = context_own[:tokens]
    context_theirs = swap_cores(context_own[tokens:])
    middle = states + (
        matmul(context_mine, out_mine, ((1,), (0,)))
        + matmul(context_theirs, out_theirs, ((1,), (0,)))
    )
    second_scale = rms_scale(middle)
    second_own = (middle * second_scale * gains_full[1]).astype(BF16)
    second_beside = permute(second_own, x_pairs())
    context = by_core(context_mine, when(context_theirs, second_own), 1)
    if wide == BLOCK:
        second_beside = after(second_beside, ff_far_across)
    seconds = [second_own, swap_cores(second_own), second_beside, swap_cores(second_beside)]

    hidden, d_gate_up, gateup_grad, down_grad = feed_forward(
        seconds, d_finals, gateup_full, down_full, wide
    )
    beside = to_beside(
        back_through_gateup(d_gate_up, gateup_full, 2 * tokens, 2 * tokens, BF16)
    )
    gateup_grad, down_grad = when(gateup_grad, beside), when(down_grad, beside)
    ff_sends = ()
    if wide == BLOCK:
        pair_at, y = me // 8, (me // 2) % 2
        ff_sends = [
            ff_part(gateup_grad, down_grad, at, 1 - y) for at in (1 - pair_at, pair_at)
        ]
        arrived_far, arrived_near = (permute(send, Y_PAIR) for send in ff_sends)
    hidden = when(hidden, *ff_sends)
    result_parts = matmul(hidden, down_full, ((1,), (0,)))
    d_second_here = on_chip(
        back_through_gateup(d_gate_up, gateup_full, 0, 2 * tokens, F32, ff_sends)
    )
    d_second_here = when(d_second_here, result_parts)
    d_second = d_second_here + permute(beside, x_pairs()).astype(F32)
    result_beside = when(to_beside(result_parts[2 * tokens :]), d_second)
    result_arrived = permute(result_beside, x_pairs())
    output = middle + (on_chip(result_parts[: 2 * tokens]) + result_arrived.astype(F32))
    output = output.astype(BF16).reshape(inputs.shape)

    d_output = d_final_own.astype(F32)
    second_gain, d_norm_two = norm_back(middle, second_scale, gains_full[1], d_second)
    d_middle = d_output + d_norm_two
    d_attended = d_middle.astype(BF16)
    theirs = matmul(d_attended, out_theirs, ((1,), (1,)), BF16)
    mine = matmul(d_attended, out_mine, ((1,), (1,)), BF16)
    d_context_all = jnp.concatenate([mine, swap_cores(theirs)])
    out_part = lax.dynamic_slice_in_dim(d_attended, (1 - core) * own_cols, own_cols, axis=1)
    out_sent = matmul(context, out_part, ((0,), (0,)), BF16)
    out_part = lax.dynamic_slice_in_dim(d_attended, core * own_cols, own_cols, axis=1)
    out_kept = matmul(context, out_part, ((0,), (0,)), BF16)
    d_context_all = when(d_context_all, out_sent, out_kept)
    if wide == BLOCK:
        far = fold(ff_part(gateup_grad, down_grad, 1 - pair_at, y), arrived_far)
        d_context_all = after(d_context_all, far)
        ff_steps = line_begin(far)
    d_projected, taps_grad, mix_grad = attention_backward(
        projected,
        probs,
        d_context_all,
        base_rows_of(taps_own, seq_len, True),
        mix_own,
        seq_lengths,
        lags,
        reach,
    )
    if wide == BLOCK:
        d_projected = after(d_projected, result_arrived, *ff_steps)
    qkv_grad = matmul(normed, d_projected, ((0,), (0,)), BF16)
    out_grad = fold(out_kept, swap_cores(out_sent))
    sends, kept = scatter_begin(qkv_grad, out_grad)
    arrivals = scatter_first(sends, kept)
    d_normed_parts = matmul(when(d_projected, *sends), qkv_full, ((1,), (1,)))
    ff_steps_done = ()
    if wide == BLOCK:
        ff_steps = line_middle(far, *(after(step, *sends) for step in ff_steps))
        d_normed_parts = after(d_normed_parts, *ff_steps)
        near = fold(
            ff_part(gateup_grad, down_grad, pair_at, y), after(arrived_near, *sends)
        )
        ff_total = line_end(near, far, *ff_steps)
        ff_steps_done = (ff_total,)
    else:
        ff_total = ff_scatter_whole(gateup_grad, down_grad)
    ff_mine, ff_theirs = ff_last(ff_total)
    first_sums = scatter_plane(sends, kept, arrivals, ff_steps_done)
    d_normed = d_normed_parts[:tokens] + swap_cores(d_normed_parts[tokens:])
    first_gain, d_norm_one = norm_back(states, first_scale, gains_full[0], d_normed)
    input_grad = (d_middle + d_norm_one).astype(BF16).reshape(inputs.shape)

    def spread(values):
        held = jnp.zeros((cores,) + values.shape, F32)
        return lax.dynamic_update_index_in_dim(held, values, core, 0).reshape(-1)

    packed = jnp.concatenate([first_gain, second_gain, spread(taps_grad), spread(mix_grad)])
    packed = sum_small(packed)
    gains_grad = lax.dynamic_slice_in_dim(
        packed[: 2 * width].reshape(2, width), me * rows, rows, axis=1
    )
    taps_total = packed[2 * width : 2 * width + conv_taps.size].reshape(conv_taps.shape)
    mix_total = packed[2 * width + conv_taps.size :].reshape(head_mix.shape)

    tokens_all = tokens * cores * wide

    def rate_for(position):
        return RATES[position] / math.sqrt(tokens_all * (seq_len if PER_PAIR[position] else 1))

    def step(master, moment, average, gradient, position):
        return nesterov(master, moment, average, gradient.astype(F32), rate_for(position))

    ff_shares = [ff_mine, swap_cores(ff_mine), ff_theirs, swap_cores(ff_theirs)]
    gateup_tall = ff_mine.shape[0] - width // wide_block * units
    down_shares = jnp.stack([share[gateup_tall:] for share in ff_shares])
    down_total = down_shares[jnp.arange(4) ^ quarter].reshape(4, -1, units, wide_block)
    down_total = down_total.transpose(0, 2, 1, 3).reshape(down_weight.shape)
    gateup_done = gateup_step(
        gateup_weight,
        gateup_momentum,
        gateup_average,
        [share[:gateup_tall] for share in ff_shares],
        quarter,
        rate_for(5),
    )
    down_done = step(down_weight, down_momentum, down_average, down_total, 6)

    first_share = scatter_line(first_sums, gateup_done[0], down_done[0], packed)
    first_other = swap_cores(first_share)
    qkv_total = by_core(
        first_share[:, : 3 * own_cols].reshape(rows, 3, own_cols),
        first_other[:, : 3 * own_cols].reshape(rows, 3, own_cols),
        2,
    ).transpose(1, 0, 2)
    out_total = by_core(first_share[:, 3 * own_cols :], first_other[:, 3 * own_cols :], 1)
    return (
        output,
        input_grad,
        *step(gains, gains_momentum, gains_average, gains_grad, 0),
        *step(qkv_weight, qkv_momentum, qkv_average, qkv_total, 1),
        *step(out_weight, out_momentum, out_average, out_total, 2),
        *step(conv_taps, taps_momentum, taps_average, taps_total, 3),
        *step(head_mix, mix_momentum, mix_average, mix_total, 4),
        *gateup_done,
        *down_done,
    )


def solution(mesh):
    batch = P(None, ("narrow", "wide"), None, None)
    gain = P(None, "wide")
    qkv = P(None, "wide", None)
    row = P("wide", None)
    row3 = P("wide", None, None)
    params = (gain,) * 3 + (qkv,) * 3 + (row,) * 3 + (P(),) * 6 + (row3,) * 3 + (row,) * 3
    return jax.shard_map(
        on_device,
        mesh=mesh,
        in_specs=(batch, batch, P(None, ("narrow", "wide"))) + params,
        out_specs=(batch, batch) + params,
        check_vma=False,
    )
```

```python
import math

import jax
import jax.numpy as jnp
from jax import lax
from jax.experimental import pallas as pl
from jax.experimental.pallas import tpu as pltpu
from jax.sharding import PartitionSpec as P

H = 16
E = 96
G = 2


EPSILON = 1e-05
MOMENTUM = 0.9
AVERAGE = 0.7
RATES = (0.1, 0.019, 0.19, 0.2, 0.5, 0.031, 0.0097)
PER_PAIR = (False, False, False, True, True, False, False)
F32 = jnp.float32
BF16 = jnp.bfloat16
SCALE = 1.0 / math.sqrt(E)
FREE = pl.CostEstimate(flops=1, bytes_accessed=1, transcendentals=0)


def permute(values, pairs):
    return lax.ppermute(values, "wide", pairs)


def swap_cores(values):
    return lax.ppermute(values, "narrow", [(0, 1), (1, 0)])


BLOCK = 16


def z_pairs(moves):
    return [(a * 4 + q, b * 4 + q) for a, b in moves for q in range(4)]


Z_PAIR = z_pairs([(0, 1), (1, 0), (2, 3), (3, 2)])
Z_MID = z_pairs([(1, 2), (2, 1)])
Z_OUT = z_pairs([(1, 0), (2, 3)])
Z_IN = z_pairs([(0, 1), (3, 2)])
X_PAIR = [(i, i ^ 1) for i in range(BLOCK)]
Y_PAIR = [(i, i ^ 2) for i in range(BLOCK)]


def after(values, *needed):
    def nothing(*refs):
        del refs

    return pl.pallas_call(
        nothing,
        cost_estimate=FREE,
        out_shape=jax.ShapeDtypeStruct(values.shape, values.dtype),
        in_specs=[pl.BlockSpec(memory_space=pl.ANY)] * (1 + len(needed)),
        out_specs=pl.BlockSpec(memory_space=pl.ANY),
        input_output_aliases={0: 0},
    )(values, *needed)


def line_gather(piece):
    z = lax.axis_index("wide") // 4
    odd = (z % 2) == 1
    up = [permute(piece, z_pairs([(0, 1), (1, 2), (2, 3)]))]
    down = [permute(piece, z_pairs([(1, 0), (2, 1), (3, 2)]))]
    up.append(permute(up[0], z_pairs([(1, 2), (2, 3)])))
    down.append(permute(down[0], z_pairs([(1, 0), (2, 1)])))
    up.append(permute(up[1], z_pairs([(2, 3)])))
    down.append(permute(down[1], z_pairs([(1, 0)])))
    near = jnp.stack([jnp.where(odd, up[0], piece), jnp.where(odd, piece, down[0])])

    def by_place(*choices):
        return jnp.where(
            z < 2,
            jnp.where(z == 0, choices[0], choices[1]),
            jnp.where(z == 2, choices[2], choices[3]),
        )

    def far(*needed):
        up_last, down_last = after(up[2], *needed), after(down[2], *needed)
        return jnp.stack(
            [
                by_place(down[1], down[0], up[1], up_last),
                by_place(down_last, down[1], up[0], up[1]),
            ]
        )

    return near, far, up[1], down[1]


def line_and_plane(piece):
    z = lax.axis_index("wide") // 4
    odd = (z % 2) == 1

    def across(values, x_first):
        return (values, permute(values, X_PAIR), permute(values, Y_PAIR), x_first)

    own = across(piece, False)
    up = permute(piece, z_pairs([(0, 1), (1, 2), (2, 3)]))
    down = permute(piece, z_pairs([(1, 0), (2, 1), (3, 2)]))
    beside = across(jnp.where(odd, up, down), True)
    up_two = permute(after(up, *own[1:3]), z_pairs([(1, 2), (2, 3)]))
    down_two = permute(after(down, *own[1:3]), z_pairs([(1, 0), (2, 1)]))
    up_three = permute(after(up_two, *beside[1:3]), z_pairs([(2, 3)]))
    down_three = permute(after(down_two, *beside[1:3]), z_pairs([(1, 0)]))

    def by_place(*choices):
        return jnp.where(
            z < 2,
            jnp.where(z == 0, choices[0], choices[1]),
            jnp.where(z == 2, choices[2], choices[3]),
        )

    far0 = across(by_place(down_two, down, up_two, up_three), False)
    far1 = across(by_place(down_three, down_two, up, up_two), True)
    return [("own", own), ("beside", beside), ("far0", far0), ("far1", far1)]


def gather(piece, lines, widths, needed=()):
    count = lax.axis_size("wide")
    rows = piece.shape[0]
    starts = [sum(widths[:i]) for i in range(len(widths))]
    if count != BLOCK:
        full = lax.all_gather(piece, "wide", axis=0, tiled=True)
        return [full[:, low : low + width] for low, width in zip(starts, widths)]
    me = lax.axis_index("wide")
    index = jnp.stack([me // 4, me % 4]).astype(jnp.int32)
    arrays = []
    places = []
    for place, across in lines:
        kept, by_x, by_y, x_first = across
        both = permute(by_x, Y_PAIR) if x_first else permute(by_y, X_PAIR)
        for lane, array in enumerate((kept, by_x, by_y, both)):
            arrays.append(array)
            places.append((place, lane))

    def assemble(index_ref, *refs):
        out_refs, sems = refs[-1 - len(widths) : -1], refs[-1]
        z = index_ref[0]
        z_places = {"own": z, "beside": z ^ 1, "far0": 2 - (z // 2) * 2, "far1": 3 - (z // 2) * 2}
        copies = []
        for n, (place, lane) in enumerate(places):
            for out_ref, low, width in zip(out_refs, starts, widths):
                copies.append(
                    pltpu.make_async_copy(
                        refs[n].at[:, pl.ds(low, width)],
                        out_ref.at[z_places[place], index_ref[1] ^ lane],
                        sems.at[len(copies)],
                    )
                )
        for copy in copies:
            copy.start()
        for copy in copies:
            copy.wait()

    full = pl.pallas_call(
        assemble,
        cost_estimate=FREE,
        out_shape=[jax.ShapeDtypeStruct((4, 4, rows, width), piece.dtype) for width in widths],
        in_specs=[pl.BlockSpec(memory_space=pltpu.SMEM)]
        + [pl.BlockSpec(memory_space=pl.ANY)] * (len(arrays) + len(needed)),
        out_specs=[pl.BlockSpec(memory_space=pltpu.VMEM)] * len(widths),
        scratch_shapes=[pltpu.SemaphoreType.DMA((len(arrays) * len(widths),))],
        compiler_params=pltpu.CompilerParams(vmem_limit_bytes=48 << 20),
    )(index, *arrays, *needed)
    return [part.reshape(count * rows, -1) for part in full]


def fold(*terms):
    return sum(term.astype(F32) for term in terms).astype(BF16)


def trade(values, bit, pairs):
    keep = lax.dynamic_index_in_dim(values, bit, 0, keepdims=False)
    give = lax.dynamic_index_in_dim(values, 1 - bit, 0, keepdims=False)
    return fold(keep, permute(give, pairs))


def line_begin(far):
    z = lax.axis_index("wide") // 4
    farthest = jnp.where(z < 2, far[1], far[0])
    up = permute(farthest, z_pairs([(0, 1)]))
    down = permute(farthest, z_pairs([(3, 2)]))
    return up, down


def line_middle(far, up, down):
    z = lax.axis_index("wide") // 4
    up = permute(fold(jnp.where(z == 0, far[0], far[1]), up), z_pairs([(0, 1), (1, 2)]))
    down = permute(fold(jnp.where(z == 3, far[1], far[0]), down), z_pairs([(3, 2), (2, 1)]))
    return up, down


def line_end(near, far, up, down):
    z = lax.axis_index("wide") // 4
    up = permute(
        fold(jnp.where(z == 1, far[0], near[1]), up), z_pairs([(0, 1), (1, 2), (2, 3)])
    )
    down = permute(
        fold(jnp.where(z == 2, far[1], near[0]), down), z_pairs([(3, 2), (2, 1), (1, 0)])
    )
    return fold(jnp.where(z % 2 == 1, near[1], near[0]), up, down)


def scatter_begin(*partials):
    count = lax.axis_size("wide")
    if count != BLOCK:
        return (jnp.concatenate(partials, axis=1),), None
    me = lax.axis_index("wide")
    pair, y, x = me // 8, (me // 2) % 2, me % 2

    def block(half, y_at, x_at):
        found = []
        for partial in partials:
            rows, columns = partial.shape[0] // count, partial.shape[1]
            part = lax.dynamic_slice(
                partial.reshape(2, 2, 2, 2, rows, columns),
                (half, 0, y_at, x_at, 0, 0),
                (1, 2, 1, 1, rows, columns),
            )
            found.append(part.reshape(2, rows, columns))
        return jnp.concatenate(found, axis=2)

    out = (
        block(1 - pair, 1 - y, 1 - x),
        block(pair, 1 - y, 1 - x),
        block(1 - pair, 1 - y, x),
        block(pair, y, 1 - x),
    )
    return out, block


def scatter_first(out, block):
    if block is None:
        return ()
    return permute(out[0], Y_PAIR), permute(out[1], X_PAIR)


def scatter_plane(out, block, arrivals, needed):
    if block is None:
        return out
    me = lax.axis_index("wide")
    pair, y, x = me // 8, (me // 2) % 2, me % 2
    by_y, by_x = permute(out[2], Y_PAIR), after(permute(out[3], X_PAIR), *needed)
    far = fold(block(1 - pair, y, 1 - x), arrivals[0])
    near = fold(block(pair, 1 - y, x), arrivals[1])
    far = fold(block(1 - pair, y, x), by_y, permute(far, X_PAIR))
    near = fold(block(pair, y, x), by_x, permute(near, Y_PAIR))
    return near, far


def scatter_line(sums, *needed):
    if lax.axis_size("wide") != BLOCK:
        return lax.psum_scatter(sums[0], "wide", scatter_dimension=0, tiled=True)
    near, far = sums
    steps = line_middle(far, *line_begin(far))
    return line_end(after(near, *needed), far, *steps)


def pair_groups():
    count = lax.axis_size("wide")
    return [[i for i in range(count) if i % 2 == x] for x in range(2)]


def x_pairs():
    return [(i, i ^ 1) for i in range(lax.axis_size("wide"))]


def both_by(bit, mine, other):
    return jnp.where(bit == 0, jnp.stack([mine, other]), jnp.stack([other, mine]))


def ff_pair(mine, theirs):
    return both_by(lax.axis_index("wide") % 2, mine, permute(theirs, x_pairs()))


def ff_cross(lines):
    return permute(lines, Y_PAIR)


def ff_end(arrays, rows, units):
    count = lax.axis_size("wide")
    tall, columns = arrays[0].shape[-2:]
    cols = (rows * count) // columns
    blocks = (tall - cols * units) // rows
    gateup_shape = (blocks, count * rows, columns)
    down_shape = (count * units, cols * columns)
    if count != BLOCK:
        full = lax.all_gather(arrays[0], "wide", axis_index_groups=pair_groups())
        full = full.reshape(count, tall, columns)
        gateup = full[:, : blocks * rows].reshape(count, blocks, rows, columns)
        down = full[:, blocks * rows :].reshape(count, cols, units, columns)
        return (
            gateup.transpose(1, 0, 2, 3).reshape(gateup_shape),
            down.transpose(0, 2, 1, 3).reshape(down_shape),
        )
    me = lax.axis_index("wide")
    index = jnp.stack([me // 8, (me // 2) % 2]).astype(jnp.int32)

    def assemble(index_ref, *refs):
        gateup_out, down_out, gateup_ref, down_ref, sems, out_sems = refs[len(arrays) :]
        groups = [[] for _ in range(blocks + 1)]

        def copy(group, source, target):
            number = sum(len(known) for known in groups)
            groups[group].append(pltpu.make_async_copy(source, target, sems.at[number]))

        for n in range(len(arrays)):
            half, lane = n // 2, n % 2
            for z in range(2):
                for x in range(2):
                    z_at = 2 * (index_ref[0] ^ half) + z
                    at = z_at * 4 + (index_ref[1] ^ lane) * 2 + x
                    source = refs[n].at[z, x]
                    for j in range(blocks):
                        target = gateup_ref.at[j, pl.ds(pl.multiple_of(at * rows, 16), rows)]
                        copy(j, source.at[pl.ds(j * rows, rows)], target)
                    for i in range(cols):
                        target = down_ref.at[
                            pl.ds(pl.multiple_of(at * units, 16), units),
                            pl.ds(i * columns, columns),
                        ]
                        copy(blocks, source.at[pl.ds(blocks * rows + i * units, units)], target)
        for group in groups:
            for started in group:
                started.start()
        outs = [
            pltpu.make_async_copy(gateup_ref.at[j], gateup_out.at[j], out_sems.at[j])
            for j in range(blocks)
        ]
        outs.append(pltpu.make_async_copy(down_ref, down_out, out_sems.at[blocks]))
        for group, out in zip(groups, outs):
            for started in group:
                started.wait()
            out.start()
        for out in outs:
            out.wait()

    return pl.pallas_call(
        assemble,
        cost_estimate=FREE,
        out_shape=(
            jax.ShapeDtypeStruct(gateup_shape, BF16),
            jax.ShapeDtypeStruct(down_shape, BF16),
        ),
        in_specs=[pl.BlockSpec(memory_space=pltpu.SMEM)]
        + [pl.BlockSpec(memory_space=pl.ANY)] * len(arrays),
        out_specs=(pl.BlockSpec(memory_space=pl.ANY),) * 2,
        scratch_shapes=[
            pltpu.VMEM(gateup_shape, BF16),
            pltpu.VMEM(down_shape, BF16),
            pltpu.SemaphoreType.DMA((len(arrays) * 4 * (blocks + cols),)),
            pltpu.SemaphoreType.DMA((blocks + 1,)),
        ],
        compiler_params=pltpu.CompilerParams(vmem_limit_bytes=48 << 20),
    )(index, *arrays)


def ff_part(gateup_grad, down_grad, half, y):
    parts = []
    for grad in (gateup_grad, down_grad):
        blocks = grad.reshape((2, 2, 2, 2) + grad.shape[1:])
        found = lax.dynamic_slice(
            blocks, (half, 0, y, 0, 0, 0), (1, 2, 1, 2) + grad.shape[1:]
        )
        parts.append(found.reshape((2, 2) + grad.shape[1:]))
    return jnp.concatenate(parts, axis=2)


def ff_scatter_whole(gateup_grad, down_grad):
    packed = jnp.concatenate([gateup_grad, down_grad], axis=1)
    return lax.psum_scatter(
        packed.reshape((packed.shape[0] // 2, 2) + packed.shape[1:]),
        "wide",
        scatter_dimension=0,
        axis_index_groups=pair_groups(),
    )


def ff_last(total):
    x = lax.axis_index("wide") % 2
    keep = lax.dynamic_index_in_dim(total, x, 0, keepdims=False)
    give = lax.dynamic_index_in_dim(total, 1 - x, 0, keepdims=False)
    return keep, permute(give, x_pairs())


def gather_small(values):
    if lax.axis_size("wide") != BLOCK:
        return lax.all_gather(values, "wide")
    me = lax.axis_index("wide")
    pair, y, x = me // 8, (me // 2) % 2, me % 2

    def both(mine, other, bit):
        return jnp.where(bit == 0, jnp.stack([mine, other]), jnp.stack([other, mine]))

    row = both(values, permute(values, X_PAIR), x)
    plane = both(row, permute(row, Y_PAIR), y)
    near, far = line_gather(plane)[:2]
    return both(near, far(), pair).reshape((BLOCK,) + values.shape)


def sum_small(values):
    values = values + swap_cores(values)
    if lax.axis_size("wide") != BLOCK:
        return lax.psum(values, "wide")
    corner = [(i, i ^ 3) for i in range(BLOCK)]
    values = (values + permute(values, X_PAIR)) + (
        permute(values, Y_PAIR) + permute(values, corner)
    )
    one, two, three = (
        permute(values, z_pairs([(z, (z + hop) % 4) for z in range(4)])) for hop in (1, 2, 3)
    )
    return (values + two) + (one + three)


def allowed_mask(length, size):
    rows = lax.broadcasted_iota(jnp.int32, (size, size), 0)
    cols = lax.broadcasted_iota(jnp.int32, (size, size), 1)
    return (cols <= rows) & (cols < length)


def near_diagonal(size, reach):
    rows = lax.broadcasted_iota(jnp.int32, (size, size), 0)
    cols = lax.broadcasted_iota(jnp.int32, (size, size), 1)
    return jnp.abs(rows - cols) <= reach


def dot_nn(a, b):
    return lax.dot_general(a, b, (((1,), (0,)), ((), ())), preferred_element_type=F32)


def dot_nt(a, b):
    return lax.dot_general(a, b, (((1,), (1,)), ((), ())), preferred_element_type=F32)


def dot_tn(a, b):
    return lax.dot_general(a, b, (((0,), (0,)), ((), ())), preferred_element_type=F32)


def split_low(values):
    top = values.astype(BF16)
    return top, (values - top.astype(F32)).astype(BF16)


def attention_forward(projected, base_rows, head_mix, seq_lengths, lags, reach):
    heads = head_mix.shape[0]
    groups = heads // G
    seqs = seq_lengths.shape[0]
    size = projected.shape[0] // seqs

    def kernel(
        len_ref, mix_ref, base_ref, proj_ref, ctx_ref, p_ref,
        top_taps, low_taps, pad_top, pad_low, left_top, left_low, split, joined,
    ):
        seq = pl.program_id(0)

        @pl.when(seq == 0)
        def _():
            band = near_diagonal(size, reach)

            def build(h, carry):
                for a in range(lags):
                    row = jnp.broadcast_to(base_ref[h, a : a + 1, :], (size, size))
                    rolled = pltpu.roll(row, 0, 1, stride=1, stride_axis=0)
                    top, low = split_low(jnp.where(band, rolled, 0.0))
                    top_taps[h, a * size : (a + 1) * size, :] = top
                    low_taps[h, a * size : (a + 1) * size, :] = low
                return carry

            lax.fori_loop(0, heads, build, 0)
            pad_top[:, 0:8, :] = jnp.zeros((G, 8, size), F32)
            pad_low[:, 0:8, :] = jnp.zeros((G, 8, size), F32)

        for n in range(3 * heads):
            split[n] = proj_ref[:, n * E : (n + 1) * E]
        allowed = allowed_mask(len_ref[seq], size)

        def group_step(group, carry):
            probs = []
            for c in range(G):
                h = G * group + c
                raw = dot_nt(split[h], split[heads + h])
                masked = jnp.where(allowed, raw * SCALE, 0.0)
                top = masked.astype(BF16).astype(F32)
                pad_top[c, 8 : 8 + size, :] = top
                pad_low[c, 8 : 8 + size, :] = masked - top
                for a in range(lags):
                    cols = slice(a * size, (a + 1) * size)
                    left_top[c, :, cols] = pad_top[c, 8 - a : 8 - a + size, :].astype(BF16)
                    left_low[c, :, cols] = pad_low[c, 8 - a : 8 - a + size, :].astype(BF16)
                logits = (
                    dot_nn(left_top[c], top_taps[h])
                    + dot_nn(left_low[c], top_taps[h])
                    + dot_nn(left_top[c], low_taps[h])
                )
                logits = jnp.where(allowed, logits, -jnp.inf)
                terms = jnp.exp(logits - jnp.max(logits, axis=-1, keepdims=True))
                prob = terms * (1.0 / jnp.sum(terms, axis=-1, keepdims=True))
                p_ref[h, 0] = prob
                probs.append(prob)
            for c in range(G):
                h = G * group + c
                mixed = sum(mix_ref[h, i] * probs[i] for i in range(G))
                joined[h] = dot_nn(mixed.astype(BF16), split[2 * heads + h]).astype(BF16)
            return carry

        lax.fori_loop(0, groups, group_step, 0, unroll=4)
        for h in range(heads):
            ctx_ref[:, h * E : (h + 1) * E] = joined[h]

    flops = 2 * heads * seqs * size * size * (3 * lags * size + 2 * E)
    return pl.pallas_call(
        kernel,
        cost_estimate=FREE,
        grid=(seqs,),
        out_shape=(
            jax.ShapeDtypeStruct((seqs * size, heads * E), BF16),
            jax.ShapeDtypeStruct((heads, seqs, size, size), F32),
        ),
        in_specs=[
            pl.BlockSpec(memory_space=pltpu.SMEM),
            pl.BlockSpec(memory_space=pltpu.SMEM),
            pl.BlockSpec((heads, 8, size), lambda s: (0, 0, 0)),
            pl.BlockSpec((size, 3 * heads * E), lambda s: (s, 0)),
        ],
        out_specs=(
            pl.BlockSpec((size, heads * E), lambda s: (s, 0)),
            pl.BlockSpec((heads, 1, size, size), lambda s: (0, s, 0, 0)),
        ),
        scratch_shapes=[
            pltpu.VMEM((heads, lags * size, size), BF16),
            pltpu.VMEM((heads, lags * size, size), BF16),
            pltpu.VMEM((G, size + 8, size), F32),
            pltpu.VMEM((G, size + 8, size), F32),
            pltpu.VMEM((G, size, lags * size), BF16),
            pltpu.VMEM((G, size, lags * size), BF16),
            pltpu.VMEM((3 * heads, size, E), BF16),
            pltpu.VMEM((heads, size, E), BF16),
        ],
        compiler_params=pltpu.CompilerParams(vmem_limit_bytes=48 << 20),
    )(seq_lengths, head_mix, base_rows, projected)


def attention_backward(projected, probs, d_context, base_rows, head_mix, seq_lengths, lags, reach):
    heads = head_mix.shape[0]
    groups = heads // G
    seqs = seq_lengths.shape[0]
    size = projected.shape[0] // seqs

    def kernel(
        len_ref, mix_ref, base_ref, proj_ref, p_ref, dc_ref, dproj_ref, tap_ref, dmix_ref,
        back_taps, pad, left, products, split, split_dc, joined,
    ):
        seq = pl.program_id(0)
        rows = lax.broadcasted_iota(jnp.int32, (size, size), 0)
        cols = lax.broadcasted_iota(jnp.int32, (size, size), 1)

        @pl.when(seq == 0)
        def _():
            band = near_diagonal(size, reach)

            def build(h, carry):
                for a in range(lags):
                    row = jnp.broadcast_to(base_ref[h, a : a + 1, :], (size, size))
                    rolled = pltpu.roll(row, 0, 1, stride=1, stride_axis=0)
                    back_taps[h, a * size : (a + 1) * size, :] = jnp.where(
                        band, rolled, 0.0
                    ).astype(BF16)
                products[h] = jnp.zeros((size, lags * size), F32)
                return carry

            lax.fori_loop(0, heads, build, 0)
            pad[:, size : size + 8, :] = jnp.zeros((G, 8, size), F32)
            dmix_ref[...] = jnp.zeros_like(dmix_ref)

        for n in range(3 * heads):
            split[n] = proj_ref[:, n * E : (n + 1) * E]
        for h in range(heads):
            split_dc[h] = dc_ref[:, h * E : (h + 1) * E]
        allowed = allowed_mask(len_ref[seq], size)
        reverse = (rows + cols == size - 1).astype(F32).astype(BF16)

        def group_step(group, carry):
            d_probs = [None] * G
            sums = []
            for c in range(G):
                h = G * group + c
                d_mixed = dot_nt(split_dc[h], split[2 * heads + h])
                mixed = sum(mix_ref[h, i] * p_ref[G * group + i, 0] for i in range(G))
                joined[2 * heads + h] = dot_tn(mixed.astype(BF16), split_dc[h]).astype(BF16)
                for i in range(G):
                    prob = p_ref[G * group + i, 0]
                    sums.append(jnp.sum(d_mixed * prob, axis=0, keepdims=True))
                    term = mix_ref[h, i] * d_mixed
                    d_probs[i] = term if d_probs[i] is None else d_probs[i] + term
            sums.append(jnp.zeros((8 - G * G, size), F32))
            dmix_ref[group] += jnp.concatenate(sums, axis=0)
            for c in range(G):
                h = G * group + c
                prob = p_ref[h, 0]
                weighted = prob * d_probs[c]
                pad[c, 0:size, :] = weighted - prob * jnp.sum(weighted, axis=-1, keepdims=True)
                for a in range(lags):
                    left[c, :, a * size : (a + 1) * size] = pad[c, a : a + size, :].astype(BF16)
                d_masked = dot_nn(left[c], back_taps[h])
                raw = dot_nt(split[h], split[heads + h])
                masked = jnp.where(allowed, raw * SCALE, 0.0).astype(BF16)
                turned = dot_nn(masked, reverse).astype(BF16)
                products[h] += dot_tn(turned, left[c])
                d_raw = jnp.where(allowed, d_masked * SCALE, 0.0).astype(BF16)
                joined[h] = dot_nn(d_raw, split[heads + h]).astype(BF16)
                joined[heads + h] = dot_tn(d_raw, split[h]).astype(BF16)
            return carry

        lax.fori_loop(0, groups, group_step, 0, unroll=4)
        for n in range(3 * heads):
            dproj_ref[:, n * E : (n + 1) * E] = joined[n]

        @pl.when(seq == seqs - 1)
        def _():
            band = jnp.abs(size - 1 - rows - cols) <= reach

            def collect(h, carry):
                for a in range(lags):
                    kept = jnp.where(band, products[h, :, a * size : (a + 1) * size], 0.0)
                    rolled = pltpu.roll(kept, 0, 1, stride=1, stride_axis=0)
                    tap_ref[h, a : a + 1, :] = jnp.sum(rolled, axis=0, keepdims=True)
                tap_ref[h, lags:8, :] = jnp.zeros((8 - lags, size), F32)
                return carry

            lax.fori_loop(0, heads, collect, 0)

    flops = 2 * heads * seqs * size * size * ((2 * lags + 1) * size + 5 * E)
    d_projected, taps_rows, mix_rows = pl.pallas_call(
        kernel,
        cost_estimate=FREE,
        grid=(seqs,),
        out_shape=(
            jax.ShapeDtypeStruct(projected.shape, BF16),
            jax.ShapeDtypeStruct((heads, 8, size), F32),
            jax.ShapeDtypeStruct((groups, 8, size), F32),
        ),
        in_specs=[
            pl.BlockSpec(memory_space=pltpu.SMEM),
            pl.BlockSpec(memory_space=pltpu.SMEM),
            pl.BlockSpec((heads, 8, size), lambda s: (0, 0, 0)),
            pl.BlockSpec((size, 3 * heads * E), lambda s: (s, 0)),
            pl.BlockSpec((heads, 1, size, size), lambda s: (0, s, 0, 0)),
            pl.BlockSpec((size, heads * E), lambda s: (s, 0)),
        ],
        out_specs=(
            pl.BlockSpec((size, 3 * heads * E), lambda s: (s, 0)),
            pl.BlockSpec((heads, 8, size), lambda s: (0, 0, 0)),
            pl.BlockSpec((groups, 8, size), lambda s: (0, 0, 0)),
        ),
        scratch_shapes=[
            pltpu.VMEM((heads, lags * size, size), BF16),
            pltpu.VMEM((G, size + 8, size), F32),
            pltpu.VMEM((G, size, lags * size), BF16),
            pltpu.VMEM((heads, size, lags * size), F32),
            pltpu.VMEM((3 * heads, size, E), BF16),
            pltpu.VMEM((heads, size, E), BF16),
            pltpu.VMEM((3 * heads, size, E), BF16),
        ],
        compiler_params=pltpu.CompilerParams(vmem_limit_bytes=52 << 20),
    )(seq_lengths, head_mix, base_rows, projected, probs, d_context)
    shifts = 2 * reach + 1
    at = [(size - 1 - reach + b) % size for b in range(shifts)]
    taps_grad = jnp.stack([taps_rows[:, :lags, i] for i in at], axis=-1)
    mix_grad = jnp.sum(mix_rows[:, : G * G], axis=-1).reshape(heads, G)
    return d_projected, taps_grad, mix_grad


def base_rows_of(taps, size, turned):
    heads, lags, shifts = taps.shape
    reach = shifts // 2
    rows = taps[:, :, ::-1] if turned else taps
    rows = jnp.concatenate(
        [rows[:, :, reach:], jnp.zeros((heads, lags, size - shifts), F32), rows[:, :, :reach]],
        axis=-1,
    )
    return jnp.pad(rows, ((0, 0), (0, 8 - lags), (0, 0)))


HIDDEN_BLOCK = 256


def feed_forward(seconds, d_finals, gateup, down, count):
    part, width = seconds[0].shape
    tokens = 4 * part
    blocks = gateup.shape[0]
    block = HIDDEN_BLOCK
    rows, units = width // count, down.shape[0] // count
    cols = width // (2 * block)
    packed = count == BLOCK

    def kernel(*refs):
        x_refs, d_refs, (gu_ref, down_ref) = refs[:4], refs[4:8], refs[8:10]
        hidden_ref, dgu_ref, grad_ref, down_grad_ref, turned = refs[10:]

        @pl.when(pl.program_id(0) == 0)
        def _():
            for m in range(0, tokens, 256):
                source = x_refs[m // part][m % part : m % part + 256, :]
                turned[:, m : m + 256] = source.T

        down_grad = None
        for n in range(4):
            at = slice(n * part, (n + 1) * part)
            gate_up = dot_nn(x_refs[n][...], gu_ref[0])
            gate, up = gate_up[:, :block], gate_up[:, block:]
            sig = jax.nn.sigmoid(gate)
            silu = gate * sig
            hidden = (silu * up).astype(BF16)
            hidden_ref[at, :] = hidden
            d_hidden = dot_nt(d_refs[n][...], down_ref[...])
            d_gate = d_hidden * up * sig * (1.0 + gate * (1.0 - sig))
            dgu_ref[at, :block] = d_gate.astype(BF16)
            dgu_ref[at, block:] = (d_hidden * silu).astype(BF16)
            term = dot_tn(hidden, d_refs[n][...])
            down_grad = term if down_grad is None else down_grad + term
        grad = dot_nn(turned[...], dgu_ref[...]).astype(BF16)
        down_grad = down_grad.astype(BF16)
        if packed:
            grad_ref[...] = grad.reshape(count, rows, 2 * block)
            for i in range(cols):
                columns = down_grad[:, i * 2 * block : (i + 1) * 2 * block]
                down_grad_ref[:, i * units : (i + 1) * units, :] = columns.reshape(
                    block // units, units, 2 * block
                )
        else:
            grad_ref[0] = grad
            down_grad_ref[...] = down_grad

    def whole(shape):
        return pl.BlockSpec(shape, lambda j: (0, 0), pipeline_mode=pl.Buffered(1))

    gateup_part = pl.BlockSpec((1, width, 2 * block), lambda j: (j, 0, 0))
    down_part = pl.BlockSpec((block, width), lambda j: (j, 0))
    if packed:
        grad_shapes = ((count, blocks * rows, 2 * block), (count, cols * units, 2 * block))
        grad_specs = (
            pl.BlockSpec((count, rows, 2 * block), lambda j: (0, j, 0)),
            pl.BlockSpec((block // units, cols * units, 2 * block), lambda j: (j, 0, 0)),
        )
    else:
        grad_shapes = (gateup.shape, down.shape)
        grad_specs = (gateup_part, down_part)
    hidden, d_gate_up, gateup_grad, down_grad = pl.pallas_call(
        kernel,
        cost_estimate=FREE,
        grid=(blocks,),
        out_shape=(
            jax.ShapeDtypeStruct((tokens, blocks * block), BF16),
            jax.ShapeDtypeStruct((tokens, 2 * blocks * block), BF16),
        )
        + tuple(jax.ShapeDtypeStruct(shape, BF16) for shape in grad_shapes),
        in_specs=[whole((part, width))] * 8 + [gateup_part, down_part],
        out_specs=(
            pl.BlockSpec((tokens, block), lambda j: (0, j)),
            pl.BlockSpec((tokens, 2 * block), lambda j: (0, j)),
        )
        + grad_specs,
        scratch_shapes=[pltpu.VMEM((width, tokens), BF16)],
        compiler_params=pltpu.CompilerParams(vmem_limit_bytes=56 << 20),
    )(*seconds, *d_finals, gateup, down)
    if not packed:
        gateup_grad = gateup_grad.reshape(blocks, count, rows, 2 * block)
        gateup_grad = gateup_grad.transpose(1, 0, 2, 3).reshape(count, -1, 2 * block)
        down_grad = down_grad.reshape(count, units, cols, 2 * block)
        down_grad = down_grad.transpose(0, 2, 1, 3).reshape(count, -1, 2 * block)
    return hidden, d_gate_up, gateup_grad, down_grad


def back_through_gateup(d_gate_up, gateup, first, count, kind, needed=()):
    blocks, width, columns = gateup.shape
    part = 256

    def kernel(d_ref, gu_ref, *refs):
        total = dot_nt(d_ref[:, :columns], gu_ref[0])
        for j in range(1, blocks):
            total = total + dot_nt(d_ref[:, j * columns : (j + 1) * columns], gu_ref[j])
        refs[-1][...] = total.astype(kind)

    return pl.pallas_call(
        kernel,
        cost_estimate=FREE,
        grid=(count // part,),
        out_shape=jax.ShapeDtypeStruct((count, width), kind),
        in_specs=[
            pl.BlockSpec((part, blocks * columns), lambda m: (first // part + m, 0)),
            pl.BlockSpec(gateup.shape, lambda m: (0, 0, 0), pipeline_mode=pl.Buffered(1)),
        ]
        + [pl.BlockSpec(memory_space=pl.ANY)] * len(needed),
        out_specs=pl.BlockSpec((part, width), lambda m: (m, 0)),
        compiler_params=pltpu.CompilerParams(vmem_limit_bytes=48 << 20),
    )(d_gate_up, gateup, *needed)


def quarter_columns(wide, hidden_all):
    units = hidden_all // (4 * wide)
    return units, HIDDEN_BLOCK // units


def gateup_cast(weight, quarter):
    rows, _, hidden_all = weight.shape
    wide = lax.axis_size("wide")
    units, each = quarter_columns(wide, hidden_all)
    block = HIDDEN_BLOCK
    blocks = hidden_all // (4 * block)
    if wide != BLOCK:
        split = weight.astype(BF16).reshape(rows, 2, blocks, each, 4, units)
        split = split.transpose(4, 2, 0, 1, 3, 5).reshape(4, blocks * rows, 2 * block)
        return split[quarter], split[quarter ^ 2]

    def kernel(quarter_ref, in_ref, mine_ref, theirs_ref):
        found = []
        for t in range(4):
            parts = []
            for k in range(2):
                for w in range(each):
                    low = (4 * w + t) * units
                    parts.append(in_ref[:, k, low : low + units])
            found.append(jnp.concatenate(parts, axis=1).astype(BF16).astype(F32))
        for ref, flip in ((mine_ref, 0), (theirs_ref, 2)):
            at = quarter_ref[0] ^ flip
            chosen = found[0]
            for t in range(1, 4):
                chosen = jnp.where(at == t, found[t], chosen)
            ref[...] = chosen.astype(BF16)

    part = pl.BlockSpec((rows, 2 * block), lambda j: (j, 0))
    return pl.pallas_call(
        kernel,
        cost_estimate=FREE,
        grid=(blocks,),
        out_shape=(jax.ShapeDtypeStruct((blocks * rows, 2 * block), BF16),) * 2,
        in_specs=[
            pl.BlockSpec(memory_space=pltpu.SMEM),
            pl.BlockSpec((rows, 2, 4 * block), lambda j: (0, 0, j)),
        ],
        out_specs=(part, part),
        compiler_params=pltpu.CompilerParams(vmem_limit_bytes=32 << 20),
    )(quarter.reshape(1).astype(jnp.int32), weight)


def gateup_step(master, moment, average, shares, quarter, rate):
    rows, _, hidden_all = master.shape
    wide = lax.axis_size("wide")
    units, each = quarter_columns(wide, hidden_all)
    block = HIDDEN_BLOCK
    blocks = hidden_all // (4 * block)
    if wide != BLOCK:
        split = jnp.stack(shares)[jnp.arange(4) ^ quarter]
        split = split.reshape(4, blocks, rows, 2, each, units).transpose(2, 3, 1, 4, 0, 5)
        return nesterov(
            master, moment, average, split.reshape(master.shape).astype(F32), rate
        )

    def kernel(quarter_ref, p_ref, m_ref, a_ref, *refs):
        ins, outs = refs[:4], refs[4:]
        given = [ref[...].astype(F32) for ref in ins]
        found = []
        for t in range(4):
            at = quarter_ref[0] ^ t
            chosen = given[0]
            for n in range(1, 4):
                chosen = jnp.where(at == n, given[n], chosen)
            found.append(chosen)
        for k in range(2):
            parts = []
            for w in range(each):
                low = k * block + w * units
                parts += [found[t][:, low : low + units] for t in range(4)]
            done = nesterov(
                p_ref[:, k, :], m_ref[:, k, :], a_ref[:, k, :], jnp.concatenate(parts, 1), rate
            )
            for ref, value in zip(outs, done):
                ref[:, k, :] = value

    whole = pl.BlockSpec((rows, 2, 4 * block), lambda j: (0, 0, j))
    part = pl.BlockSpec((rows, 2 * block), lambda j: (j, 0))
    return pl.pallas_call(
        kernel,
        cost_estimate=FREE,
        grid=(blocks,),
        out_shape=(jax.ShapeDtypeStruct(master.shape, F32),) * 3,
        in_specs=[pl.BlockSpec(memory_space=pltpu.SMEM)] + [whole] * 3 + [part] * 4,
        out_specs=(whole,) * 3,
        compiler_params=pltpu.CompilerParams(vmem_limit_bytes=32 << 20),
    )(quarter.reshape(1).astype(jnp.int32), master, moment, average, *shares)


def rms_scale(values):
    return lax.rsqrt(jnp.mean(values * values, axis=-1, keepdims=True) + EPSILON)


def norm_back(values, scale_rows, gain_row, upstream):
    normal_rows = values * scale_rows
    gain_grad = jnp.sum(upstream * normal_rows, axis=0)
    weighted = upstream * gain_row
    values_grad = scale_rows * (
        weighted - normal_rows * jnp.mean(weighted * normal_rows, axis=-1, keepdims=True)
    )
    return (gain_grad, values_grad)


def matmul(a, b, dims, out=F32):
    return lax.dot_general(a, b, (dims, ((), ())), preferred_element_type=F32).astype(out)


def nesterov(master, moment, average, gradient, step_rate):
    new_moment = MOMENTUM * moment + gradient
    new_master = master - step_rate * (gradient + MOMENTUM * new_moment)
    return (new_moment, new_master, AVERAGE * average + (1.0 - AVERAGE) * new_master)


def on_device(
    inputs,
    cotangent,
    lengths,
    gains,
    gains_momentum,
    gains_average,
    qkv_weight,
    qkv_momentum,
    qkv_average,
    out_weight,
    out_momentum,
    out_average,
    conv_taps,
    taps_momentum,
    taps_average,
    head_mix,
    mix_momentum,
    mix_average,
    gateup_weight,
    gateup_momentum,
    gateup_average,
    down_weight,
    down_momentum,
    down_average,
):
    micro_count, seq_count, seq_len, width = inputs.shape
    lags, shifts = conv_taps.shape[1:]
    reach = shifts // 2
    core = lax.axis_index("narrow")
    me = lax.axis_index("wide")
    wide = lax.axis_size("wide")
    cores = lax.axis_size("narrow")
    rows = width // wide
    own_heads = H // cores
    own_cols = own_heads * E
    hidden_all = gateup_weight.shape[2]
    units = hidden_all // (wide * 2 * cores)
    quarter = (me % 2) * cores + core
    tokens = micro_count * seq_count * seq_len

    def by_core(mine, other, axis):
        return jnp.where(
            core == 0,
            jnp.concatenate([mine, other], axis=axis),
            jnp.concatenate([other, mine], axis=axis),
        )

    def core_part(values, axis):
        return lax.dynamic_index_in_dim(values, core, axis, keepdims=False)

    def other_part(values, axis):
        return lax.dynamic_index_in_dim(values, 1 - core, axis, keepdims=False)

    def rows_of_core(values, axis):
        shape = values.shape
        split = values.reshape(
            shape[:axis] + (cores, shape[axis] // cores) + shape[axis + 1 :]
        )
        return core_part(split, axis), other_part(split, axis)

    def to_beside(partial):
        other = swap_cores(partial[tokens:].astype(BF16))
        return fold(partial[:tokens], other)

    def on_chip(partial):
        other = swap_cores(partial[tokens:].astype(BF16))
        return partial[:tokens].astype(F32) + other.astype(F32)

    def when(values, *needed):
        return after(values, *needed) if wide == BLOCK else values

    qkv_piece = rows_of_core(qkv_weight.astype(BF16).transpose(1, 0, 2), 2)[0]
    qkv_piece = qkv_piece.reshape(rows, 3 * own_cols)
    gains_piece = jnp.pad(gains.T.astype(BF16), ((0, 0), (0, 126)))
    out_piece = rows_of_core(out_weight.astype(BF16), 1)[0]
    first_piece = jnp.concatenate([qkv_piece, out_piece, gains_piece], axis=1)
    widths = (3 * own_cols, width // cores, 128)
    wide_block = 2 * HIDDEN_BLOCK
    gateup_mine, gateup_theirs = gateup_cast(gateup_weight, quarter)
    down_split = down_weight.astype(BF16).reshape(4, units, width // wide_block, wide_block)
    down_split = down_split.transpose(0, 2, 1, 3).reshape(4, -1, wide_block)

    def ff_piece(gateup_part, at):
        down_part = lax.dynamic_index_in_dim(down_split, at, 0, keepdims=False)
        return jnp.concatenate([gateup_part, down_part])

    inputs_own = inputs.reshape(tokens, width)
    inputs_other = swap_cores(inputs_own)
    lengths_own = lengths.reshape(-1)
    seq_lengths = jnp.concatenate([lengths_own, swap_cores(lengths_own)])
    pair = ff_pair(ff_piece(gateup_mine, quarter), ff_piece(gateup_theirs, quarter ^ 2))
    if wide == BLOCK:
        first_lines = line_and_plane(first_piece)
        ff_lines = line_gather(after(pair, first_lines[2][1][0], first_lines[3][1][0]))
        first_full = gather(first_piece, first_lines, widths, ff_lines[2:])
    else:
        first_full = gather(first_piece, None, widths)
    qkv_full, out_half, gains_full = first_full
    gains_full = gains_full[:, :2].T.astype(F32)
    out_full = by_core(out_half, swap_cores(out_half), 1)
    out_mine, out_theirs = rows_of_core(out_full, 0)

    states = inputs_own.astype(F32)
    first_scale = rms_scale(states)

    def first_norm(values):
        values = values.astype(F32)
        return (values * rms_scale(values) * gains_full[0]).astype(BF16)

    normed = jnp.concatenate([first_norm(inputs_own), first_norm(inputs_other)])
    d_final_own = cotangent.reshape(tokens, width)
    d_final_beside = permute(d_final_own, x_pairs())
    d_finals = [d_final_own, swap_cores(d_final_own), d_final_beside, swap_cores(d_final_beside)]
    all_tokens = cores * tokens

    taps_own = rows_of_core(conv_taps, 0)[0]
    mix_own = rows_of_core(head_mix, 0)[0]

    projected = matmul(normed, qkv_full, ((1,), (0,)), BF16)
    if wide == BLOCK:
        ff_near = after(ff_lines[0], qkv_full)
        ff_near_across = ff_cross(ff_near)
    context_own, probs = attention_forward(
        projected, base_rows_of(taps_own, seq_len, False), mix_own, seq_lengths, lags, reach
    )
    if wide == BLOCK:
        context_own = after(context_own, ff_near_across, d_final_beside)
        ff_far = ff_lines[1](context_own)
        ff_far_across = ff_cross(ff_far)
        ff_arrays = (ff_near, ff_near_across, ff_far, ff_far_across)
    else:
        ff_arrays = (pair,)
    gateup_full, down_full = ff_end(ff_arrays, rows, units)
    context_mine = context_own[:tokens]
    context_theirs = swap_cores(context_own[tokens:])
    middle = states + (
        matmul(context_mine, out_mine, ((1,), (0,)))
        + matmul(context_theirs, out_theirs, ((1,), (0,)))
    )
    second_scale = rms_scale(middle)
    second_own = (middle * second_scale * gains_full[1]).astype(BF16)
    second_beside = permute(second_own, x_pairs())
    context = by_core(context_mine, when(context_theirs, second_own), 1)
    if wide == BLOCK:
        second_beside = after(second_beside, ff_far_across)
    seconds = [second_own, swap_cores(second_own), second_beside, swap_cores(second_beside)]

    hidden, d_gate_up, gateup_grad, down_grad = feed_forward(
        seconds, d_finals, gateup_full, down_full, wide
    )
    beside = to_beside(
        back_through_gateup(d_gate_up, gateup_full, 2 * tokens, 2 * tokens, BF16)
    )
    gateup_grad, down_grad = when(gateup_grad, beside), when(down_grad, beside)
    ff_sends = ()
    if wide == BLOCK:
        pair_at, y = me // 8, (me // 2) % 2
        ff_sends = [
            ff_part(gateup_grad, down_grad, at, 1 - y) for at in (1 - pair_at, pair_at)
        ]
        arrived_far, arrived_near = (permute(send, Y_PAIR) for send in ff_sends)
    hidden = when(hidden, *ff_sends)
    result_parts = matmul(hidden, down_full, ((1,), (0,)))
    d_second_here = on_chip(
        back_through_gateup(d_gate_up, gateup_full, 0, 2 * tokens, F32, ff_sends)
    )
    d_second_here = when(d_second_here, result_parts)
    d_second = d_second_here + permute(beside, x_pairs()).astype(F32)
    result_beside = when(to_beside(result_parts[2 * tokens :]), d_second)
    result_arrived = permute(result_beside, x_pairs())
    output = middle + (on_chip(result_parts[: 2 * tokens]) + result_arrived.astype(F32))
    output = output.astype(BF16).reshape(inputs.shape)

    d_output = d_final_own.astype(F32)
    second_gain, d_norm_two = norm_back(middle, second_scale, gains_full[1], d_second)
    d_middle = d_output + d_norm_two
    d_attended = d_middle.astype(BF16)
    theirs = matmul(d_attended, out_theirs, ((1,), (1,)), BF16)
    mine = matmul(d_attended, out_mine, ((1,), (1,)), BF16)
    d_context_all = jnp.concatenate([mine, swap_cores(theirs)])
    out_part = lax.dynamic_slice_in_dim(d_attended, (1 - core) * own_cols, own_cols, axis=1)
    out_sent = matmul(context, out_part, ((0,), (0,)), BF16)
    out_part = lax.dynamic_slice_in_dim(d_attended, core * own_cols, own_cols, axis=1)
    out_kept = matmul(context, out_part, ((0,), (0,)), BF16)
    d_context_all = when(d_context_all, out_sent, out_kept)
    if wide == BLOCK:
        far = fold(ff_part(gateup_grad, down_grad, 1 - pair_at, y), arrived_far)
        d_context_all = after(d_context_all, far)
        ff_steps = line_begin(far)
    d_projected, taps_grad, mix_grad = attention_backward(
        projected,
        probs,
        d_context_all,
        base_rows_of(taps_own, seq_len, True),
        mix_own,
        seq_lengths,
        lags,
        reach,
    )
    if wide == BLOCK:
        d_projected = after(d_projected, result_arrived, *ff_steps)
    qkv_grad = matmul(normed, d_projected, ((0,), (0,)), BF16)
    out_grad = fold(out_kept, swap_cores(out_sent))
    sends, kept = scatter_begin(qkv_grad, out_grad)
    arrivals = scatter_first(sends, kept)
    d_normed_parts = matmul(when(d_projected, *sends), qkv_full, ((1,), (1,)))
    ff_steps_done = ()
    if wide == BLOCK:
        ff_steps = line_middle(far, *(after(step, *sends) for step in ff_steps))
        d_normed_parts = after(d_normed_parts, *ff_steps)
        near = fold(
            ff_part(gateup_grad, down_grad, pair_at, y), after(arrived_near, *sends)
        )
        ff_total = line_end(near, far, *ff_steps)
        ff_steps_done = (ff_total,)
    else:
        ff_total = ff_scatter_whole(gateup_grad, down_grad)
    ff_mine, ff_theirs = ff_last(ff_total)
    first_sums = scatter_plane(sends, kept, arrivals, ff_steps_done)
    d_normed = d_normed_parts[:tokens] + swap_cores(d_normed_parts[tokens:])
    first_gain, d_norm_one = norm_back(states, first_scale, gains_full[0], d_normed)
    input_grad = (d_middle + d_norm_one).astype(BF16).reshape(inputs.shape)

    def spread(values):
        held = jnp.zeros((cores,) + values.shape, F32)
        return lax.dynamic_update_index_in_dim(held, values, core, 0).reshape(-1)

    packed = jnp.concatenate([first_gain, second_gain, spread(taps_grad), spread(mix_grad)])
    packed = sum_small(packed)
    gains_grad = lax.dynamic_slice_in_dim(
        packed[: 2 * width].reshape(2, width), me * rows, rows, axis=1
    )
    taps_total = packed[2 * width : 2 * width + conv_taps.size].reshape(conv_taps.shape)
    mix_total = packed[2 * width + conv_taps.size :].reshape(head_mix.shape)

    tokens_all = tokens * cores * wide

    def rate_for(position):
        return RATES[position] / math.sqrt(tokens_all * (seq_len if PER_PAIR[position] else 1))

    def step(master, moment, average, gradient, position):
        return nesterov(master, moment, average, gradient.astype(F32), rate_for(position))

    ff_shares = [ff_mine, swap_cores(ff_mine), ff_theirs, swap_cores(ff_theirs)]
    gateup_tall = ff_mine.shape[0] - width // wide_block * units
    down_shares = jnp.stack([share[gateup_tall:] for share in ff_shares])
    down_total = down_shares[jnp.arange(4) ^ quarter].reshape(4, -1, units, wide_block)
    down_total = down_total.transpose(0, 2, 1, 3).reshape(down_weight.shape)
    gateup_done = gateup_step(
        gateup_weight,
        gateup_momentum,
        gateup_average,
        [share[:gateup_tall] for share in ff_shares],
        quarter,
        rate_for(5),
    )
    down_done = step(down_weight, down_momentum, down_average, down_total, 6)

    first_share = scatter_line(first_sums, gateup_done[0], down_done[0], packed)
    first_other = swap_cores(first_share)
    qkv_total = by_core(
        first_share[:, : 3 * own_cols].reshape(rows, 3, own_cols),
        first_other[:, : 3 * own_cols].reshape(rows, 3, own_cols),
        2,
    ).transpose(1, 0, 2)
    out_total = by_core(first_share[:, 3 * own_cols :], first_other[:, 3 * own_cols :], 1)
    return (
        output,
        input_grad,
        *step(gains, gains_momentum, gains_average, gains_grad, 0),
        *step(qkv_weight, qkv_momentum, qkv_average, qkv_total, 1),
        *step(out_weight, out_momentum, out_average, out_total, 2),
        *step(conv_taps, taps_momentum, taps_average, taps_total, 3),
        *step(head_mix, mix_momentum, mix_average, mix_total, 4),
        *gateup_done,
        *down_done,
    )


def solution(mesh):
    batch = P(None, ("narrow", "wide"), None, None)
    gain = P(None, "wide")
    qkv = P(None, "wide", None)
    row = P("wide", None)
    row3 = P("wide", None, None)
    params = (gain,) * 3 + (qkv,) * 3 + (row,) * 3 + (P(),) * 6 + (row3,) * 3 + (row,) * 3
    return jax.shard_map(
        on_device,
        mesh=mesh,
        in_specs=(batch, batch, P(None, ("narrow", "wide"))) + params,
        out_specs=(batch, batch) + params,
        check_vma=False,
    )
```
